128 devices in a mesh: dp: 16 (over z_lo, y, core), tensor: 8 (over z_hi, x).
Axes of the slice: x: 4, y: 4, z: 4 (z_hi: 2, z_lo: 2; z = z_hi * 2 + z_lo), core: 2. Of those that a mesh axis runs over, the one named last changes fastest.
Arguments:
- hidden: bfloat16 [32768, 1536], P(('dp', 'tensor')), may hold values from -6 to 6
- doc_ids: int32 [32768], P('dp'), may hold values from 0 to 2, as said below
- norm_gain: float32 [1536], replicated, may hold values from 0.1 to 1.9
- main_proj: bfloat16 [1536, 2, 3072], P('dp', None, 'tensor'), may hold values from -0.15625 to 0.15625
- step_proj: bfloat16 [1536, 48], P('dp', 'tensor'), may hold values from -0.15625 to 0.15625
- state_proj: bfloat16 [1536, 256], P('dp', 'tensor'), may hold values from -0.15625 to 0.15625
- conv_main: float32 [4, 3072], P(None, 'tensor'), may hold values from -3 to 3
- conv_main_bias: float32 [3072], P('tensor'), may hold values from -3 to 3
- conv_state: float32 [4, 256], P(None, 'tensor'), may hold values from -3 to 3
- conv_state_bias: float32 [256], P('tensor'), may hold values from -3 to 3
- step_bias: float32 [48], P('tensor'), may hold values from -6 to -2
- decay_log: float32 [48], P('tensor'), may hold values from 0 to 2.77
- skip_gain: float32 [48], P('tensor'), may hold values from 0.5 to 2
- gate_gain: float32 [3072], P('tensor'), may hold values from 0.1 to 1.9
- out_proj: bfloat16 [1536, 3072], P('dp', 'tensor'), may hold values from -0.109375 to 0.109375
- cotangent: bfloat16 [32768, 1536], P(('dp', 'tensor')), may hold values from -6 to 6
Outputs:
- mixed: bfloat16 [32768, 1536], P(('dp', 'tensor'))
- grad_hidden: float32 [32768, 1536], P(('dp', 'tensor'))
- grad_norm_gain: float32 [1536], replicated
- grad_main_proj: float32 [1536, 2, 3072], P('dp', None, 'tensor')
- grad_step_proj: float32 [1536, 48], P('dp', 'tensor')
- grad_state_proj: float32 [1536, 256], P('dp', 'tensor')
- grad_conv_main: float32 [4, 3072], P(None, 'tensor')
- grad_conv_main_bias: float32 [3072], P('tensor')
- grad_conv_state: float32 [4, 256], P(None, 'tensor')
- grad_conv_state_bias: float32 [256], P('tensor')
- grad_step_bias: float32 [48], P('tensor')
- grad_decay_log: float32 [48], P('tensor')
- grad_skip_gain: float32 [48], P('tensor')
- grad_gate_gain: float32 [3072], P('tensor')
- grad_out_proj: float32 [1536, 3072], P('dp', 'tensor')
The draws below stay inside these ranges and needn't reach their ends.
Inputs may be any that keep to these rules, and one draw needn't show every extreme that they name: `doc_ids`: in each sequence (the 2048 tokens of one index of dp) the ids run from 0 to 2 in order, never falling, each id on 200 or more consecutive positions.
All inputs are finite; a program needn't handle non-finite values.
Results may differ from the reference program's by a relative error of at most 0.02.
Values may be sent and summed in bfloat16 or wider, within the bound.
A program may use at most 128 MiB of HBM per device.

```python
import jax
import jax.numpy as jnp
from jax import lax

D = 1536
DI = 3072
H = 48
P_SIZE = 64
NS = 128
CONV = 4
BLOCK = 256
DOCS = 3
DOC_MIN = 200
SEQ_LEN = 2048
TOKENS = 32768


def draw_doc_ids(key, part):
    key = jax.random.fold_in(key, 7)
    sequences = TOKENS // SEQ_LEN
    spare_room = SEQ_LEN - DOCS * DOC_MIN
    cut_points = jnp.sort(jax.random.randint(key, (sequences, DOCS - 1), 0, spare_room + 1), axis=1)
    bounds = cut_points + DOC_MIN * jnp.arange(1, DOCS, dtype=jnp.int32)[None, :]
    places = jnp.arange(SEQ_LEN, dtype=jnp.int32)
    doc_numbers = jnp.sum((places[None, :, None] >= bounds[:, None, :]).astype(jnp.int32), axis=2)
    return doc_numbers.reshape(TOKENS).astype(jnp.int32)


def block_levels(rng, dims, pieces, least, largest):
    def one(dim, blocks):
        draws = jax.random.uniform(jax.random.fold_in(jax.random.fold_in(rng, 6), dim), (blocks,), jnp.float32, least / len(pieces), largest / len(pieces))
        return jnp.repeat(jnp.exp(draws), dims[dim] // blocks).reshape((-1,) + (1,) * (len(dims) - dim - 1))

    loudness = one(*pieces[0])
    for cut in pieces[1:]:
        loudness = loudness * one(*cut)
    return loudness


def scatter_about(own_key, dims, width, limit, shards=(), kind=jnp.bfloat16):
    drawn = width * jax.random.normal(own_key, dims, jnp.float32)
    if shards:
        drawn = drawn * block_levels(own_key, dims, shards, -0.22, 0.18)
    return jnp.clip(drawn, -limit, limit).astype(kind)


def setup_inputs(seed: int = 0) -> dict:
    key_list = jax.random.split(jax.random.key(seed), 17)
    return {
        "hidden": scatter_about(key_list[0], (TOKENS, D), 1.0, 6.0, ((0, 128),)),
        "doc_ids": draw_doc_ids(jax.random.fold_in(key_list[16], 71), 0),
        "norm_gain": jnp.clip(1.0 + 0.18 * jax.random.normal(key_list[2], (D,), jnp.float32), 0.1, 1.9),
        "main_proj": scatter_about(key_list[3], (D, 2, DI), D ** -0.5, 0.15625, ((0, 16), (2, 8))),
        "step_proj": scatter_about(key_list[4], (D, H), D ** -0.5, 0.15625, ((0, 16), (1, 8))),
        "state_proj": scatter_about(key_list[5], (D, 2 * NS), D ** -0.5, 0.15625, ((0, 16), (1, 8))),
        "conv_main": scatter_about(key_list[6], (CONV, DI), 0.5, 3.0, ((1, 8),), jnp.float32),
        "conv_main_bias": scatter_about(key_list[7], (DI,), 0.5, 3.0, ((0, 8),), jnp.float32),
        "conv_state": scatter_about(key_list[8], (CONV, 2 * NS), 0.5, 3.0, ((1, 8),), jnp.float32),
        "conv_state_bias": scatter_about(key_list[9], (2 * NS,), 0.5, 3.0, ((0, 8),), jnp.float32),
        "step_bias": jnp.clip(-6.0 + 4.0 * jax.random.uniform(key_list[10], (H,), jnp.float32) ** block_levels(key_list[10], (H,), ((0, 8),), -0.2, 0.2), -6.0, -2.0),
        "decay_log": jnp.clip(2.77 * jax.random.uniform(key_list[11], (H,), jnp.float32) ** block_levels(key_list[11], (H,), ((0, 8),), -0.2, 0.2), 0.0, 2.77),
        "skip_gain": jnp.clip(0.5 + 1.5 * jax.random.uniform(key_list[12], (H,), jnp.float32) ** block_levels(key_list[12], (H,), ((0, 8),), -0.2, 0.2), 0.5, 2.0),
        "gate_gain": jnp.clip(1.0 + 0.18 * jax.random.normal(key_list[13], (DI,), jnp.float32), 0.1, 1.9),
        "out_proj": scatter_about(key_list[14], (D, DI), DI ** -0.5, 0.109375, ((0, 16), (1, 8))),
        "cotangent": scatter_about(key_list[15], (TOKENS, D), 1.0, 6.0, ((0, 128),)),
    }


epsilon = 1e-05
precise = lax.Precision.HIGHEST

@jax.custom_vjp
def low(v):
    return lax.optimization_barrier(v.astype(jnp.bfloat16)).astype(jnp.float32)

@jax.custom_vjp
def low_back(v):
    return v

def low_keep(v):
    return (low(v), None)

def low_pass(kept, grad):
    return (grad,)

def back_keep(v):
    return (v, None)

def back_low(kept, grad):
    return (low(grad),)
low.defvjp(low_keep, low_pass)
low_back.defvjp(back_keep, back_low)

def causal_conv(values, kernel, bias_row, doc_row):
    length = values.shape[0]
    taps = kernel.shape[0]
    total = bias_row[None, :] + kernel[taps - 1][None, :] * values
    for offset in range(1, taps):
        earlier = jnp.concatenate([jnp.zeros((offset, values.shape[1]), values.dtype), values[:length - offset]], axis=0)
        earlier_doc = jnp.concatenate([jnp.full((offset,), -1, jnp.int32), doc_row[:length - offset]])
        linked = (earlier_doc == doc_row).astype(values.dtype)
        total = total + kernel[taps - 1 - offset][None, :] * earlier * linked[:, None]
    return total

def block_mix(state_in, block_in, decay_rate, skip_gain):
    x_block, b_block, c_block, step_block, doc_block, doc_prev = block_in
    block_len = doc_block.shape[0]
    head_count = step_block.shape[1]
    cum_decay = jnp.cumsum(step_block * decay_rate[None, :], axis=0)
    scores = jnp.dot(c_block, b_block.T, precision=precise)
    scores = low_back(jnp.broadcast_to(scores[None], (head_count, block_len, block_len)))
    row_pos = lax.broadcasted_iota(jnp.int32, (block_len, block_len), 0)
    col_pos = lax.broadcasted_iota(jnp.int32, (block_len, block_len), 1)
    linked = (doc_block[:, None] == doc_block[None, :]) & (row_pos >= col_pos)
    cum_heads = cum_decay.T
    spread = jnp.where(linked[None], cum_heads[:, :, None] - cum_heads[:, None, :], -10000.0)
    decay_mat = jnp.exp(spread) * linked[None].astype(cum_decay.dtype)
    mixing = low(scores * (decay_mat * step_block.T[:, None, :]))
    y_intra = jnp.einsum('hij,jhp->ihp', mixing, x_block, precision=precise)
    carried = low_back(jnp.einsum('in,hnp->ihp', c_block, low(state_in), precision=precise))
    enter_decay = jnp.exp(cum_decay) * (doc_block == doc_prev).astype(cum_decay.dtype)[:, None]
    cum_end = cum_decay[block_len - 1]
    end_link = (doc_block == doc_block[block_len - 1]).astype(cum_decay.dtype)
    weight = jnp.exp(cum_end[None, :] - cum_decay) * end_link[:, None] * step_block
    scaled = low(weight.T[:, :, None] * b_block[None])
    update = low_back(jnp.einsum('hjn,jhp->hnp', scaled, x_block, precision=precise))
    keep_decay = jnp.exp(cum_end) * (doc_block[block_len - 1] == doc_prev).astype(cum_decay.dtype)
    state_out = keep_decay[:, None, None] * state_in + update
    y_block = y_intra + carried * enter_decay[:, :, None] + skip_gain[None, :, None] * x_block
    return (state_out, y_block)

def scan_mix(x_heads, b_rows, c_rows, step_size, decay_rate, skip_gain, doc_row):
    length = x_heads.shape[0]
    block_count = length // BLOCK
    doc_blocks = doc_row.reshape(block_count, BLOCK)
    doc_before = jnp.concatenate([jnp.full((1,), -1, jnp.int32), doc_blocks[:-1, -1]])
    blocks_all = (x_heads.reshape(block_count, BLOCK, H, P_SIZE), b_rows.reshape(block_count, BLOCK, NS), c_rows.reshape(block_count, BLOCK, NS), step_size.reshape(block_count, BLOCK, H), doc_blocks, doc_before)

    def block_step(state_in, block_in):
        return block_mix(state_in, block_in, decay_rate, skip_gain)
    start_state = jnp.zeros((H, NS, P_SIZE), x_heads.dtype)
    _, y_blocks = lax.scan(block_step, start_state, blocks_all)
    return y_blocks.reshape(length, H, P_SIZE)

def layer_forward(params, rows_in, doc_row):
    norm_gain, main_proj, step_proj, state_proj, conv_main, conv_main_bias, conv_state, conv_state_bias, step_bias, decay_log, skip_gain, gate_gain, out_proj = params
    length = rows_in.shape[0]
    inv_rms = lax.rsqrt(lax.optimization_barrier(jnp.mean(rows_in * rows_in, axis=1, keepdims=True)) + epsilon)
    normed = low(rows_in * inv_rms * norm_gain[None, :])
    main_raw = low_back(jnp.einsum('td,dkc->tkc', normed, main_proj, precision=precise))
    step_raw = low_back(jnp.dot(normed, step_proj, precision=precise))
    state_raw = low_back(jnp.dot(normed, state_proj, precision=precise))
    gate_in = main_raw[:, 0, :]
    x_act = low(jax.nn.silu(causal_conv(main_raw[:, 1, :], conv_main, conv_main_bias, doc_row)))
    state_act = low(jax.nn.silu(causal_conv(state_raw, conv_state, conv_state_bias, doc_row)))
    step_size = jax.nn.softplus(step_raw + step_bias[None, :])
    decay_rate = -jnp.exp(decay_log)
    y_heads = scan_mix(x_act.reshape(length, H, P_SIZE), state_act[:, :NS], state_act[:, NS:], step_size, decay_rate, skip_gain, doc_row)
    y_ssd = low_back(y_heads).reshape(length, DI)
    gated = y_ssd * jax.nn.silu(gate_in)
    gate_inv = lax.rsqrt(lax.optimization_barrier(jnp.mean(gated * gated, axis=1, keepdims=True)) + epsilon)
    gate_out = low(gated * gate_inv * gate_gain[None, :])
    return rows_in + jnp.dot(gate_out, out_proj.T, precision=precise)

def reference(hidden, doc_ids, norm_gain, main_proj, step_proj, state_proj, conv_main, conv_main_bias, conv_state, conv_state_bias, step_bias, decay_log, skip_gain, gate_gain, out_proj, cotangent):
    params = tuple((weight_arg.astype(jnp.float32) for weight_arg in (norm_gain, main_proj, step_proj, state_proj, conv_main, conv_main_bias, conv_state, conv_state_bias, step_bias, decay_log, skip_gain, gate_gain, out_proj)))
    sequences = TOKENS // SEQ_LEN
    rows_all = hidden.astype(jnp.float32).reshape(sequences, SEQ_LEN, D)
    cot_all = cotangent.astype(jnp.float32).reshape(sequences, SEQ_LEN, D)
    docs_all = doc_ids.reshape(sequences, SEQ_LEN)

    def one_sequence(totals, block_in):
        seq_rows, doc_row, cot_rows = block_in

        def forward(weights, inputs):
            return layer_forward(weights, inputs, doc_row)
        out_rows, pullback = jax.vjp(forward, params, seq_rows)
        grad_params, grad_rows = pullback(cot_rows)
        totals = jax.tree.map(jnp.add, totals, grad_params)
        return (totals, (out_rows.astype(jnp.bfloat16), grad_rows))
    start_totals = jax.tree.map(jnp.zeros_like, params)
    totals, (mixed, grad_hidden) = lax.scan(one_sequence, start_totals, (rows_all, docs_all, cot_all))
    return (mixed.reshape(TOKENS, D), grad_hidden.reshape(TOKENS, D), totals[0], totals[1], totals[2], totals[3], totals[4], totals[5], totals[6], totals[7], totals[8], totals[9], totals[10], totals[11], totals[12])
```

```python
import functools

import jax
import jax.numpy as jnp
from jax import lax
from jax.experimental import pallas as pl
from jax.experimental.pallas import tpu as pltpu
from jax.sharding import PartitionSpec as P

BLOCK = 256
epsilon = 1e-05

MESH = pl.DeviceIdType.MESH
AXES = (0, 1, 2)
SIDE = 4


def coordinates():
    dp = lax.axis_index("dp")
    t = lax.axis_index("tensor")
    z = lax.div(t, 4) * 2 + lax.div(dp, 8)
    return (lax.rem(t, 4), lax.rem(lax.div(dp, 2), 4), z), lax.rem(dp, 2)


def device(at, core):
    x, y, z = at
    return (lax.rem(z, 2) * 8 + y * 2 + core, lax.div(z, 2) * 4 + x)


def moved(at, axis, by):
    return tuple(lax.rem(v + by + SIDE, SIDE) if i == axis else v for i, v in enumerate(at))


def pieces(at, whole, width):
    x, y, z = at
    lo = pl.ds(0, 2) if 2 in whole else pl.ds(lax.rem(z, 2), 1)
    row = pl.ds(0, 4) if 1 in whole else pl.ds(y, 1)
    hi = lax.div(z, 2)
    if 0 in whole and 2 in whole:
        cols = [pl.ds(0, 8 * width)]
    elif 0 in whole:
        cols = [pl.ds(pl.multiple_of(hi * 4 * width, 128), 4 * width)]
    elif 2 in whole:
        cols = [
            pl.ds(pl.multiple_of(x * width, 128), width),
            pl.ds(pl.multiple_of((4 + x) * width, 128), width),
        ]
    else:
        cols = [pl.ds(pl.multiple_of((hi * 4 + x) * width, 128), width)]
    return [(lo, row, c) for c in cols]


def greet(at, core, group):
    barrier = pltpu.get_barrier_semaphore()
    others = [device(moved(at, axis, by), core) for axis in AXES for by in (1, -1)]
    others.append(device(at, 1 - core))
    others += group
    for other in others:
        pl.semaphore_signal(barrier, inc=1, device_id=other, device_id_type=MESH)
    pl.semaphore_wait(barrier, len(others))


def tensor_peer(by):
    return (lax.axis_index("dp"), lax.rem(lax.axis_index("tensor") + by, 8))


ROWS, WIDTH, SMALL_ROWS, SMALL_WIDTH = 96, 384, 32, 128
UNITS = [(0, q * 32, q) for q in range(3)] + [(1, 0, 0)]
WIDTHS = [WIDTH, SMALL_WIDTH]
STACK = [3, 1]


def axes_of(u):
    return [(UNITS[u][2] + j) % 3 for j in range(3)]


def region(ref, u, core, mats, where, whole, half=None):
    which, first, rows = UNITS[u][0], UNITS[u][1], 32
    if half is not None:
        first, rows = first + half * 16, 16
    return [
        ref.at[mats, lo, row, core, pl.ds(first, rows), cols]
        for lo, row, cols in pieces(where, whole, WIDTHS[which])
    ]


def sized(ref, u, mats, blocks, halves=2):
    width = WIDTHS[UNITS[u][0]]
    cols = min(blocks, 8)
    rest = blocks // cols
    return ref.at[mats, pl.ds(0, max(rest // 4, 1)), pl.ds(0, min(rest, 4)), 0, pl.ds(0, 16 * halves), pl.ds(0, cols * width)]


def gather_kernel(*refs):
    shards, small, tail, params = refs[0], refs[1], refs[2], refs[3]
    full, halo, params_all = refs[4:6], refs[6], refs[7]
    own_sem, halo_sem, param_send, param_recv, send, recv, core_send, core_recv = refs[8:]
    at, core = coordinates()
    t = lax.axis_index("tensor")
    own = []
    for w, source in enumerate((shards, small)):
        for lo, row, cols in pieces(at, (), WIDTHS[w]):
            own.append(
                pltpu.make_async_copy(source, full[w].at[:, lo.start, row.start, core, :, cols], own_sem.at[w])
            )
    own.append(pltpu.make_async_copy(params, params_all.at[t], own_sem.at[2]))
    for c in own:
        c.start()
    greet(at, core, [tensor_peer(by) for by in range(1, 8)])
    last = []

    def go(copy, wait=True):
        copy.start()
        if wait:
            last.append(copy)

    def tail_copy():
        return pltpu.make_async_remote_copy(
            src_ref=tail, dst_ref=halo, send_sem=halo_sem.at[0], recv_sem=halo_sem.at[1],
            device_id=tensor_peer(1), device_id_type=MESH,
        )

    def param_copy(by, of):
        return pltpu.make_async_remote_copy(
            src_ref=params, dst_ref=params_all.at[of], send_sem=param_send.at[by - 1],
            recv_sem=param_recv.at[by - 1], device_id=tensor_peer(by), device_id_type=MESH,
        )

    go(tail_copy())
    for by in range(1, 8):
        go(param_copy(by, t))
    for c in own:
        c.wait()

    def slot(u, phase, m):
        return (phase if phase < 2 else 2 + m), [u]

    def mats_of(u, phase, m):
        return pl.ds(0, STACK[UNITS[u][0]]) if phase < 2 else pl.ds(m, 1)

    def sends(u, phase, m, step):
        axes = axes_of(u)
        whole, axis = axes[:phase], axes[phase]
        index = phase if phase < 2 else 2 + m
        ref = full[UNITS[u][0]]
        for kind, by in ((0, 1), (1, -1)):
            where = at if step == 0 else moved(at, axis, -by)
            for part in region(ref, u, core, mats_of(u, phase, m), where, whole, kind if step else None):
                pltpu.make_async_remote_copy(
                    src_ref=part, dst_ref=part, send_sem=send.at[u, index, step],
                    recv_sem=recv.at[u, index, step],
                    device_id=device(moved(at, axis, by), core), device_id_type=MESH,
                ).start()

    def await_step(u, phase, m, step, sem):
        index = phase if phase < 2 else 2 + m
        part = sized(full[UNITS[u][0]], u, mats_of(u, phase, m), 2 * 4**phase // (1 + step))
        pltpu.make_async_copy(part, part, sem.at[u, index, step]).wait()

    def to_partner(u, m, where, whole):
        for part in region(full[UNITS[u][0]], u, core, mats_of(u, 2, m), where, whole):
            pltpu.make_async_remote_copy(
                src_ref=part, dst_ref=part, send_sem=core_send.at[u, m],
                recv_sem=core_recv.at[u, m], device_id=device(at, 1 - core), device_id_type=MESH,
            ).start()

    everything = range(len(UNITS))
    late = [(u, m) for m in range(3) for u in everything if m < STACK[UNITS[u][0]]]
    for phase in (0, 1):
        for u in everything:
            sends(u, phase, 0, 0)
        for u in everything:
            await_step(u, phase, 0, 0, recv)
            sends(u, phase, 0, 1)
        for u in everything:
            await_step(u, phase, 0, 1, recv)
    for u, m in late:
        sends(u, 2, m, 0)
    for u, m in late:
        to_partner(u, m, at, axes_of(u)[:2])
    for u, m in late:
        await_step(u, 2, m, 0, recv)
        sends(u, 2, m, 1)
        whole, axis = axes_of(u)[:2], axes_of(u)[2]
        for by in (-1, 1):
            to_partner(u, m, moved(at, axis, by), whole)
    for u, m in late:
        await_step(u, 2, m, 1, recv)
        whole, axis = axes_of(u)[:2], axes_of(u)[2]
        to_partner(u, m, moved(at, axis, 2), whole)
    for u, m in late:
        part = sized(full[UNITS[u][0]], u, mats_of(u, 2, m), 64)
        pltpu.make_async_copy(part, part, core_recv.at[u, m]).wait()
        pltpu.make_async_copy(part, part, core_send.at[u, m]).wait()
    tail_copy().wait_recv()
    for by in range(1, 8):
        param_copy(by, lax.rem(t + 8 - by, 8)).wait_recv()
    for u in everything:
        for phase in (0, 1):
            for step in (0, 1):
                await_step(u, phase, 0, step, send)
    for u, m in late:
        for step in (0, 1):
            await_step(u, 2, m, step, send)
    for c in last:
        c.wait_send()


def gather_weights(shards, small, tail, params):
    units = len(UNITS)
    return pl.pallas_call(
        gather_kernel,
        name="gather_weights",
        out_shape=[
            jax.ShapeDtypeStruct((3, 2, 4, 2, ROWS, 8 * WIDTH), jnp.bfloat16),
            jax.ShapeDtypeStruct((1, 2, 4, 2, SMALL_ROWS, 8 * SMALL_WIDTH), jnp.bfloat16),
            jax.ShapeDtypeStruct(tail.shape, tail.dtype),
            jax.ShapeDtypeStruct((8,) + params.shape, params.dtype),
        ],
        in_specs=[pl.BlockSpec(memory_space=pl.ANY)] * 4,
        out_specs=[pl.BlockSpec(memory_space=pl.ANY)] * 4,
        scratch_shapes=[
            pltpu.SemaphoreType.DMA((3,)),
            pltpu.SemaphoreType.DMA((2,)),
            pltpu.SemaphoreType.DMA((7,)),
            pltpu.SemaphoreType.DMA((7,)),
            pltpu.SemaphoreType.DMA((units, 5, 2)),
            pltpu.SemaphoreType.DMA((units, 5, 2)),
            pltpu.SemaphoreType.DMA((units, 3)),
            pltpu.SemaphoreType.DMA((units, 3)),
        ],
        compiler_params=pltpu.CompilerParams(collective_id=0, has_side_effects=True),
    )(shards, small, tail, params)


VEC_ROWS = 168


def spread(whole):
    return (2 if 2 in whole else 1, 4 if 1 in whole else 1, (4 if 0 in whole else 1) * (2 if 2 in whole else 1))


def half_shape(u, phase, rows):
    lo, y, cols = spread(axes_of(u)[:phase])
    which = UNITS[u][0]
    return (2, STACK[which], lo, y, rows, cols * WIDTHS[which])


def scatter_kernel(*refs):
    grads, vec = refs[0:2], refs[2]
    outs, vec_out = refs[3:5], refs[5]
    own, other = refs[6:8], refs[8:10]
    units = len(UNITS)
    half_buf = [[refs[10 + 3 * u + p] for p in range(3)] for u in range(units)]
    full_buf = [[refs[10 + 3 * (units + u) + p] for p in range(3)] for u in range(units)]
    rest = refs[10 + 6 * units :]
    vec_acc, vec_in, own_sem, vec_send, vec_recv, send, recv, core_send, core_recv = rest
    at, core = coordinates()
    loads = [
        [pltpu.make_async_copy(grads[w].at[m, :, :, core], own[w].at[m], own_sem.at[w, m]) for m in range(STACK[w])]
        for w in range(2)
    ]
    for w in range(2):
        for c in loads[w]:
            c.start()
    greet(at, core, [device(moved(at, axis, 2), core) for axis in AXES])

    everything = range(units)
    late = [(u, m) for m in range(3) for u in everything if m < STACK[UNITS[u][0]]]

    def part_of(ref, u, mats, where, whole, half=None):
        which, first, rows = UNITS[u][0], UNITS[u][1], 32
        if half is not None:
            first, rows = first + half * 16, 16
        return [ref.at[mats, lo, y, pl.ds(first, rows), cols] for lo, y, cols in pieces(where, whole, WIDTHS[which])]

    groups = [[2], [1, -1], [0]]

    for u, m in late:
        axes = axes_of(u)
        which = UNITS[u][0]
        for g, group in enumerate(groups):
            for by in group:
                where = moved(at, axes[2], by) if by else at
                for src, dst in zip(
                    region(grads[which], u, 1 - core, pl.ds(m, 1), where, axes[:2]),
                    part_of(other[which], u, pl.ds(m, 1), where, axes[:2]),
                ):
                    pltpu.make_async_remote_copy(
                        src_ref=src, dst_ref=dst, send_sem=core_send.at[u, m], recv_sem=core_recv.at[u, m, g],
                        device_id=device(at, 1 - core), device_id_type=MESH,
                    ).start()

    def await_partner(u, m, g):
        which = UNITS[u][0]
        rows = 2 * len(groups[g])
        part = other[which].at[pl.ds(m, 1), pl.ds(0, 1), pl.ds(0, rows), pl.ds(0, 32)]
        pltpu.make_async_copy(part, part, core_recv.at[u, m, g]).wait()

    def add(u, phase, m, where, half, terms, result=None):
        which, first, rows = UNITS[u][0], UNITS[u][1], 32
        if half is not None:
            first, rows = first + half * 16, 16
        whole = axes_of(u)[:phase]
        n_lo, n_y, _ = spread(whole)
        mats = STACK[which] if m is None else 1
        for i, (lo, y, cols) in enumerate(pieces(where, whole, WIDTHS[which])):

            @pl.loop(0, mats * n_lo * n_y)
            def _(k, i=i, lo=lo, y=y, cols=cols):
                mat = lax.div(k, n_lo * n_y) if m is None else m
                a, b = lax.rem(lax.div(k, n_y), n_lo), lax.rem(k, n_y)
                here = (mat, lo.start + a, y.start + b, pl.ds(first, rows), cols)
                total = own[which][here].astype(jnp.float32)
                for term in terms:
                    total = total + term(mat, i, a, b, here).astype(jnp.float32)
                if result is None:
                    own[which][here] = total.astype(jnp.bfloat16)
                else:
                    result[mat, pl.ds(first, rows), :] = total

    def from_other(u):
        return lambda mat, i, a, b, here: other[UNITS[u][0]][here]

    def from_buf(ref, side, u, phase):
        which = UNITS[u][0]
        whole = axes_of(u)[:phase]
        width = spread(whole)[2] * WIDTHS[which] // (2 if 2 in whole and 0 not in whole else 1)
        return lambda mat, i, a, b, here: ref[side, mat, a, b, :, pl.ds(i * width, width)]

    def send_step(u, phase, m, step):
        axes = axes_of(u)
        whole, axis = axes[:phase], axes[phase]
        which = UNITS[u][0]
        mats = pl.ds(0, STACK[which]) if m is None else pl.ds(m, 1)
        index = phase if m is None else 2 + m
        buf = half_buf[u][phase] if step == 0 else full_buf[u][phase]
        for side, by in ((0, 1), (1, -1)):
            where = moved(at, axis, 2 if step == 0 else by)
            sources = part_of(own[which], u, mats, where, whole, side if step == 0 else None)
            width = buf.shape[-1] // len(sources)
            for i, src in enumerate(sources):
                pltpu.make_async_remote_copy(
                    src_ref=src, dst_ref=buf.at[side, mats, :, :, :, pl.ds(i * width, width)],
                    send_sem=send.at[u, index, step], recv_sem=recv.at[u, index, step],
                    device_id=device(moved(at, axis, by), core), device_id_type=MESH,
                ).start()

    def await_step(u, phase, m, step, sem):
        index = phase if m is None else 2 + m
        buf = half_buf[u][phase] if step == 0 else full_buf[u][phase]
        part = buf if m is None else buf.at[:, pl.ds(m, 1)]
        pltpu.make_async_copy(part, part, sem.at[u, index, step]).wait()

    def vec_copy(k):
        (x, y, z) = at
        flip = lambda v: v + 1 - 2 * lax.rem(v, 2)
        to = [
            device(at, 1 - core),
            device((flip(x), y, z), core),
            device((x, flip(y), z), core),
            device((x, y, flip(z)), core),
            device(moved(at, 0, 2), core),
            device(moved(at, 1, 2), core),
            device(moved(at, 2, 2), core),
        ][k]
        return pltpu.make_async_remote_copy(
            src_ref=vec_acc.at[k], dst_ref=vec_in.at[k], send_sem=vec_send.at[k], recv_sem=vec_recv.at[k],
            device_id=to, device_id_type=MESH,
        )

    def vec_step(k):
        if k == 0:
            vec_acc[0] = vec[...]
        else:
            vec_copy(k - 1).wait_recv()
            vec_acc[k] = vec_acc[k - 1] + vec_in[k - 1]
        if k < 7:
            vec_copy(k).start()
        else:
            vec_out[...] = vec_acc[7]

    def stage_a(m):
        for u, n in late:
            if n == m:
                axis = axes_of(u)[2]
                loads[UNITS[u][0]][m].wait() if u == 0 or u == 3 else None
                await_partner(u, m, 0)
                add(u, 2, m, moved(at, axis, 2), None, [from_other(u)])
                send_step(u, 2, m, 0)

    def stage_b(m):
        for u, n in late:
            if n == m:
                axis = axes_of(u)[2]
                await_partner(u, m, 1)
                await_step(u, 2, m, 0, recv)
                for side, by in ((0, 1), (1, -1)):
                    where = moved(at, axis, by)
                    add(u, 2, m, where, side, [from_other(u), from_buf(half_buf[u][2], side, u, 2)])
                    add(u, 2, m, where, 1 - side, [from_other(u)])
                send_step(u, 2, m, 1)

    def stage_c(m):
        for u, n in late:
            if n == m:
                await_partner(u, m, 2)
                await_step(u, 2, m, 1, recv)
                add(u, 2, m, at, None, [from_other(u)] + [from_buf(full_buf[u][2], side, u, 2) for side in (0, 1)])

    vec_step(0)
    stage_a(0)
    stage_a(1)
    vec_step(1)
    stage_b(0)
    stage_a(2)
    vec_step(2)
    stage_b(1)
    vec_step(3)
    stage_c(0)
    vec_step(4)
    stage_b(2)
    vec_step(5)
    stage_c(1)
    vec_step(6)
    stage_c(2)
    vec_step(7)
    for phase in (1, 0):
        for u in everything:
            send_step(u, phase, None, 0)
        for u in everything:
            axis = axes_of(u)[phase]
            await_step(u, phase, None, 0, recv)
            for side, by in ((0, 1), (1, -1)):
                add(u, phase, None, moved(at, axis, by), side, [from_buf(half_buf[u][phase], side, u, phase)])
            send_step(u, phase, None, 1)
        for u in everything:
            await_step(u, phase, None, 1, recv)
            add(
                u, phase, None, at, None, [from_buf(full_buf[u][phase], side, u, phase) for side in (0, 1)],
                None if phase else outs[UNITS[u][0]],
            )
    for u, m in late:
        part = other[UNITS[u][0]].at[pl.ds(m, 1), :, :, pl.ds(0, 32)]
        pltpu.make_async_copy(part, part, core_send.at[u, m]).wait()
        for step in (0, 1):
            await_step(u, 2, m, step, send)
    for u in everything:
        for phase in (0, 1):
            for step in (0, 1):
                await_step(u, phase, None, step, send)
    for k in range(7):
        vec_copy(k).wait_send()


def scatter_grads(main, small, vec):
    units = range(len(UNITS))
    n = len(UNITS)
    held = [(3, 2, 4, ROWS, 8 * WIDTH), (1, 2, 4, SMALL_ROWS, 8 * SMALL_WIDTH)]
    return pl.pallas_call(
        scatter_kernel,
        name="scatter_grads",
        out_shape=[
            jax.ShapeDtypeStruct((3, ROWS, WIDTH), jnp.float32),
            jax.ShapeDtypeStruct((1, SMALL_ROWS, SMALL_WIDTH), jnp.float32),
            jax.ShapeDtypeStruct((VEC_ROWS, 128), jnp.float32),
        ],
        in_specs=[pl.BlockSpec(memory_space=pl.ANY)] * 2 + [pl.BlockSpec(memory_space=pltpu.VMEM)],
        out_specs=[pl.BlockSpec(memory_space=pltpu.VMEM)] * 3,
        scratch_shapes=[pltpu.VMEM(s, jnp.bfloat16) for s in held + held]
        + [pltpu.VMEM(half_shape(u, p, 16), jnp.bfloat16) for u in units for p in range(3)]
        + [pltpu.VMEM(half_shape(u, p, 32), jnp.bfloat16) for u in units for p in range(3)]
        + [
            pltpu.VMEM((8, VEC_ROWS, 128), jnp.float32),
            pltpu.VMEM((7, VEC_ROWS, 128), jnp.float32),
            pltpu.SemaphoreType.DMA((2, 3)),
            pltpu.SemaphoreType.DMA((7,)),
            pltpu.SemaphoreType.DMA((7,)),
            pltpu.SemaphoreType.DMA((n, 5, 2)),
            pltpu.SemaphoreType.DMA((n, 5, 2)),
            pltpu.SemaphoreType.DMA((n, 3)),
            pltpu.SemaphoreType.DMA((n, 3, 3)),
        ],
        compiler_params=pltpu.CompilerParams(
            collective_id=3, has_side_effects=True, vmem_limit_bytes=58 * 2**20
        ),
    )(main, small, vec)


CHUNK = 256


def chain_kernel(forward, add_ref, keep_ref, out_ref, sending, arriving, send, recv):
    t = lax.axis_index("tensor")
    by = 1 if forward else 7
    is_first = t == (0 if forward else 7)
    is_last = t == (7 if forward else 0)
    barrier = pltpu.get_barrier_semaphore()
    for other in (tensor_peer(1), tensor_peer(7)):
        pl.semaphore_signal(barrier, inc=1, device_id=other, device_id_type=MESH)
    pl.semaphore_wait(barrier, 2)

    def copy(cols, g):
        return pltpu.make_async_remote_copy(
            src_ref=sending.at[:, cols], dst_ref=arriving.at[:, cols], send_sem=send.at[g], recv_sem=recv.at[g],
            device_id=tensor_peer(by), device_id_type=MESH,
        )

    chunks = add_ref.shape[1] // CHUNK

    @pl.loop(0, chunks)
    def _(g):
        cols = pl.ds(pl.multiple_of(g * CHUNK, CHUNK), CHUNK)

        @pl.when(is_first)
        def _():
            out_ref[:, cols] = jnp.zeros((add_ref.shape[0], CHUNK), jnp.float32)

        @pl.when(jnp.logical_not(is_first))
        def _():
            copy(cols, g).wait_recv()
            out_ref[:, cols] = arriving[:, cols].astype(jnp.float32)

        @pl.when(jnp.logical_not(is_last))
        def _():
            sending[:, cols] = (keep_ref[:, cols] * out_ref[:, cols] + add_ref[:, cols]).astype(jnp.bfloat16)
            copy(cols, g).start()

    @pl.when(jnp.logical_not(is_last))
    def _():
        @pl.loop(0, chunks)
        def _(g):
            cols = pl.ds(pl.multiple_of(g * CHUNK, CHUNK), CHUNK)
            copy(cols, g).wait_send()


def chain(add, keep, forward):
    chunks = add.shape[1] // CHUNK
    return pl.pallas_call(
        functools.partial(chain_kernel, forward),
        name="state_chain" if forward else "state_grad_chain",
        out_shape=jax.ShapeDtypeStruct(add.shape, jnp.float32),
        in_specs=[pl.BlockSpec(memory_space=pltpu.VMEM)] * 2,
        out_specs=pl.BlockSpec(memory_space=pltpu.VMEM),
        scratch_shapes=[
            pltpu.VMEM(add.shape, jnp.bfloat16),
            pltpu.VMEM(add.shape, jnp.bfloat16),
            pltpu.SemaphoreType.DMA((chunks,)),
            pltpu.SemaphoreType.DMA((chunks,)),
        ],
        compiler_params=pltpu.CompilerParams(
            collective_id=1 if forward else 2, has_side_effects=True, vmem_limit_bytes=32 * 2**20
        ),
    )(add, keep)


D, DI, HEADS, HEAD_DIM, STATE, TAPS, HALO = 1536, 3072, 48, 64, 128, 4, 16
BF16, F32 = jnp.bfloat16, jnp.float32


def silu_slope(values):
    sigmoid_val = jax.nn.sigmoid(values)
    return sigmoid_val * (1.0 + values * (1.0 - sigmoid_val))


def dot(a, b, dims):
    return lax.dot_general(a, b, ((dims[:1], dims[1:]), ((), ())), preferred_element_type=F32)


def conv(ext, kernel, bias_row, link):
    total = bias_row[None, :] + kernel[TAPS - 1][None, :] * ext[HALO:]
    for offset in range(1, TAPS):
        total = total + kernel[TAPS - 1 - offset][None, :] * ext[HALO - offset : -offset] * link[offset]
    return total


def conv_backward(grad_ext, ext, kernel, link_ext):
    grad_out = grad_ext[:BLOCK]
    grad_in = kernel[TAPS - 1][None, :] * grad_out
    rows = [None] * TAPS
    rows[TAPS - 1] = jnp.sum(grad_out * ext[HALO:], axis=0)
    for offset in range(1, TAPS):
        masked = grad_ext * link_ext[offset]
        rows[TAPS - 1 - offset] = jnp.sum(masked[:BLOCK] * ext[HALO - offset : -offset], axis=0)
        grad_in = grad_in + kernel[TAPS - 1 - offset][None, :] * masked[offset : offset + BLOCK]
    return grad_in, jnp.stack(rows, axis=0), jnp.sum(grad_out, axis=0)


def per_device(
    hidden,
    doc_ids,
    norm_gain,
    main_proj,
    step_proj,
    state_proj,
    conv_main,
    conv_main_bias,
    conv_state,
    conv_state_bias,
    step_bias,
    decay_log,
    skip_gain,
    gate_gain,
    out_proj,
    cotangent,
):
    t = lax.axis_index("tensor")
    shards = jnp.stack([main_proj[:, 1], main_proj[:, 0], out_proj])
    small = jnp.concatenate([state_proj, step_proj], axis=1).reshape(3, SMALL_ROWS, 38)
    small = jnp.pad(small.transpose(1, 0, 2).reshape(SMALL_ROWS, 114), ((0, 0), (0, 14)))[None]
    own_params = [conv_main, conv_main_bias, conv_state, conv_state_bias, step_bias, decay_log, skip_gain, gate_gain]
    params = jnp.concatenate([v.reshape(-1) for v in own_params])
    params = jnp.pad(params, (0, 20 * 128 - params.size)).reshape(20, 128)
    full, small_full, halo, params_all = gather_weights(shards, small, hidden[BLOCK - HALO :], params)
    w_x, w_gate, w_out = (full[i].reshape(D, DI) for i in range(3))
    w_small = small_full.reshape(16, SMALL_ROWS, 8, 128)[..., :114].reshape(16, SMALL_ROWS, 8, 3, 38)
    w_small = w_small.transpose(0, 3, 1, 2, 4).reshape(D, 8, 38)
    w_state, w_step = w_small[..., :32].reshape(D, 256), w_small[..., 32:].reshape(D, HEADS)
    flat = params_all.reshape(8, 20 * 128)
    position, full_params = 0, []
    for v in own_params:
        part = flat[:, position : position + v.size].reshape((8,) + v.shape)
        position += v.size
        full_params.append(jnp.moveaxis(part, 0, -2).reshape(v.shape[:-1] + (8 * v.shape[-1],)))
    conv_main, conv_main_bias, conv_state, conv_state_bias, step_bias, decay_log, skip_gain, gate_gain = full_params

    docs_all = jnp.concatenate([jnp.full((HALO,), -1, jnp.int32), doc_ids, jnp.full((8,), -2, jnp.int32)])
    docs = lax.dynamic_slice(docs_all, (t * BLOCK,), (HALO + BLOCK + 8,))
    doc_block = docs[HALO : HALO + BLOCK]
    doc_prev = docs[HALO - 1]
    link_ext = [None] + [
        (docs[HALO : HALO + BLOCK + 8] == docs[HALO - o : BLOCK + 8 + HALO - o]).astype(F32)[:, None]
        for o in range(1, TAPS)
    ]
    link = [None] + [v[:BLOCK] for v in link_ext[1:]]

    hidden_ext = jnp.concatenate([halo, hidden]).astype(F32)
    inv_ext = lax.rsqrt(jnp.mean(hidden_ext * hidden_ext, axis=1, keepdims=True) + epsilon)
    rows_ext = hidden_ext * inv_ext
    normed_ext = (rows_ext * norm_gain[None, :]).astype(BF16)
    normed, norm_rows, inv_rms = normed_ext[HALO:], rows_ext[HALO:], inv_ext[HALO:]
    hidden_float = hidden_ext[HALO:]

    x_ext = dot(normed_ext, w_x, (1, 0))
    state_ext = dot(normed_ext, w_state, (1, 0))
    gate_in = dot(normed, w_gate, (1, 0))
    step_in = dot(normed, w_step, (1, 0)) + step_bias[None, :]
    x_pre = conv(x_ext, conv_main, conv_main_bias, link)
    x_act = jax.nn.silu(x_pre).astype(BF16)
    state_pre = conv(state_ext, conv_state, conv_state_bias, link)
    state_act = jax.nn.silu(state_pre).astype(BF16)
    b_rows, c_rows = state_act[:, :STATE], state_act[:, STATE:]
    step = jax.nn.softplus(step_in)
    decay_rate = -jnp.exp(decay_log)

    x_heads = x_act.reshape(BLOCK, HEADS, HEAD_DIM)
    cum = jnp.cumsum(step * decay_rate[None, :], axis=0)
    cum_heads, step_heads = cum.T, step.T
    scores = dot(c_rows, b_rows, (1, 1))
    row_pos = lax.broadcasted_iota(jnp.int32, (BLOCK, BLOCK), 0)
    col_pos = lax.broadcasted_iota(jnp.int32, (BLOCK, BLOCK), 1)
    linked = (doc_block[:, None] == doc_block[None, :]) & (row_pos >= col_pos)
    spread_ = jnp.where(linked[None], cum_heads[:, :, None] - cum_heads[:, None, :], -10000.0)
    decay_mat = jnp.exp(spread_) * linked[None].astype(F32)
    decay_step = decay_mat * step_heads[:, None, :]
    mix_exact = scores[None] * decay_step
    mixing = mix_exact.astype(BF16)
    cum_end = cum[BLOCK - 1]
    end_link = (doc_block == doc_block[BLOCK - 1]).astype(F32)
    tail_decay = jnp.exp(cum_end[None, :] - cum) * end_link[:, None]
    weight = tail_decay * step
    enter = jnp.exp(cum) * (doc_block == doc_prev).astype(F32)[:, None]
    keep = jnp.exp(cum_end) * (doc_block[BLOCK - 1] == doc_prev).astype(F32)
    keep_row = jnp.repeat(keep, HEAD_DIM)[None, :]
    scaled = (weight.T[:, :, None] * b_rows.astype(F32)[None]).astype(BF16)
    update = jnp.einsum("hjn,jhp->nhp", scaled, x_heads, preferred_element_type=F32).reshape(STATE, DI)
    state_in = chain(update, keep_row, True)
    state_low = state_in.astype(BF16)
    carried = dot(c_rows, state_low, (1, 0))
    y_intra = jnp.einsum("hij,jhp->ihp", mixing, x_heads, preferred_element_type=F32).reshape(BLOCK, DI)
    enter_wide = jnp.repeat(enter, HEAD_DIM, axis=1)
    skip_wide = jnp.repeat(skip_gain, HEAD_DIM)[None, :]
    x_float = x_act.astype(F32)
    y_ssd = y_intra + carried * enter_wide + skip_wide * x_float

    gate_act = jax.nn.silu(gate_in)
    gated = y_ssd * gate_act
    gate_inv = lax.rsqrt(jnp.mean(gated * gated, axis=1, keepdims=True) + epsilon)
    gate_hat = gated * gate_inv
    gate_out = (gate_hat * gate_gain[None, :]).astype(BF16)
    mixed = (hidden_float + dot(gate_out, w_out, (1, 1))).astype(BF16)

    grad_out = dot(cotangent, gate_out, (0, 0)).astype(BF16)
    grad_gate = dot(cotangent, w_out, (1, 0))
    grad_gate_gain = jnp.sum(grad_gate * gate_hat, axis=0)
    gate_dn = grad_gate * gate_gain[None, :]
    inner = jnp.mean(gate_dn * gated, axis=1, keepdims=True)
    grad_gated = gate_inv * gate_dn - gated * gate_inv**3 * inner
    grad_y = (grad_gated * gate_act).astype(BF16)
    grad_gate_in = grad_gated * y_ssd * silu_slope(gate_in)

    dy_float = grad_y.astype(F32)
    dy_heads = grad_y.reshape(BLOCK, HEADS, HEAD_DIM)
    grad_carried = (dy_float * enter_wide).astype(BF16)
    grad_state = chain(dot(c_rows, grad_carried, (0, 0)), keep_row, False)

    grad_mix = jnp.einsum("ihp,jhp->hij", dy_heads, x_heads, preferred_element_type=F32)
    grad_x = jnp.einsum("hij,ihp->jhp", mixing, dy_heads, preferred_element_type=F32).reshape(BLOCK, DI)
    grad_x = grad_x + skip_wide * dy_float
    grad_scores = (grad_mix * decay_step).astype(BF16)
    grad_c = jnp.einsum("hij,jn->in", grad_scores, b_rows, preferred_element_type=F32)
    grad_b = jnp.einsum("hij,in->jn", grad_scores, c_rows, preferred_element_type=F32)
    pull = grad_mix * mix_exact
    grad_cum = (jnp.sum(pull, axis=2) - jnp.sum(pull, axis=1)).T
    grad_step = jnp.sum(grad_mix * scores[None] * decay_mat, axis=1).T
    by_head = lambda v: jnp.sum(v.reshape(-1, HEADS, HEAD_DIM), axis=2)
    grad_cum = grad_cum + by_head(dy_float * carried) * enter
    grad_c = grad_c + dot(grad_carried, state_low, (1, 1))
    grad_update = grad_state.astype(BF16)
    update_heads = grad_update.reshape(STATE, HEADS, HEAD_DIM)
    grad_scaled = jnp.einsum("jhp,nhp->hjn", x_heads, update_heads, preferred_element_type=F32)
    grad_x = grad_x + jnp.einsum("hjn,nhp->jhp", scaled, update_heads, preferred_element_type=F32).reshape(BLOCK, DI)
    grad_b = grad_b + jnp.sum(grad_scaled * weight.T[:, :, None], axis=0)
    grad_weight = jnp.sum(grad_scaled * b_rows.astype(F32)[None], axis=2).T
    weight_pull = grad_weight * weight
    grad_keep = jnp.sum(by_head(grad_state * state_in), axis=0)
    grad_end = jnp.sum(weight_pull, axis=0) + grad_keep * keep
    last_row = (lax.broadcasted_iota(jnp.int32, (BLOCK, 1), 0) == BLOCK - 1).astype(F32)
    grad_cum = grad_cum - weight_pull + last_row * grad_end[None, :]
    grad_step = grad_step + grad_weight * tail_decay
    grad_log = jnp.flip(jnp.cumsum(jnp.flip(grad_cum, 0), axis=0), 0)
    grad_step = grad_step + grad_log * decay_rate[None, :]
    grad_decay_log = jnp.sum(grad_log * step, axis=0) * decay_rate
    grad_skip = jnp.sum(by_head(dy_float * x_float), axis=0)
    grad_step_in = grad_step * jax.nn.sigmoid(step_in)
    grad_step_bias = jnp.sum(grad_step_in, axis=0)

    grad_pre = jnp.concatenate(
        [grad_x * silu_slope(x_pre), jnp.concatenate([grad_b, grad_c], axis=1) * silu_slope(state_pre)], axis=1
    )
    after = lax.ppermute(grad_pre[:8], "tensor", [(i, i - 1) for i in range(1, 8)])
    grad_pre = jnp.concatenate([grad_pre, after])
    grad_x_raw, grad_conv_main, grad_conv_main_bias = conv_backward(grad_pre[:, :DI], x_ext, conv_main, link_ext)
    grad_state_raw, grad_conv_state, grad_conv_state_bias = conv_backward(
        grad_pre[:, DI:], state_ext, conv_state, link_ext
    )
    grad_x_raw, grad_gate_in, grad_state_raw, grad_step_raw = (
        v.astype(BF16) for v in (grad_x_raw, grad_gate_in, grad_state_raw, grad_step_in)
    )
    grad_main = [dot(normed, v, (0, 0)).astype(BF16) for v in (grad_x_raw, grad_gate_in)]
    small_raw = jnp.concatenate([grad_state_raw.reshape(BLOCK, 8, 32), grad_step_raw.reshape(BLOCK, 8, 6)], axis=2)
    grad_small = dot(normed, small_raw.reshape(BLOCK, 8 * 38), (0, 0)).astype(BF16)
    grad_small = grad_small.reshape(16, 3, SMALL_ROWS, 8, 38).transpose(0, 2, 3, 1, 4).reshape(16, SMALL_ROWS, 8, 114)
    grad_small = jnp.pad(grad_small, ((0, 0), (0, 0), (0, 0), (0, 14)))
    grad_normed = (
        dot(grad_x_raw, w_x, (1, 1))
        + dot(grad_gate_in, w_gate, (1, 1))
        + dot(grad_step_raw, w_step, (1, 1))
        + dot(grad_state_raw, w_state, (1, 1))
    )
    grad_norm_gain = jnp.sum(grad_normed * norm_rows, axis=0)
    norm_dn = grad_normed * norm_gain[None, :]
    grad_hidden = (
        cotangent.astype(F32)
        + inv_rms * norm_dn
        - norm_rows * inv_rms * jnp.mean(norm_dn * norm_rows, axis=1, keepdims=True)
    )

    local = [
        grad_conv_main, grad_conv_main_bias, grad_conv_state, grad_conv_state_bias,
        grad_step_bias, grad_decay_log, grad_skip, grad_gate_gain, grad_norm_gain,
    ]
    by_tensor = [jnp.moveaxis(v.reshape(v.shape[:-1] + (8, -1)), -2, 0).reshape(8, -1) for v in local]
    vec = jnp.concatenate(by_tensor, axis=1)
    vec = jnp.pad(vec, ((0, 0), (0, VEC_ROWS * 16 - vec.shape[1]))).reshape(VEC_ROWS, 128)
    main_grads = jnp.stack(grad_main + [grad_out]).reshape(3, 2, 4, 2, ROWS, DI)
    own_main, own_small, vec = scatter_grads(main_grads, grad_small.reshape(1, 2, 4, 2, SMALL_ROWS, 1024), vec)
    vec = vec.reshape(8, VEC_ROWS * 16)
    own = lax.dynamic_index_in_dim(vec, t, 0, keepdims=False)
    results, position = [], 0
    for v in own_params:
        results.append(own[position : position + v.size].reshape(v.shape))
        position += v.size
    grad_norm_gain = vec[:, position : position + D // 8].reshape(D)
    own_small = own_small[0, :, :114].reshape(SMALL_ROWS, 3, 38).transpose(1, 0, 2).reshape(ROWS, 38)
    return (
        mixed,
        grad_hidden,
        grad_norm_gain,
        jnp.stack([own_main[1], own_main[0]], axis=1),
        own_small[:, 32:],
        own_small[:, :32],
        *results,
        own_main[2],
    )


def solution(mesh):
    placed = (
        P(("dp", "tensor"), None),
        P("dp"),
        P(),
        P("dp", None, "tensor"),
        P("dp", "tensor"),
        P("dp", "tensor"),
        P(None, "tensor"),
        P("tensor"),
        P(None, "tensor"),
        P("tensor"),
        P("tensor"),
        P("tensor"),
        P("tensor"),
        P("tensor"),
        P("dp", "tensor"),
        P(("dp", "tensor"), None),
    )
    return jax.shard_map(
        per_device,
        mesh=mesh,
        in_specs=placed,
        out_specs=(
            P(("dp", "tensor"), None),
            P(("dp", "tensor"), None),
            P(),
            P("dp", None, "tensor"),
            P("dp", "tensor"),
            P("dp", "tensor"),
            P(None, "tensor"),
            P("tensor"),
            P(None, "tensor"),
            P("tensor"),
            P("tensor"),
            P("tensor"),
            P("tensor"),
            P("tensor"),
            P("dp", "tensor"),
        ),
        check_vma=False,
    )
```

```python
import functools

import jax
import jax.numpy as jnp
from jax import lax
from jax.experimental import pallas as pl
from jax.experimental.pallas import tpu as pltpu
from jax.sharding import PartitionSpec as P

BLOCK = 256
epsilon = 1e-05

MESH = pl.DeviceIdType.MESH
AXES = (0, 1, 2)
SIDE = 4


def coordinates():
    dp = lax.axis_index("dp")
    t = lax.axis_index("tensor")
    z = lax.div(t, 4) * 2 + lax.div(dp, 8)
    return (lax.rem(t, 4), lax.rem(lax.div(dp, 2), 4), z), lax.rem(dp, 2)


def device(at, core):
    x, y, z = at
    return (lax.rem(z, 2) * 8 + y * 2 + core, lax.div(z, 2) * 4 + x)


def moved(at, axis, by):
    return tuple(lax.rem(v + by + SIDE, SIDE) if i == axis else v for i, v in enumerate(at))


def pieces(at, whole, width):
    x, y, z = at
    lo = pl.ds(0, 2) if 2 in whole else pl.ds(lax.rem(z, 2), 1)
    row = pl.ds(0, 4) if 1 in whole else pl.ds(y, 1)
    hi = lax.div(z, 2)
    if 0 in whole and 2 in whole:
        cols = [pl.ds(0, 8 * width)]
    elif 0 in whole:
        cols = [pl.ds(pl.multiple_of(hi * 4 * width, 128), 4 * width)]
    elif 2 in whole:
        cols = [
            pl.ds(pl.multiple_of(x * width, 128), width),
            pl.ds(pl.multiple_of((4 + x) * width, 128), width),
        ]
    else:
        cols = [pl.ds(pl.multiple_of((hi * 4 + x) * width, 128), width)]
    return [(lo, row, c) for c in cols]


def greet(at, core, group):
    barrier = pltpu.get_barrier_semaphore()
    others = [device(moved(at, axis, by), core) for axis in AXES for by in (1, -1)]
    others.append(device(at, 1 - core))
    others += group
    for other in others:
        pl.semaphore_signal(barrier, inc=1, device_id=other, device_id_type=MESH)
    pl.semaphore_wait(barrier, len(others))


def tensor_peer(by):
    return (lax.axis_index("dp"), lax.rem(lax.axis_index("tensor") + by, 8))


ROWS, WIDTH, SMALL_ROWS, SMALL_WIDTH = 96, 384, 32, 128
UNITS = [(0, q * 32, q) for q in range(3)] + [(1, 0, 0)]
WIDTHS = [WIDTH, SMALL_WIDTH]
STACK = [3, 1]


def axes_of(u):
    return [(UNITS[u][2] + j) % 3 for j in range(3)]


def region(ref, u, core, mats, where, whole, half=None):
    which, first, rows = UNITS[u][0], UNITS[u][1], 32
    if half is not None:
        first, rows = first + half * 16, 16
    return [
        ref.at[mats, lo, row, core, pl.ds(first, rows), cols]
        for lo, row, cols in pieces(where, whole, WIDTHS[which])
    ]


def sized(ref, u, mats, blocks, halves=2):
    width = WIDTHS[UNITS[u][0]]
    cols = min(blocks, 8)
    rest = blocks // cols
    return ref.at[mats, pl.ds(0, max(rest // 4, 1)), pl.ds(0, min(rest, 4)), 0, pl.ds(0, 16 * halves), pl.ds(0, cols * width)]


def gather_kernel(*refs):
    shards, small, tail, params = refs[0], refs[1], refs[2], refs[3:5]
    full, halo, params_all = refs[5:7], refs[7], refs[8:10]
    own_sem, halo_sem, param_send, param_recv, send, recv, core_send, core_recv = refs[10:]
    at, core = coordinates()
    t = lax.axis_index("tensor")
    own = []
    for w, source in enumerate((shards, small)):
        for lo, row, cols in pieces(at, (), WIDTHS[w]):
            own.append(
                pltpu.make_async_copy(source, full[w].at[:, lo.start, row.start, core, :, cols], own_sem.at[w])
            )
    def columns(i, of):
        width = params[i].shape[-1]
        return params_all[i].at[:, pl.ds(pl.multiple_of(of * width, 128), width)]

    for i in range(2):
        own.append(pltpu.make_async_copy(params[i], columns(i, t), own_sem.at[2 + i]))
    for c in own:
        c.start()
    greet(at, core, [tensor_peer(by) for by in range(1, 8)])
    last = []

    def go(copy, wait=True):
        copy.start()
        if wait:
            last.append(copy)

    def tail_copy():
        return pltpu.make_async_remote_copy(
            src_ref=tail, dst_ref=halo, send_sem=halo_sem.at[0], recv_sem=halo_sem.at[1],
            device_id=tensor_peer(1), device_id_type=MESH,
        )

    def param_copy(by, i, of):
        return pltpu.make_async_remote_copy(
            src_ref=params[i], dst_ref=columns(i, of), send_sem=param_send.at[i, by - 1],
            recv_sem=param_recv.at[i, by - 1], device_id=tensor_peer(by), device_id_type=MESH,
        )

    go(tail_copy())
    for by in range(1, 8):
        for i in range(2):
            go(param_copy(by, i, t))
    for c in own:
        c.wait()

    def slot(u, phase, m):
        return (phase if phase < 2 else 2 + m), [u]

    def mats_of(u, phase, m):
        return pl.ds(0, STACK[UNITS[u][0]]) if phase < 2 else pl.ds(m, 1)

    def sends(u, phase, m, step):
        axes = axes_of(u)
        whole, axis = axes[:phase], axes[phase]
        index = phase if phase < 2 else 2 + m
        ref = full[UNITS[u][0]]
        for kind, by in ((0, 1), (1, -1)):
            where = at if step == 0 else moved(at, axis, -by)
            for part in region(ref, u, core, mats_of(u, phase, m), where, whole, kind if step else None):
                pltpu.make_async_remote_copy(
                    src_ref=part, dst_ref=part, send_sem=send.at[u, index, step],
                    recv_sem=recv.at[u, index, step],
                    device_id=device(moved(at, axis, by), core), device_id_type=MESH,
                ).start()

    def await_step(u, phase, m, step, sem):
        index = phase if phase < 2 else 2 + m
        part = sized(full[UNITS[u][0]], u, mats_of(u, phase, m), 2 * 4**phase // (1 + step))
        pltpu.make_async_copy(part, part, sem.at[u, index, step]).wait()

    def to_partner(u, m, where, whole):
        for part in region(full[UNITS[u][0]], u, core, mats_of(u, 2, m), where, whole):
            pltpu.make_async_remote_copy(
                src_ref=part, dst_ref=part, send_sem=core_send.at[u, m],
                recv_sem=core_recv.at[u, m], device_id=device(at, 1 - core), device_id_type=MESH,
            ).start()

    everything = range(len(UNITS))
    late = [(u, m) for m in range(3) for u in everything if m < STACK[UNITS[u][0]]]
    for phase in (0, 1):
        for u in everything:
            sends(u, phase, 0, 0)
        for u in everything:
            await_step(u, phase, 0, 0, recv)
            sends(u, phase, 0, 1)
        for u in everything:
            await_step(u, phase, 0, 1, recv)
    for u, m in late:
        sends(u, 2, m, 0)
    for u, m in late:
        to_partner(u, m, at, axes_of(u)[:2])
    for u, m in late:
        await_step(u, 2, m, 0, recv)
        sends(u, 2, m, 1)
        whole, axis = axes_of(u)[:2], axes_of(u)[2]
        for by in (-1, 1):
            to_partner(u, m, moved(at, axis, by), whole)
    for u, m in late:
        await_step(u, 2, m, 1, recv)
        whole, axis = axes_of(u)[:2], axes_of(u)[2]
        to_partner(u, m, moved(at, axis, 2), whole)
    for u, m in late:
        part = sized(full[UNITS[u][0]], u, mats_of(u, 2, m), 64)
        pltpu.make_async_copy(part, part, core_recv.at[u, m]).wait()
        pltpu.make_async_copy(part, part, core_send.at[u, m]).wait()
    tail_copy().wait_recv()
    for by in range(1, 8):
        for i in range(2):
            param_copy(by, i, lax.rem(t + 8 - by, 8)).wait_recv()
    for u in everything:
        for phase in (0, 1):
            for step in (0, 1):
                await_step(u, phase, 0, step, send)
    for u, m in late:
        for step in (0, 1):
            await_step(u, 2, m, step, send)
    for c in last:
        c.wait_send()


def gather_weights(shards, small, tail, params):
    units = len(UNITS)
    return pl.pallas_call(
        gather_kernel,
        name="gather_weights",
        out_shape=[
            jax.ShapeDtypeStruct((3, 2, 4, 2, ROWS, 8 * WIDTH), jnp.bfloat16),
            jax.ShapeDtypeStruct((1, 2, 4, 2, SMALL_ROWS, 8 * SMALL_WIDTH), jnp.bfloat16),
            jax.ShapeDtypeStruct(tail.shape, tail.dtype),
        ]
        + [jax.ShapeDtypeStruct((8, 8 * p.shape[1]), p.dtype) for p in params],
        in_specs=[pl.BlockSpec(memory_space=pl.ANY)] * 5,
        out_specs=[pl.BlockSpec(memory_space=pl.ANY)] * 5,
        scratch_shapes=[
            pltpu.SemaphoreType.DMA((4,)),
            pltpu.SemaphoreType.DMA((2,)),
            pltpu.SemaphoreType.DMA((2, 7)),
            pltpu.SemaphoreType.DMA((2, 7)),
            pltpu.SemaphoreType.DMA((units, 5, 2)),
            pltpu.SemaphoreType.DMA((units, 5, 2)),
            pltpu.SemaphoreType.DMA((units, 3)),
            pltpu.SemaphoreType.DMA((units, 3)),
        ],
        compiler_params=pltpu.CompilerParams(collective_id=0, has_side_effects=True),
    )(shards, small, tail, *params)


VEC = (8, 8 * WIDTH + 384)


def spread(whole):
    return (2 if 2 in whole else 1, 4 if 1 in whole else 1, (4 if 0 in whole else 1) * (2 if 2 in whole else 1))


def half_shape(u, phase, rows):
    lo, y, cols = spread(axes_of(u)[:phase])
    which = UNITS[u][0]
    return (2, STACK[which], lo, y, rows, cols * WIDTHS[which])


def scatter_kernel(*refs):
    grads, vec = refs[0:3], refs[3]
    outs, vec_out = refs[4:6], refs[6]
    refs = refs[1:]
    own, other = refs[6:8], refs[8:10]

    def grad_of(which, m):
        return (grads[2], 0) if which else (grads[1], 0) if m == 2 else (grads[0], m)

    def load(w, m):
        ref, i = grad_of(w, m)
        return pltpu.make_async_copy(ref.at[i, :, :, core], own[w].at[m], own_sem.at[w, m])

    units = len(UNITS)
    half_buf = [[refs[10 + 3 * u + p] for p in range(3)] for u in range(units)]
    full_buf = [[refs[10 + 3 * (units + u) + p] for p in range(3)] for u in range(units)]
    rest = refs[10 + 6 * units :]
    vec_acc, vec_in, own_sem, vec_send, vec_recv, send, recv, core_send, core_recv = rest
    at, core = coordinates()
    loads = [
        [load(w, m) for m in range(STACK[w])]
        for w in range(2)
    ]
    for w in range(2):
        for c in loads[w]:
            c.start()
    greet(at, core, [device(moved(at, axis, 2), core) for axis in AXES])

    everything = range(units)
    late = [(u, m) for m in range(3) for u in everything if m < STACK[UNITS[u][0]]]

    def part_of(ref, u, mats, where, whole, half=None):
        which, first, rows = UNITS[u][0], UNITS[u][1], 32
        if half is not None:
            first, rows = first + half * 16, 16
        return [ref.at[mats, lo, y, pl.ds(first, rows), cols] for lo, y, cols in pieces(where, whole, WIDTHS[which])]

    groups = [[2], [1, -1], [0]]

    for u, m in late:
        axes = axes_of(u)
        which = UNITS[u][0]
        source, index = grad_of(which, m)
        for g, group in enumerate(groups):
            for by in group:
                where = moved(at, axes[2], by) if by else at
                for src, dst in zip(
                    region(source, u, 1 - core, pl.ds(index, 1), where, axes[:2]),
                    part_of(other[which], u, pl.ds(m, 1), where, axes[:2]),
                ):
                    pltpu.make_async_remote_copy(
                        src_ref=src, dst_ref=dst, send_sem=core_send.at[u, m], recv_sem=core_recv.at[u, m, g],
                        device_id=device(at, 1 - core), device_id_type=MESH,
                    ).start()

    def await_partner(u, m, g):
        which = UNITS[u][0]
        rows = 2 * len(groups[g])
        part = other[which].at[pl.ds(m, 1), pl.ds(0, 1), pl.ds(0, rows), pl.ds(0, 32)]
        pltpu.make_async_copy(part, part, core_recv.at[u, m, g]).wait()

    def add(u, phase, m, where, half, terms, result=None):
        which, first, rows = UNITS[u][0], UNITS[u][1], 32
        if half is not None:
            first, rows = first + half * 16, 16
        whole = axes_of(u)[:phase]
        n_lo, n_y, _ = spread(whole)
        mats = STACK[which] if m is None else 1
        for i, (lo, y, cols) in enumerate(pieces(where, whole, WIDTHS[which])):

            @pl.loop(0, mats * n_lo * n_y)
            def _(k, i=i, lo=lo, y=y, cols=cols):
                mat = lax.div(k, n_lo * n_y) if m is None else m
                a, b = lax.rem(lax.div(k, n_y), n_lo), lax.rem(k, n_y)
                here = (mat, lo.start + a, y.start + b, pl.ds(first, rows), cols)
                total = own[which][here].astype(jnp.float32)
                for term in terms:
                    total = total + term(mat, i, a, b, here).astype(jnp.float32)
                if result is None:
                    own[which][here] = total.astype(jnp.bfloat16)
                else:
                    result[mat, pl.ds(first, rows), :] = total

    def from_other(u):
        return lambda mat, i, a, b, here: other[UNITS[u][0]][here]

    def from_buf(ref, side, u, phase):
        which = UNITS[u][0]
        whole = axes_of(u)[:phase]
        width = spread(whole)[2] * WIDTHS[which] // (2 if 2 in whole and 0 not in whole else 1)
        return lambda mat, i, a, b, here: ref[side, mat, a, b, :, pl.ds(i * width, width)]

    def send_step(u, phase, m, step):
        axes = axes_of(u)
        whole, axis = axes[:phase], axes[phase]
        which = UNITS[u][0]
        mats = pl.ds(0, STACK[which]) if m is None else pl.ds(m, 1)
        index = phase if m is None else 2 + m
        buf = half_buf[u][phase] if step == 0 else full_buf[u][phase]
        for side, by in ((0, 1), (1, -1)):
            where = moved(at, axis, 2 if step == 0 else by)
            sources = part_of(own[which], u, mats, where, whole, side if step == 0 else None)
            width = buf.shape[-1] // len(sources)
            for i, src in enumerate(sources):
                pltpu.make_async_remote_copy(
                    src_ref=src, dst_ref=buf.at[side, mats, :, :, :, pl.ds(i * width, width)],
                    send_sem=send.at[u, index, step], recv_sem=recv.at[u, index, step],
                    device_id=device(moved(at, axis, by), core), device_id_type=MESH,
                ).start()

    def await_step(u, phase, m, step, sem):
        index = phase if m is None else 2 + m
        buf = half_buf[u][phase] if step == 0 else full_buf[u][phase]
        part = buf if m is None else buf.at[:, pl.ds(m, 1)]
        pltpu.make_async_copy(part, part, sem.at[u, index, step]).wait()

    def vec_copy(k):
        (x, y, z) = at
        flip = lambda v: v + 1 - 2 * lax.rem(v, 2)
        to = [
            device(at, 1 - core),
            device((flip(x), y, z), core),
            device((x, flip(y), z), core),
            device((x, y, flip(z)), core),
            device(moved(at, 0, 2), core),
            device(moved(at, 1, 2), core),
            device(moved(at, 2, 2), core),
        ][k]
        return pltpu.make_async_remote_copy(
            src_ref=vec_acc.at[k], dst_ref=vec_in.at[k], send_sem=vec_send.at[k], recv_sem=vec_recv.at[k],
            device_id=to, device_id_type=MESH,
        )

    def vec_step(k):
        if k == 0:
            vec_acc[0] = vec[...]
        else:
            vec_copy(k - 1).wait_recv()
            vec_acc[k] = vec_acc[k - 1] + vec_in[k - 1]
        if k < 7:
            vec_copy(k).start()
        else:
            vec_out[...] = vec_acc[7]

    def stage_a(m):
        for u, n in late:
            if n == m:
                axis = axes_of(u)[2]
                loads[UNITS[u][0]][m].wait() if u == 0 or u == 3 else None
                await_partner(u, m, 0)
                add(u, 2, m, moved(at, axis, 2), None, [from_other(u)])
                send_step(u, 2, m, 0)

    def stage_b(m):
        for u, n in late:
            if n == m:
                axis = axes_of(u)[2]
                await_partner(u, m, 1)
                await_step(u, 2, m, 0, recv)
                for side, by in ((0, 1), (1, -1)):
                    where = moved(at, axis, by)
                    add(u, 2, m, where, side, [from_other(u), from_buf(half_buf[u][2], side, u, 2)])
                    add(u, 2, m, where, 1 - side, [from_other(u)])
                send_step(u, 2, m, 1)

    def stage_c(m):
        for u, n in late:
            if n == m:
                await_partner(u, m, 2)
                await_step(u, 2, m, 1, recv)
                add(u, 2, m, at, None, [from_other(u)] + [from_buf(full_buf[u][2], side, u, 2) for side in (0, 1)])

    vec_step(0)
    stage_a(0)
    stage_a(1)
    vec_step(1)
    stage_b(0)
    stage_a(2)
    vec_step(2)
    stage_b(1)
    vec_step(3)
    stage_c(0)
    vec_step(4)
    stage_b(2)
    vec_step(5)
    stage_c(1)
    vec_step(6)
    stage_c(2)
    vec_step(7)
    for phase in (1, 0):
        for u in everything:
            send_step(u, phase, None, 0)
        for u in everything:
            axis = axes_of(u)[phase]
            await_step(u, phase, None, 0, recv)
            for side, by in ((0, 1), (1, -1)):
                add(u, phase, None, moved(at, axis, by), side, [from_buf(half_buf[u][phase], side, u, phase)])
            send_step(u, phase, None, 1)
        for u in everything:
            await_step(u, phase, None, 1, recv)
            add(
                u, phase, None, at, None, [from_buf(full_buf[u][phase], side, u, phase) for side in (0, 1)],
                None if phase else outs[UNITS[u][0]],
            )
    for u, m in late:
        part = other[UNITS[u][0]].at[pl.ds(m, 1), :, :, pl.ds(0, 32)]
        pltpu.make_async_copy(part, part, core_send.at[u, m]).wait()
        for step in (0, 1):
            await_step(u, 2, m, step, send)
    for u in everything:
        for phase in (0, 1):
            for step in (0, 1):
                await_step(u, phase, None, step, send)
    for k in range(7):
        vec_copy(k).wait_send()


def scatter_grads(main, out, small, vec):
    units = range(len(UNITS))
    n = len(UNITS)
    held = [(3, 2, 4, ROWS, 8 * WIDTH), (1, 2, 4, SMALL_ROWS, 8 * SMALL_WIDTH)]
    return pl.pallas_call(
        scatter_kernel,
        name="scatter_grads",
        out_shape=[
            jax.ShapeDtypeStruct((3, ROWS, WIDTH), jnp.float32),
            jax.ShapeDtypeStruct((1, SMALL_ROWS, SMALL_WIDTH), jnp.float32),
            jax.ShapeDtypeStruct(VEC, jnp.float32),
        ],
        in_specs=[pl.BlockSpec(memory_space=pl.ANY)] * 3 + [pl.BlockSpec(memory_space=pltpu.VMEM)],
        out_specs=[pl.BlockSpec(memory_space=pltpu.VMEM)] * 3,
        scratch_shapes=[pltpu.VMEM(s, jnp.bfloat16) for s in held + held]
        + [pltpu.VMEM(half_shape(u, p, 16), jnp.bfloat16) for u in units for p in range(3)]
        + [pltpu.VMEM(half_shape(u, p, 32), jnp.bfloat16) for u in units for p in range(3)]
        + [
            pltpu.VMEM((8,) + VEC, jnp.float32),
            pltpu.VMEM((7,) + VEC, jnp.float32),
            pltpu.SemaphoreType.DMA((2, 3)),
            pltpu.SemaphoreType.DMA((7,)),
            pltpu.SemaphoreType.DMA((7,)),
            pltpu.SemaphoreType.DMA((n, 5, 2)),
            pltpu.SemaphoreType.DMA((n, 5, 2)),
            pltpu.SemaphoreType.DMA((n, 3)),
            pltpu.SemaphoreType.DMA((n, 3, 3)),
        ],
        compiler_params=pltpu.CompilerParams(
            collective_id=3, has_side_effects=True, vmem_limit_bytes=58 * 2**20
        ),
    )(main, out, small, vec)


D, DI, HEADS, HEAD_DIM, STATE, TAPS, HALO = 1536, 3072, 48, 64, 128, 4, 16
BF16, F32 = jnp.bfloat16, jnp.float32
TILE, LANES, SMALL = 512, 128, 384
TILES = DI // TILE
LOG2E = 1.4426950408889634
EXT = HALO + BLOCK
VMEM = pltpu.VMEM


def dot(a, b, dims=(1, 0), precision=None):
    return lax.dot_general(
        a, b, ((dims[:1], dims[1:]), ((), ())), precision=precision, preferred_element_type=F32
    )


def iota(shape, dim):
    return lax.broadcasted_iota(jnp.int32, shape, dim)


def sigmoid(v):
    return 1.0 / (1.0 + jnp.exp(-v))


def silu(v):
    return v * sigmoid(v)


def silu_slope(v):
    s = sigmoid(v)
    return s * (1.0 + v * (1.0 - s))


def softplus(v):
    return jnp.maximum(v, 0.0) + jnp.log1p(jnp.exp(-jnp.abs(v)))


def split(v):
    high = v.astype(BF16)
    return high, (v - high.astype(F32)).astype(BF16)


def head_map(j):
    return (iota((LANES, TILE), 0) == j * (TILE // HEAD_DIM) + iota((LANES, TILE), 1) // HEAD_DIM).astype(BF16)


def widen(v, j):
    high, low = split(v)
    return dot(high, head_map(j)) + dot(low, head_map(j))


def by_head(v, j):
    high, low = split(v)
    return dot(high, head_map(j), (1, 1)) + dot(low, head_map(j), (1, 1))


def small_map(r):
    row, col = iota((8 * LANES, SMALL), 0), iota((8 * LANES, SMALL), 1)
    t, lane = row // LANES, row % LANES - 38 * r
    state = (lane >= 0) & (lane < 32) & (col == t * 32 + lane)
    step = (lane >= 32) & (lane < 38) & (col == 256 + t * 6 + lane - 32)
    return (state | step).astype(BF16)


def tile_of(j):
    return pl.ds(pl.multiple_of(j * TILE, TILE), TILE)


def conv_links(doc_col, offset, rows):
    return (doc_col[HALO : HALO + rows] == doc_col[HALO - offset : HALO - offset + rows]).astype(F32)


def conv(ext, taps, bias, links):
    total = bias + taps[TAPS - 1 : TAPS] * ext[HALO:]
    for offset in range(1, TAPS):
        total = total + taps[TAPS - 1 - offset : TAPS - offset] * ext[HALO - offset : EXT - offset] * links[offset]
    return total


def small_params(phead):
    return dot(phead, small_map(0).astype(F32), precision=lax.Precision.HIGHEST)


def decay_terms(step, cum, doc_col, doc_prev):
    block = doc_col[HALO:EXT]
    end = cum[BLOCK - 1 : BLOCK]
    tail = jnp.exp(end - cum) * (block == block[BLOCK - 1 : BLOCK]).astype(F32)
    enter = jnp.exp(cum) * (block == doc_prev).astype(F32)
    keep = jnp.exp(end) * (block[BLOCK - 1 : BLOCK] == doc_prev).astype(F32)
    return enter, tail, tail * step, keep


def front_kernel(
    hidden, halo, gain, full, packed, pmain, phead, doc_col,
    normed_out, x_ext, x_pre, x_act, gate_in, update, raw_out, state_pre, bc, steps, scores,
    w_small, w_x, w_gate, normed, weight_ref, sems,
):
    loads = []
    for m, w in ((0, w_x), (1, w_gate)):
        for j in range(TILES):
            cols = pl.ds(j * TILE, TILE)
            loads.append(pltpu.make_async_copy(full.at[m, :, cols], w.at[:, cols], sems.at[m, j]))
    for c in loads:
        c.start()
    for rows, part in ((pl.ds(0, HALO), halo), (pl.ds(HALO, BLOCK), hidden)):
        value = part[...].astype(F32)
        inv = lax.rsqrt(jnp.mean(value * value, axis=1, keepdims=True) + epsilon)
        normed[rows] = (value * inv * gain[...]).astype(BF16)
    normed_out[...] = normed[pl.ds(HALO, BLOCK)]
    for r in range(3):
        rows = dot(packed[...], small_map(r)).astype(BF16)
        for d in range(16):
            w_small[pl.ds(d * 96 + r * 32, 32)] = rows[d * 32 : d * 32 + 32]
    raw = dot(normed[...], w_small[...])
    raw_out[...] = raw
    params = small_params(phead[...])
    docs = doc_col[...]
    links = [None] + [conv_links(docs, o, BLOCK) for o in range(1, TAPS)]
    pre = conv(raw[:, :256], params[:TAPS, :256], params[TAPS : TAPS + 1, :256], links)
    state_pre[...] = pre
    act = silu(pre).astype(BF16)
    bc[...] = act
    b_rows, c_rows = act[:, :STATE], act[:, STATE:]
    scores[...] = dot(c_rows, b_rows, (1, 1))
    step_in = raw[HALO:, 256:] + params[5:6, 256:]
    step = softplus(step_in)
    log_step = step * -jnp.exp(params[6:7, 256:])
    lower = (iota((BLOCK, BLOCK), 0) >= iota((BLOCK, BLOCK), 1)).astype(F32)
    cum = dot(lower, log_step, precision=lax.Precision.HIGHEST)
    steps[0] = step_in
    steps[1] = step
    steps[2] = cum
    weight_ref[...] = decay_terms(step, cum, docs, docs[HALO - 1 : HALO])[2]

    @pl.loop(0, TILES)
    def _(j):
        cols = tile_of(j)
        pltpu.make_async_copy(full.at[0, :, cols], w_x.at[:, cols], sems.at[0, j]).wait()
        ext = dot(normed[...], w_x[:, cols])
        x_ext[:, cols] = ext
        pre = conv(ext, pmain[0:TAPS, cols], pmain[TAPS : TAPS + 1, cols], links)
        x_pre[:, cols] = pre
        act = silu(pre).astype(BF16)
        x_act[:, cols] = act
        heavy = (act.astype(F32) * widen(weight_ref[...], j)).astype(BF16)
        update[:, cols] = dot(bc[:, :STATE], heavy, (0, 0))

    @pl.loop(0, TILES)
    def _(j):
        cols = tile_of(j)
        pltpu.make_async_copy(full.at[1, :, cols], w_gate.at[:, cols], sems.at[1, j]).wait()
        gate_in[:, cols] = dot(normed[pl.ds(HALO, BLOCK)], w_gate[:, cols])


def front(hidden, halo, gain, full, packed, pmain, phead, doc_col):
    shapes = [
        ((BLOCK, D), BF16), ((EXT, DI), F32), ((BLOCK, DI), F32), ((BLOCK, DI), BF16), ((BLOCK, DI), F32),
        ((STATE, DI), F32), ((EXT, SMALL), F32), ((BLOCK, 256), F32), ((BLOCK, 256), BF16),
        ((3, BLOCK, LANES), F32), ((BLOCK, BLOCK), F32), ((D, SMALL), BF16),
    ]
    vmem = pl.BlockSpec(memory_space=VMEM)
    return pl.pallas_call(
        front_kernel,
        name="front",
        out_shape=[jax.ShapeDtypeStruct(*s) for s in shapes],
        in_specs=[vmem] * 3 + [pl.BlockSpec(memory_space=pl.ANY)] + [vmem] * 4,
        out_specs=[vmem] * len(shapes),
        scratch_shapes=[
            VMEM((D, DI), BF16), VMEM((D, DI), BF16), VMEM((EXT, D), BF16),
            VMEM((BLOCK, LANES), F32), pltpu.SemaphoreType.DMA((2, TILES)),
        ],
        compiler_params=pltpu.CompilerParams(vmem_limit_bytes=58 * 2**20),
    )(hidden, halo, gain, full, packed, pmain, phead, doc_col)


def pack_params(conv_main, conv_main_bias, conv_state, conv_state_bias, step_bias, decay_log, skip_gain, gate_gain):
    main = jnp.concatenate(
        [conv_main, conv_main_bias[None], gate_gain[None], jnp.repeat(skip_gain, HEAD_DIM)[None],
         jnp.zeros((1, WIDTH), F32)]
    )
    state = jnp.pad(jnp.concatenate([conv_state, conv_state_bias[None]]), ((0, 3), (0, 96)))
    heads = jnp.pad(jnp.stack([step_bias, decay_log, skip_gain]), ((5, 0), (32, 90)))
    return main, state + heads


PAIR = 2 * HEAD_DIM
PAIRS = DI // PAIR
HALF = BLOCK // 2
FORWARD_LAG, BACKWARD_LAG = 4, 2


def pair_of(p):
    return pl.ds(pl.multiple_of(p * PAIR, PAIR), PAIR)


def only(value, first):
    lane = iota(value.shape, 1)
    return jnp.where((lane < HEAD_DIM) == first, value, jnp.zeros_like(value))


def head_column(ref, h):
    return pltpu.roll(ref[...], lax.rem(LANES - h, LANES), axis=1)[:, :1]


def mid_kernel(
    x_act, gate_in, update, bc, steps, scores, doc_col, doc_row, pmain, phead, hidden, cot, full,
    mixed, grad_out, grad_gate_in, grad_x, grad_bc, grad_step_in, vec_gate, vec_heads,
    w_out, cot_t, grad_add, y, work, gate_out, dy, state, state_low, grad_state, keep_row, f_out, f_in, b_out, b_in,
    barred, cum2, cum_t, step_t, enter_ref, weight_ref, rows_acc, q_t, gs, acc_c, acc_heads, row_acc,
    w_sem, f_send, f_recv, b_send, b_recv,
):
    t = lax.axis_index("tensor")
    load = pltpu.make_async_copy(full.at[2], w_out, w_sem.at[0])
    load.start()
    barrier = pltpu.get_barrier_semaphore()
    for other in (tensor_peer(1), tensor_peer(7)):
        pl.semaphore_signal(barrier, inc=1, device_id=other, device_id_type=MESH)
    pl.semaphore_wait(barrier, 2)

    docs = doc_col[...]
    params = small_params(phead[...])
    rate = -jnp.exp(params[6:7, 256:])
    step, cum = steps[1], steps[2]
    enter, tail, weight, keep = decay_terms(step, cum, docs, docs[HALO - 1 : HALO])
    enter_ref[...] = enter
    weight_ref[...] = weight
    cum2[...] = cum * LOG2E
    for ref, turned in ((cum_t, (cum * LOG2E).T), (step_t, step.T)):
        for h in range(HEADS):
            ref[h] = turned[h : h + 1]
    linked = (docs[HALO:EXT] == doc_row[...]) & (iota((BLOCK, BLOCK), 0) >= iota((BLOCK, BLOCK), 1))
    barred[...] = jnp.where(linked, 0.0, -1e30)
    keep8 = jnp.broadcast_to(keep, (8, LANES))
    cot_t[...] = cot[...].T

    @pl.loop(0, TILES)
    def _(j):
        keep_row[:, tile_of(j)] = widen(keep8, j)

    def chain(forward, c, add, into, outgoing, incoming, send, recv):
        cols = pair_of(c)
        by = 1 if forward else 7
        is_first = t == (0 if forward else 7)
        is_last = t == (7 if forward else 0)

        def copy():
            return pltpu.make_async_remote_copy(
                src_ref=outgoing.at[:, cols], dst_ref=incoming.at[:, cols], send_sem=send.at[c],
                recv_sem=recv.at[c], device_id=tensor_peer(by), device_id_type=MESH,
            )

        @pl.when(is_first)
        def _():
            into[:, cols] = jnp.zeros((STATE, PAIR), F32)

        @pl.when(jnp.logical_not(is_first))
        def _():
            copy().wait_recv()
            into[:, cols] = incoming[:, cols].astype(F32)

        @pl.when(jnp.logical_not(is_last))
        def _():
            outgoing[:, cols] = (keep_row[0:1, cols] * into[:, cols] + add[:, cols]).astype(BF16)
            copy().start()

        return copy

    halves = [(slice(0, HALF), slice(0, HALF)), (slice(HALF, BLOCK), slice(0, BLOCK))]

    def decay_of(h, column, rows, cols):
        return jnp.exp2(column[rows] - cum_t[h, :, cols] + barred[rows, cols])

    def intra_forward(p):
        cols = pair_of(p)
        x = x_act[:, cols]
        x2 = [only(x, True), only(x, False)]
        columns = [head_column(cum2, 2 * p + k) for k in (0, 1)]
        for rows, js in halves:
            mix = [
                (scores[rows, js] * (decay_of(2 * p + k, columns[k], rows, js) * step_t[2 * p + k, :, js])).astype(BF16)
                for k in (0, 1)
            ]
            y[rows, cols] = dot(jnp.concatenate(mix, 1), jnp.concatenate([v[js] for v in x2], 0))

    lag = FORWARD_LAG * t

    @pl.loop(0, PAIRS + lag)
    def _(i):
        @pl.when(i < PAIRS)
        def _():
            intra_forward(i)

        @pl.when(i >= lag)
        def _():
            chain(True, i - lag, update, state, f_out, f_in, f_send, f_recv)

    row_acc[...] = jnp.zeros_like(row_acc)

    @pl.loop(0, TILES)
    def _(j):
        cols = tile_of(j)
        low = state[:, cols].astype(BF16)
        state_low[:, cols] = low
        carried = dot(bc[:, STATE:], low)
        value = y[:, cols] + carried * widen(enter_ref[...], j) + pmain[6:7, cols] * x_act[:, cols].astype(F32)
        y[:, cols] = value
        gated = value * silu(gate_in[:, cols])
        row_acc[...] += jnp.broadcast_to(jnp.sum(gated * gated, axis=1, keepdims=True), (BLOCK, LANES))

    gate_inv = lax.rsqrt(row_acc[:, :1] / DI + epsilon)
    row_acc[...] = jnp.zeros_like(row_acc)
    load.wait()

    @pl.loop(0, TILES)
    def _(j):
        cols = tile_of(j)
        gated = y[:, cols] * silu(gate_in[:, cols])
        hat = gated * gate_inv
        gain = pmain[5:6, cols]
        out = (hat * gain).astype(BF16)
        gate_out[:, cols] = out
        grad_out[:, cols] = dot(cot_t[...], out).astype(BF16)
        grad_gate = dot(cot[...], w_out[:, cols])
        vec_gate[:, cols] = jnp.broadcast_to(jnp.sum(grad_gate * hat, axis=0, keepdims=True), (8, TILE))
        dn = grad_gate * gain
        work[:, cols] = dn
        row_acc[...] += jnp.broadcast_to(jnp.sum(dn * gated, axis=1, keepdims=True), (BLOCK, LANES))

    inner = row_acc[:, :1] / DI * gate_inv * gate_inv * gate_inv
    acc_c[...] = jnp.zeros_like(acc_c)
    acc_heads[...] = jnp.zeros_like(acc_heads)

    @pl.loop(0, TILES)
    def _(j):
        cols = tile_of(j)
        gate, value = gate_in[:, cols], y[:, cols]
        s = sigmoid(gate)
        act = gate * s
        grad_gated = gate_inv * work[:, cols] - value * act * inner
        grad = (grad_gated * act).astype(BF16)
        dy[:, cols] = grad
        grad_gate_in[:, cols] = (grad_gated * value * (s * (1.0 + gate * (1.0 - s)))).astype(BF16)
        grad = grad.astype(F32)
        carried_grad = (grad * widen(enter_ref[...], j)).astype(BF16)
        low = state_low[:, cols]
        work_cols = dot(bc[:, STATE:], carried_grad, (0, 0))
        grad_add[:, cols] = work_cols
        acc_c[...] += dot(carried_grad, low, (1, 1))
        acc_heads[0] += by_head(grad * dot(bc[:, STATE:], low), j)

    rows_acc[...] = jnp.zeros_like(rows_acc)
    gs[...] = jnp.zeros_like(gs)

    def intra_backward(p):
        cols = pair_of(p)
        x, grad = x_act[:, cols], dy[:, cols]
        grad2 = [only(grad, True), only(grad, False)]
        columns = [head_column(cum2, 2 * p + k) for k in (0, 1)]
        lane = iota((HALF, LANES), 1)
        parts = []
        q_rows = [[], []]
        for rows, js in halves:
            mixes = []
            gs_sum = gs[rows, js]
            pulls = jnp.zeros((HALF, LANES), F32)
            for k in (0, 1):
                h = 2 * p + k
                decay = decay_of(h, columns[k], rows, js)
                decay_step = decay * step_t[h, :, js]
                mixes.append((scores[rows, js] * decay_step).astype(BF16))
                grad_mix = dot(grad2[k][rows], x[js], (1, 1))
                gs_sum = gs_sum + grad_mix * decay_step
                q = grad_mix * scores[rows, js] * decay
                q_rows[k].append(jnp.sum(q, axis=0, keepdims=True))
                pull = jnp.sum(q * step_t[h, :, js], axis=1, keepdims=True)
                pulls = jnp.where(lane == h, pull, pulls)
            gs[rows, js] = gs_sum
            rows_acc[rows] += pulls
            parts.append(dot(jnp.concatenate(mixes, 0), jnp.concatenate([v[rows] for v in grad2], 0), (0, 0)))
        grad_x[pl.ds(0, HALF), cols] = parts[0] + parts[1][:HALF]
        grad_x[pl.ds(HALF, HALF), cols] = parts[1][HALF:]
        for k in (0, 1):
            first, second = q_rows[k]
            q_t[2 * p + k, :, 0:HALF] = first + second[:, :HALF]
            q_t[2 * p + k, :, HALF:BLOCK] = second[:, HALF:]

    back_lag = BACKWARD_LAG * (7 - t)

    @pl.loop(0, PAIRS + back_lag)
    def _(i):
        @pl.when(i < PAIRS)
        def _():
            intra_backward(i)

        @pl.when(i >= back_lag)
        def _():
            chain(False, i - back_lag, grad_add, grad_state, b_out, b_in, b_send, b_recv)

    gs_low = gs[...].astype(BF16)
    grad_bc[:, STATE:] = acc_c[...] + dot(gs_low, bc[:, :STATE])
    acc_c[...] = dot(gs_low, bc[:, STATE:], (0, 0))

    @pl.loop(0, TILES)
    def _(j):
        cols = tile_of(j)
        wide = widen(weight_ref[...], j)
        grad_update = grad_state[:, cols].astype(BF16)
        spread_grad = dot(bc[:, :STATE], grad_update)
        x, grad = x_act[:, cols].astype(F32), dy[:, cols].astype(F32)
        grad_x[:, cols] += wide * spread_grad + pmain[6:7, cols] * grad
        acc_heads[1] += by_head(x * spread_grad, j)
        acc_c[...] += dot((x * wide).astype(BF16), grad_update, (1, 1))
        kept = jnp.sum(grad_state[:, cols] * state[:, cols], axis=0, keepdims=True)
        skip = jnp.sum(x * grad, axis=0, keepdims=True)
        row = iota((8, TILE), 0)
        both = jnp.where(row == 0, kept, jnp.where(row == 1, skip, 0.0))
        acc_heads[2, 0:8] += by_head(both, j)

    grad_bc[:, :STATE] = acc_c[...]
    grad_weight = acc_heads[1]
    q = jnp.concatenate([q_t[h] for h in range(HEADS)] + [jnp.zeros((LANES - HEADS, BLOCK), F32)], 0).T
    weight_pull = grad_weight * weight
    grad_end = jnp.sum(weight_pull, axis=0, keepdims=True) + acc_heads[2, 0:1] * keep
    grad_cum = rows_acc[...] - step * q + enter * acc_heads[0] - weight_pull
    grad_cum = grad_cum + jnp.where(iota((BLOCK, LANES), 0) == BLOCK - 1, grad_end, 0.0)
    upper = (iota((BLOCK, BLOCK), 0) <= iota((BLOCK, BLOCK), 1)).astype(F32)
    grad_log = dot(upper, grad_cum, precision=lax.Precision.HIGHEST)
    grad_step = q + grad_weight * tail + rate * grad_log
    grad_in = grad_step * sigmoid(steps[0])
    grad_step_in[...] = grad_in
    row = iota((8, LANES), 0)
    heads = jnp.where(row == 5, jnp.sum(grad_in, axis=0, keepdims=True), 0.0)
    heads = jnp.where(row == 6, rate * jnp.sum(grad_log * step, axis=0, keepdims=True), heads)
    vec_heads[...] = jnp.where(row == 7, acc_heads[2, 1:2], heads)

    @pl.loop(0, D // TILE)
    def _(j):
        cols = tile_of(j)
        part = dot(gate_out[...], w_out[cols, :], (1, 1))
        mixed[:, cols] = (hidden[:, cols].astype(F32) + part).astype(BF16)

    for by, ends, outgoing, incoming, send, recv in (
        (1, 7, f_out, f_in, f_send, f_recv),
        (7, 0, b_out, b_in, b_send, b_recv),
    ):

        @pl.when(t != ends)
        def _(by=by, outgoing=outgoing, incoming=incoming, send=send, recv=recv):
            @pl.loop(0, PAIRS)
            def _(c):
                pltpu.make_async_remote_copy(
                    src_ref=outgoing.at[:, pair_of(c)], dst_ref=incoming.at[:, pair_of(c)], send_sem=send.at[c],
                    recv_sem=recv.at[c], device_id=tensor_peer(by), device_id_type=MESH,
                ).wait_send()


def mid(x_act, gate_in, update, bc, steps, scores, doc_col, doc_row, pmain, phead, hidden, cot, full):
    vmem = pl.BlockSpec(memory_space=VMEM)
    shapes = [
        ((BLOCK, D), BF16), ((D, DI), BF16), ((BLOCK, DI), BF16), ((BLOCK, DI), F32), ((BLOCK, 256), F32),
        ((BLOCK, LANES), F32), ((8, DI), F32), ((8, LANES), F32),
    ]
    wide, heads, square = (BLOCK, DI), (BLOCK, LANES), (BLOCK, BLOCK)
    turned = (HEADS, 1, BLOCK)
    scratch = [
        ((D, DI), BF16), ((D, BLOCK), BF16), ((STATE, DI), F32), (wide, F32), (wide, F32), (wide, BF16), (wide, BF16),
        ((STATE, DI), F32), ((STATE, DI), BF16), ((STATE, DI), F32), ((8, DI), F32),
        ((STATE, DI), BF16), ((STATE, DI), BF16), ((STATE, DI), BF16), ((STATE, DI), BF16),
        (square, F32), (heads, F32), (turned, F32), (turned, F32), (heads, F32), (heads, F32),
        (heads, F32), (turned, F32), (square, F32), (heads, F32), ((3,) + heads, F32), (heads, F32),
    ]
    return pl.pallas_call(
        mid_kernel,
        name="scan_and_gate",
        out_shape=[jax.ShapeDtypeStruct(*s) for s in shapes],
        in_specs=[vmem] * 12 + [pl.BlockSpec(memory_space=pl.ANY)],
        out_specs=[vmem] * len(shapes),
        scratch_shapes=[VMEM(*s) for s in scratch]
        + [pltpu.SemaphoreType.DMA((1,))]
        + [pltpu.SemaphoreType.DMA((PAIRS,))] * 4,
        compiler_params=pltpu.CompilerParams(
            collective_id=1, has_side_effects=True, vmem_limit_bytes=60 * 2**20
        ),
    )(x_act, gate_in, update, bc, steps, scores, doc_col, doc_row, pmain, phead, hidden, cot, full)


def tail_kernel(
    normed, x_ext, x_pre, grad_x, after, raw_ext, state_pre, grad_bc, grad_gate_in, grad_step_in, w_small, pmain, phead,
    doc_col, hidden, cot, gain, vec_gate, vec_heads, full,
    grad_main, grad_small, grad_hidden, vec,
    w_x, w_gate, normed_t, acc, small_acc, staged, sems, out_sems,
):
    loads = []
    for m, w in ((0, w_x), (1, w_gate)):
        for j in range(TILES):
            cols = pl.ds(j * TILE, TILE)
            loads.append(pltpu.make_async_copy(full.at[m, :, cols], w.at[:, cols], sems.at[m, j]))
    for c in loads:
        c.start()
    normed_t[...] = normed[...].T
    docs = doc_col[...]
    links = [None] + [conv_links(docs, o, BLOCK + 8) for o in range(1, TAPS)]
    params = small_params(phead[...])
    vec[...] = jnp.zeros_like(vec)

    def conv_back(grad, grad_after, ext, taps):
        grad_ext = jnp.concatenate([grad, grad_after], 0)
        total = taps[TAPS - 1 : TAPS] * grad
        rows = [None] * TAPS
        rows[TAPS - 1] = jnp.sum(grad * ext[HALO:], axis=0, keepdims=True)
        for offset in range(1, TAPS):
            masked = grad_ext * links[offset]
            rows[TAPS - 1 - offset] = jnp.sum(masked[:BLOCK] * ext[HALO - offset : EXT - offset], axis=0, keepdims=True)
            total = total + taps[TAPS - 1 - offset : TAPS - offset] * masked[offset : offset + BLOCK]
        return total, rows + [jnp.sum(grad, axis=0, keepdims=True)]

    grad = grad_bc[...] * silu_slope(state_pre[...])
    total, rows = conv_back(grad, after[:, DI:], raw_ext[:, :256], params[:TAPS, :256])
    for i, row in enumerate(rows):
        vec[i : i + 1, DI : DI + 256] = row
    raw = jnp.concatenate([total.astype(BF16), grad_step_in[...].astype(BF16)], 1)
    acc[...] = dot(raw, w_small[...], (1, 1))
    small_acc[...] = dot(normed_t[...], raw).astype(BF16)
    packed = jnp.zeros((512, 8 * LANES), F32)
    for r in range(3):
        rows_r = jnp.concatenate([small_acc[pl.ds(d * 96 + r * 32, 32)] for d in range(16)], 0)
        packed = packed + dot(rows_r, small_map(r), (1, 1))
    grad_small[...] = packed.astype(BF16)

    def put(m, j, slot):
        return pltpu.make_async_copy(staged.at[slot], grad_main.at[m, :, tile_of(j)], out_sems.at[slot])

    def project(m, j, grad, w):
        slot = lax.rem(j, 2)

        @pl.when(j >= 2)
        def _():
            put(m, j, slot).wait()

        staged[slot] = dot(normed_t[...], grad).astype(BF16)
        put(m, j, slot).start()
        acc[...] += dot(grad, w[:, tile_of(j)], (1, 1))

    @pl.loop(0, TILES)
    def _(j):
        cols = tile_of(j)
        pltpu.make_async_copy(full.at[0, :, cols], w_x.at[:, cols], sems.at[0, j]).wait()
        grad = grad_x[:, cols] * silu_slope(x_pre[:, cols])
        total, rows = conv_back(grad, after[:, cols], x_ext[:, cols], pmain[0:TAPS, cols])
        for i, row in enumerate(rows):
            vec[i : i + 1, cols] = row
        project(0, j, total.astype(BF16), w_x)

    for slot in range(2):
        put(0, TILES - 2 + slot, slot).wait()

    @pl.loop(0, TILES)
    def _(j):
        cols = tile_of(j)
        pltpu.make_async_copy(full.at[1, :, cols], w_gate.at[:, cols], sems.at[1, j]).wait()
        project(1, j, grad_gate_in[:, cols], w_gate)

    for slot in range(2):
        put(1, TILES - 2 + slot, slot).wait()

    value = hidden[...].astype(F32)
    inv = lax.rsqrt(jnp.mean(value * value, axis=1, keepdims=True) + epsilon)
    rows = value * inv
    grad = acc[...]
    vec[5:6, 0:DI] = vec_gate[0:1, :]
    vec[6:7, 0:D] = jnp.sum(grad * rows, axis=0, keepdims=True)
    vec[5:8, DI + 256 :] = vec_heads[5:8, :]
    dn = grad * gain[...]
    mean = jnp.mean(dn * rows, axis=1, keepdims=True)
    grad_hidden[...] = cot[...].astype(F32) + inv * dn - rows * inv * mean


def tail(*args):
    vmem = pl.BlockSpec(memory_space=VMEM)
    anywhere = pl.BlockSpec(memory_space=pl.ANY)
    return pl.pallas_call(
        tail_kernel,
        name="project_back",
        out_shape=[
            jax.ShapeDtypeStruct((2, D, DI), BF16),
            jax.ShapeDtypeStruct((512, 8 * LANES), BF16),
            jax.ShapeDtypeStruct((BLOCK, D), F32),
            jax.ShapeDtypeStruct(VEC, F32),
        ],
        in_specs=[vmem] * 19 + [anywhere],
        out_specs=[anywhere, vmem, vmem, vmem],
        scratch_shapes=[
            VMEM((D, DI), BF16), VMEM((D, DI), BF16), VMEM((D, BLOCK), BF16), VMEM((BLOCK, D), F32),
            VMEM((D, SMALL), BF16), VMEM((2, D, TILE), BF16),
            pltpu.SemaphoreType.DMA((2, TILES)), pltpu.SemaphoreType.DMA((2,)),
        ],
        compiler_params=pltpu.CompilerParams(vmem_limit_bytes=60 * 2**20),
    )(*args)


def per_device(
    hidden,
    doc_ids,
    norm_gain,
    main_proj,
    step_proj,
    state_proj,
    conv_main,
    conv_main_bias,
    conv_state,
    conv_state_bias,
    step_bias,
    decay_log,
    skip_gain,
    gate_gain,
    out_proj,
    cotangent,
):
    t = lax.axis_index("tensor")
    shards = jnp.stack([main_proj[:, 1], main_proj[:, 0], out_proj])
    small = jnp.concatenate([state_proj, step_proj], axis=1).reshape(3, SMALL_ROWS, 38)
    small = jnp.pad(small.transpose(1, 0, 2).reshape(SMALL_ROWS, 114), ((0, 0), (0, 14)))[None]
    params = pack_params(
        conv_main, conv_main_bias, conv_state, conv_state_bias, step_bias, decay_log, skip_gain, gate_gain
    )
    full, packed, halo, pmain, phead = gather_weights(shards, small, hidden[BLOCK - HALO :], params)
    full, packed = full.reshape(3, D, DI), packed.reshape(512, 8 * LANES)
    gain = norm_gain[None]

    docs_all = jnp.concatenate([jnp.full((HALO,), -1, jnp.int32), doc_ids, jnp.full((16,), -2, jnp.int32)])
    docs = lax.dynamic_slice(docs_all, (t * BLOCK,), (EXT + 16,))
    doc_col, doc_row = docs[:, None], docs[None, HALO:EXT]

    normed, x_ext, x_pre, x_act, gate_in, update, raw, state_pre, bc, steps, scores, w_small = front(
        hidden, halo, gain, full, packed, pmain, phead, doc_col
    )
    mixed, grad_out, grad_gate_in, grad_x, grad_bc, grad_step_in, vec_gate, vec_heads = mid(
        x_act, gate_in, update, bc, steps, scores, doc_col, doc_row, pmain, phead, hidden, cotangent, full
    )
    first = jnp.concatenate(
        [grad_x[:8] * silu_slope(x_pre[:8]), grad_bc[:8] * silu_slope(state_pre[:8])], axis=1
    )
    after = lax.ppermute(first, "tensor", [(i, i - 1) for i in range(1, 8)])
    grad_main, grad_small, grad_hidden, vec = tail(
        normed, x_ext, x_pre, grad_x, after, raw, state_pre, grad_bc, grad_gate_in, grad_step_in, w_small, pmain,
        phead, doc_col, hidden, cotangent, gain, vec_gate, vec_heads, full,
    )
    own_main, own_small, vec = scatter_grads(
        grad_main.reshape(2, 2, 4, 2, ROWS, DI), grad_out.reshape(1, 2, 4, 2, ROWS, DI),
        grad_small.reshape(1, 2, 4, 2, SMALL_ROWS, 8 * LANES), vec,
    )
    own_small = own_small[0, :, :114].reshape(SMALL_ROWS, 3, 38).transpose(1, 0, 2).reshape(ROWS, 38)
    vec_main = lax.dynamic_slice(vec, (0, t * WIDTH), (8, WIDTH))
    vec_state = lax.dynamic_slice(vec, (0, DI + t * 32), (5, 32))
    vec_head = lax.dynamic_slice(vec, (5, DI + 256 + t * 6), (3, 6))
    return (
        mixed,
        grad_hidden,
        vec[6, :D],
        jnp.stack([own_main[1], own_main[0]], axis=1),
        own_small[:, 32:],
        own_small[:, :32],
        vec_main[:TAPS],
        vec_main[TAPS],
        vec_state[:TAPS],
        vec_state[TAPS],
        vec_head[0],
        vec_head[1],
        vec_head[2],
        vec_main[5],
        own_main[2],
    )


def solution(mesh):
    placed = (
        P(("dp", "tensor"), None),
        P("dp"),
        P(),
        P("dp", None, "tensor"),
        P("dp", "tensor"),
        P("dp", "tensor"),
        P(None, "tensor"),
        P("tensor"),
        P(None, "tensor"),
        P("tensor"),
        P("tensor"),
        P("tensor"),
        P("tensor"),
        P("tensor"),
        P("dp", "tensor"),
        P(("dp", "tensor"), None),
    )
    return jax.shard_map(
        per_device,
        mesh=mesh,
        in_specs=placed,
        out_specs=(
            P(("dp", "tensor"), None),
            P(("dp", "tensor"), None),
            P(),
            P("dp", None, "tensor"),
            P("dp", "tensor"),
            P("dp", "tensor"),
            P(None, "tensor"),
            P("tensor"),
            P(None, "tensor"),
            P("tensor"),
            P("tensor"),
            P("tensor"),
            P("tensor"),
            P("tensor"),
            P("dp", "tensor"),
        ),
        check_vma=False,
    )
```

```python
import functools

import jax
import jax.numpy as jnp
from jax import lax
from jax.experimental import pallas as pl
from jax.experimental.pallas import tpu as pltpu
from jax.sharding import PartitionSpec as P

BLOCK = 256
epsilon = 1e-05

MESH = pl.DeviceIdType.MESH
AXES = (0, 1, 2)
SIDE = 4


def coordinates():
    dp = lax.axis_index("dp")
    t = lax.axis_index("tensor")
    z = lax.div(t, 4) * 2 + lax.div(dp, 8)
    return (lax.rem(t, 4), lax.rem(lax.div(dp, 2), 4), z), lax.rem(dp, 2)


def device(at, core):
    x, y, z = at
    return (lax.rem(z, 2) * 8 + y * 2 + core, lax.div(z, 2) * 4 + x)


def moved(at, axis, by):
    return tuple(lax.rem(v + by + SIDE, SIDE) if i == axis else v for i, v in enumerate(at))


def pieces(at, whole, width):
    x, y, z = at
    lo = pl.ds(0, 2) if 2 in whole else pl.ds(lax.rem(z, 2), 1)
    row = pl.ds(0, 4) if 1 in whole else pl.ds(y, 1)
    hi = lax.div(z, 2)
    if 0 in whole and 2 in whole:
        cols = [pl.ds(0, 8 * width)]
    elif 0 in whole:
        cols = [pl.ds(pl.multiple_of(hi * 4 * width, 128), 4 * width)]
    elif 2 in whole:
        cols = [
            pl.ds(pl.multiple_of(x * width, 128), width),
            pl.ds(pl.multiple_of((4 + x) * width, 128), width),
        ]
    else:
        cols = [pl.ds(pl.multiple_of((hi * 4 + x) * width, 128), width)]
    return [(lo, row, c) for c in cols]


def greet(at, core, group):
    barrier = pltpu.get_barrier_semaphore()
    others = [device(moved(at, axis, by), core) for axis in AXES for by in (1, -1)]
    others.append(device(at, 1 - core))
    others += group
    for other in others:
        pl.semaphore_signal(barrier, inc=1, device_id=other, device_id_type=MESH)
    pl.semaphore_wait(barrier, len(others))


def tensor_peer(by):
    return (lax.axis_index("dp"), lax.rem(lax.axis_index("tensor") + by, 8))


ROWS, WIDTH, SMALL_ROWS, SMALL_WIDTH = 96, 384, 32, 128
UNITS = [(0, q * 32, q) for q in range(3)] + [(1, 0, 0)]
WIDTHS = [WIDTH, SMALL_WIDTH]
STACK = [3, 1]


def axes_of(u):
    return [(UNITS[u][2] + j) % 3 for j in range(3)]


def region(ref, u, core, mats, where, whole, half=None):
    which, first, rows = UNITS[u][0], UNITS[u][1], 32
    if half is not None:
        first, rows = first + half * 16, 16
    return [
        ref.at[mats, lo, row, core, pl.ds(first, rows), cols]
        for lo, row, cols in pieces(where, whole, WIDTHS[which])
    ]


def sized(ref, u, mats, blocks, halves=2):
    width = WIDTHS[UNITS[u][0]]
    cols = min(blocks, 8)
    rest = blocks // cols
    return ref.at[mats, pl.ds(0, max(rest // 4, 1)), pl.ds(0, min(rest, 4)), 0, pl.ds(0, 16 * halves), pl.ds(0, cols * width)]


def gather_kernel(*refs):
    shards, small, tail, params = refs[0], refs[1], refs[2], refs[3:5]
    full, halo, params_all = refs[5:7], refs[7], refs[8:10]
    own_sem, halo_sem, param_send, param_recv, send, recv, core_send, core_recv = refs[10:]
    at, core = coordinates()
    t = lax.axis_index("tensor")
    own = []
    for w, source in enumerate((shards, small)):
        for lo, row, cols in pieces(at, (), WIDTHS[w]):
            own.append(
                pltpu.make_async_copy(source, full[w].at[:, lo.start, row.start, core, :, cols], own_sem.at[w])
            )
    def columns(i, of):
        width = params[i].shape[-1]
        return params_all[i].at[:, pl.ds(pl.multiple_of(of * width, 128), width)]

    for i in range(2):
        own.append(pltpu.make_async_copy(params[i], columns(i, t), own_sem.at[2 + i]))
    for c in own:
        c.start()
    greet(at, core, [tensor_peer(by) for by in range(1, 8)])
    last = []

    def go(copy, wait=True):
        copy.start()
        if wait:
            last.append(copy)

    def tail_copy():
        return pltpu.make_async_remote_copy(
            src_ref=tail, dst_ref=halo, send_sem=halo_sem.at[0], recv_sem=halo_sem.at[1],
            device_id=tensor_peer(1), device_id_type=MESH,
        )

    def param_copy(by, i, of):
        return pltpu.make_async_remote_copy(
            src_ref=params[i], dst_ref=columns(i, of), send_sem=param_send.at[i, by - 1],
            recv_sem=param_recv.at[i, by - 1], device_id=tensor_peer(by), device_id_type=MESH,
        )

    go(tail_copy())
    for by in range(1, 8):
        for i in range(2):
            go(param_copy(by, i, t))
    for c in own:
        c.wait()

    def slot(u, phase, m):
        return (phase if phase < 2 else 2 + m), [u]

    def mats_of(u, phase, m):
        return pl.ds(0, STACK[UNITS[u][0]]) if phase < 2 else pl.ds(m, 1)

    def sends(u, phase, m, step):
        axes = axes_of(u)
        whole, axis = axes[:phase], axes[phase]
        index = phase if phase < 2 else 2 + m
        ref = full[UNITS[u][0]]
        for kind, by in ((0, 1), (1, -1)):
            where = at if step == 0 else moved(at, axis, -by)
            for part in region(ref, u, core, mats_of(u, phase, m), where, whole, kind if step else None):
                pltpu.make_async_remote_copy(
                    src_ref=part, dst_ref=part, send_sem=send.at[u, index, step],
                    recv_sem=recv.at[u, index, step],
                    device_id=device(moved(at, axis, by), core), device_id_type=MESH,
                ).start()

    def await_step(u, phase, m, step, sem):
        index = phase if phase < 2 else 2 + m
        part = sized(full[UNITS[u][0]], u, mats_of(u, phase, m), 2 * 4**phase // (1 + step))
        pltpu.make_async_copy(part, part, sem.at[u, index, step]).wait()

    def to_partner(u, m, where, whole):
        for part in region(full[UNITS[u][0]], u, core, mats_of(u, 2, m), where, whole):
            pltpu.make_async_remote_copy(
                src_ref=part, dst_ref=part, send_sem=core_send.at[u, m],
                recv_sem=core_recv.at[u, m], device_id=device(at, 1 - core), device_id_type=MESH,
            ).start()

    everything = range(len(UNITS))
    late = [(u, m) for m in range(3) for u in everything if m < STACK[UNITS[u][0]]]
    for phase in (0, 1):
        for u in everything:
            sends(u, phase, 0, 0)
        for u in everything:
            await_step(u, phase, 0, 0, recv)
            sends(u, phase, 0, 1)
        for u in everything:
            await_step(u, phase, 0, 1, recv)
    for u, m in late:
        sends(u, 2, m, 0)
    for u, m in late:
        to_partner(u, m, at, axes_of(u)[:2])
    for u, m in late:
        await_step(u, 2, m, 0, recv)
        sends(u, 2, m, 1)
        whole, axis = axes_of(u)[:2], axes_of(u)[2]
        for by in (-1, 1):
            to_partner(u, m, moved(at, axis, by), whole)
    for u, m in late:
        await_step(u, 2, m, 1, recv)
        whole, axis = axes_of(u)[:2], axes_of(u)[2]
        to_partner(u, m, moved(at, axis, 2), whole)
    for u, m in late:
        part = sized(full[UNITS[u][0]], u, mats_of(u, 2, m), 64)
        pltpu.make_async_copy(part, part, core_recv.at[u, m]).wait()
        pltpu.make_async_copy(part, part, core_send.at[u, m]).wait()
    tail_copy().wait_recv()
    for by in range(1, 8):
        for i in range(2):
            param_copy(by, i, lax.rem(t + 8 - by, 8)).wait_recv()
    for u in everything:
        for phase in (0, 1):
            for step in (0, 1):
                await_step(u, phase, 0, step, send)
    for u, m in late:
        for step in (0, 1):
            await_step(u, 2, m, step, send)
    for c in last:
        c.wait_send()


def gather_weights(shards, small, tail, params):
    units = len(UNITS)
    return pl.pallas_call(
        gather_kernel,
        name="gather_weights",
        out_shape=[
            jax.ShapeDtypeStruct((3, 2, 4, 2, ROWS, 8 * WIDTH), jnp.bfloat16),
            jax.ShapeDtypeStruct((1, 2, 4, 2, SMALL_ROWS, 8 * SMALL_WIDTH), jnp.bfloat16),
            jax.ShapeDtypeStruct(tail.shape, tail.dtype),
        ]
        + [jax.ShapeDtypeStruct((8, 8 * p.shape[1]), p.dtype) for p in params],
        in_specs=[pl.BlockSpec(memory_space=pl.ANY)] * 5,
        out_specs=[pl.BlockSpec(memory_space=pl.ANY)] * 5,
        scratch_shapes=[
            pltpu.SemaphoreType.DMA((4,)),
            pltpu.SemaphoreType.DMA((2,)),
            pltpu.SemaphoreType.DMA((2, 7)),
            pltpu.SemaphoreType.DMA((2, 7)),
            pltpu.SemaphoreType.DMA((units, 5, 2)),
            pltpu.SemaphoreType.DMA((units, 5, 2)),
            pltpu.SemaphoreType.DMA((units, 3)),
            pltpu.SemaphoreType.DMA((units, 3)),
        ],
        compiler_params=pltpu.CompilerParams(collective_id=0, has_side_effects=True),
    )(shards, small, tail, *params)


D, DI, HEADS, HEAD_DIM, STATE, TAPS, HALO = 1536, 3072, 48, 64, 128, 4, 16
BF16, F32 = jnp.bfloat16, jnp.float32
TILE, LANES, SMALL = 512, 128, 384
TILES = DI // TILE
LOG2E = 1.4426950408889634
EXT = HALO + BLOCK
VMEM = pltpu.VMEM


def dot(a, b, dims=(1, 0), precision=None):
    return lax.dot_general(
        a, b, ((dims[:1], dims[1:]), ((), ())), precision=precision, preferred_element_type=F32
    )


def iota(shape, dim):
    return lax.broadcasted_iota(jnp.int32, shape, dim)


def sigmoid(v):
    return 1.0 / (1.0 + jnp.exp(-v))


def silu(v):
    return v * sigmoid(v)


def silu_slope(v):
    s = sigmoid(v)
    return s * (1.0 + v * (1.0 - s))


def softplus(v):
    return jnp.maximum(v, 0.0) + jnp.log1p(jnp.exp(-jnp.abs(v)))


def split(v):
    high = v.astype(BF16)
    return high, (v - high.astype(F32)).astype(BF16)


def head_map(j):
    return (iota((LANES, TILE), 0) == j * (TILE // HEAD_DIM) + iota((LANES, TILE), 1) // HEAD_DIM).astype(BF16)


def widen(v, j):
    high, low = split(v)
    return dot(high, head_map(j)) + dot(low, head_map(j))


def by_head(v, j):
    high, low = split(v)
    return dot(high, head_map(j), (1, 1)) + dot(low, head_map(j), (1, 1))


def small_map(r):
    row, col = iota((8 * LANES, SMALL), 0), iota((8 * LANES, SMALL), 1)
    t, lane = row // LANES, row % LANES - 38 * r
    state = (lane >= 0) & (lane < 32) & (col == t * 32 + lane)
    step = (lane >= 32) & (lane < 38) & (col == 256 + t * 6 + lane - 32)
    return (state | step).astype(BF16)


def tile_of(j):
    return pl.ds(pl.multiple_of(j * TILE, TILE), TILE)


def conv_links(doc_col, offset, rows):
    return (doc_col[HALO : HALO + rows] == doc_col[HALO - offset : HALO - offset + rows]).astype(F32)


def conv(ext, taps, bias, links):
    total = bias + taps[TAPS - 1 : TAPS] * ext[HALO:]
    for offset in range(1, TAPS):
        total = total + taps[TAPS - 1 - offset : TAPS - offset] * ext[HALO - offset : EXT - offset] * links[offset]
    return total


def small_params(phead):
    return dot(phead, small_map(0).astype(F32), precision=lax.Precision.HIGHEST)


def decay_terms(step, cum, doc_col, doc_prev):
    block = doc_col[HALO:EXT]
    end = cum[BLOCK - 1 : BLOCK]
    tail = jnp.exp(end - cum) * (block == block[BLOCK - 1 : BLOCK]).astype(F32)
    enter = jnp.exp(cum) * (block == doc_prev).astype(F32)
    keep = jnp.exp(end) * (block[BLOCK - 1 : BLOCK] == doc_prev).astype(F32)
    return enter, tail, tail * step, keep


def pack_params(conv_main, conv_main_bias, conv_state, conv_state_bias, step_bias, decay_log, skip_gain, gate_gain):
    main = jnp.concatenate(
        [conv_main, conv_main_bias[None], gate_gain[None], jnp.repeat(skip_gain, HEAD_DIM)[None],
         jnp.zeros((1, WIDTH), F32)]
    )
    state = jnp.pad(jnp.concatenate([conv_state, conv_state_bias[None]]), ((0, 3), (0, 96)))
    heads = jnp.pad(jnp.stack([step_bias, decay_log, skip_gain]), ((5, 0), (32, 90)))
    return main, state + heads


PAIR = 2 * HEAD_DIM
PAIRS = DI // PAIR
HALF = BLOCK // 2
CHUNK = 256
CHUNKS = DI // CHUNK
FORWARD_LAG, BACKWARD_LAG = 4, 2


def pair_of(p):
    return pl.ds(pl.multiple_of(p * PAIR, PAIR), PAIR)


def chunk_of(c):
    return pl.ds(pl.multiple_of(c * CHUNK, CHUNK), CHUNK)


def only(value, first):
    lane = iota(value.shape, 1)
    return jnp.where((lane < HEAD_DIM) == first, value, jnp.zeros_like(value))


def head_column(ref, h):
    return pltpu.roll(ref[...], lax.rem(LANES - h, LANES), axis=1)[:, :1]


def mid_kernel(
    hidden, halo, gain, packed, pmain, phead, doc_col, doc_row, cot, full,
    mixed, normed_t, raw, state_pre, grad_bc, grad_step_in, w_small, acc, grad_x, vec_gate, vec_heads,
    x_ext, x_pre, grad_out, grad_gate,
    normed, w_in, ext_out, pre_out, staged, x_act, bc, scores, gate_in, work, y, gate_out, dy, gate_grad, update,
    grad_add, state, state_low, grad_state, keep_row, f_out, f_in, b_out, b_in, cot_t, mixed_acc,
    barred, cum2, cum_t, step_t, step_in, enter_ref, weight_ref, rows_acc, q_t, gs, acc_c, acc_heads, row_acc,
    w_sem, put_sem, x_sem, f_send, f_recv, b_send, b_recv,
):
    t = lax.axis_index("tensor")

    def load(m, j, slot):
        return pltpu.make_async_copy(full.at[m, :, tile_of(j)], w_in.at[slot], w_sem.at[slot])

    load(0, 0, 0).start()
    barrier = pltpu.get_barrier_semaphore()
    for other in (tensor_peer(1), tensor_peer(7)):
        pl.semaphore_signal(barrier, inc=1, device_id=other, device_id_type=MESH)
    pl.semaphore_wait(barrier, 2)

    for rows, part in ((pl.ds(0, HALO), halo), (pl.ds(HALO, BLOCK), hidden)):
        value = part[...].astype(F32)
        inv = lax.rsqrt(jnp.mean(value * value, axis=1, keepdims=True) + epsilon)
        normed[rows] = (value * inv * gain[...]).astype(BF16)
    normed_t[...] = normed[pl.ds(HALO, BLOCK)].T
    cot_t[...] = cot[...].T
    for r in range(3):
        rows = dot(packed[...], small_map(r)).astype(BF16)
        for d in range(16):
            w_small[pl.ds(d * 96 + r * 32, 32)] = rows[d * 32 : d * 32 + 32]
    raw[...] = dot(normed[...], w_small[...])
    params = small_params(phead[...])
    docs = doc_col[...]
    links = [None] + [conv_links(docs, o, BLOCK) for o in range(1, TAPS)]
    pre = conv(raw[:, :256], params[:TAPS, :256], params[TAPS : TAPS + 1, :256], links)
    state_pre[...] = pre
    act = silu(pre).astype(BF16)
    bc[...] = act
    scores[...] = dot(act[:, STATE:], act[:, :STATE], (1, 1))
    step_in[...] = raw[HALO:, 256:] + params[5:6, 256:]
    rate = -jnp.exp(params[6:7, 256:])
    step = softplus(step_in[...])
    lower = (iota((BLOCK, BLOCK), 0) >= iota((BLOCK, BLOCK), 1)).astype(F32)
    cum = dot(lower, step * rate, precision=lax.Precision.HIGHEST)
    enter, tail, weight, keep = decay_terms(step, cum, docs, docs[HALO - 1 : HALO])
    enter_ref[...] = enter
    weight_ref[...] = weight
    cum2[...] = cum * LOG2E
    for ref, turned in ((cum_t, (cum * LOG2E).T), (step_t, step.T)):
        for h in range(HEADS):
            ref[h] = turned[h : h + 1]
    linked = (docs[HALO:EXT] == doc_row[...]) & (iota((BLOCK, BLOCK), 0) >= iota((BLOCK, BLOCK), 1))
    barred[...] = jnp.where(linked, 0.0, -1e30)
    keep8 = jnp.broadcast_to(keep, (8, LANES))

    def chain(forward, c, add, into, outgoing, incoming, send, recv):
        cols = chunk_of(c)
        by = 1 if forward else 7
        is_first = t == (0 if forward else 7)
        is_last = t == (7 if forward else 0)

        def copy():
            return pltpu.make_async_remote_copy(
                src_ref=outgoing.at[:, cols], dst_ref=incoming.at[:, cols], send_sem=send.at[c],
                recv_sem=recv.at[c], device_id=tensor_peer(by), device_id_type=MESH,
            )

        @pl.when(is_first)
        def _():
            into[:, cols] = jnp.zeros((STATE, CHUNK), F32)

        @pl.when(jnp.logical_not(is_first))
        def _():
            copy().wait_recv()
            into[:, cols] = incoming[:, cols].astype(F32)

        @pl.when(jnp.logical_not(is_last))
        def _():
            outgoing[:, cols] = (keep_row[0:1, cols] * into[:, cols] + add[:, cols]).astype(BF16)
            copy().start()

    def forward_slot(s):
        c = s - FORWARD_LAG * t

        @pl.when((c >= 0) & (c < CHUNKS))
        def _():
            chain(True, c, update, state, f_out, f_in, f_send, f_recv)

    def backward_slot(s):
        c = s - BACKWARD_LAG * (7 - t)

        @pl.when((c >= 0) & (c < CHUNKS))
        def _():
            chain(False, c, grad_add, grad_state, b_out, b_in, b_send, b_recv)

    def x_puts(j, slot):
        return [
            pltpu.make_async_copy(src.at[slot], dst.at[:, tile_of(j)], x_sem.at[i, slot])
            for i, (src, dst) in enumerate(((ext_out, x_ext), (pre_out, x_pre)))
        ]

    @pl.loop(0, TILES)
    def _(j):
        cols = tile_of(j)
        slot = lax.rem(j, 2)

        @pl.when(j + 1 < TILES)
        def _():
            load(0, j + 1, 1 - slot).start()

        @pl.when(j + 1 == TILES)
        def _():
            load(1, 0, 0).start()

        @pl.when(j >= 2)
        def _():
            for c in x_puts(j, slot):
                c.wait()

        load(0, j, slot).wait()
        ext = dot(normed[...], w_in[slot])
        ext_out[slot] = ext
        pre = conv(ext, pmain[0:TAPS, cols], pmain[TAPS : TAPS + 1, cols], links)
        pre_out[slot] = pre
        for c in x_puts(j, slot):
            c.start()
        act = silu(pre).astype(BF16)
        x_act[:, cols] = act
        heavy = (act.astype(F32) * widen(weight_ref[...], j)).astype(BF16)
        update[:, cols] = dot(bc[:, :STATE], heavy, (0, 0))
        keep_row[:, cols] = widen(keep8, j)
        forward_slot(2 * j)
        forward_slot(2 * j + 1)

    load(2, 0, 1).start()
    for slot in range(2):
        for c in x_puts(TILES - 2 + slot, slot):
            c.wait()

    halves = [(slice(0, HALF), slice(0, HALF)), (slice(HALF, BLOCK), slice(0, BLOCK))]

    def decay_of(h, column, rows, cols):
        return jnp.exp2(column[rows] - cum_t[h, :, cols] + barred[rows, cols])

    def intra_forward(p):
        cols = pair_of(p)
        x = x_act[:, cols]
        x2 = [only(x, True), only(x, False)]
        columns = [head_column(cum2, 2 * p + k) for k in (0, 1)]
        for rows, js in halves:
            mix = [
                (scores[rows, js] * (decay_of(2 * p + k, columns[k], rows, js) * step_t[2 * p + k, :, js])).astype(BF16)
                for k in (0, 1)
            ]
            y[rows, cols] = dot(jnp.concatenate(mix, 1), jnp.concatenate([v[js] for v in x2], 0))

    @pl.loop(0, PAIRS)
    def _(i):
        intra_forward(i)
        j = lax.div(i, 4)

        @pl.when(lax.rem(i, 4) == 0)
        def _():
            load(1, j, 0).wait()
            gate_in[:, tile_of(j)] = dot(normed[pl.ds(HALO, BLOCK)], w_in[0])

            @pl.when(j + 1 < TILES)
            def _():
                load(1, j + 1, 0).start()

        @pl.when(lax.rem(i, 4) == 2)
        def _():
            load(2, j, 1).wait()
            work[:, tile_of(j)] = dot(cot[...], w_in[1])

            @pl.when(j + 1 < TILES)
            def _():
                load(2, j + 1, 1).start()

        forward_slot(2 * TILES + i)

    @pl.loop(2 * TILES + PAIRS, jnp.maximum(2 * TILES + PAIRS, FORWARD_LAG * t + CHUNKS))
    def _(s):
        forward_slot(s)

    load(2, 0, 1).start()
    load(1, 0, 0).start()
    row_acc[...] = jnp.zeros_like(row_acc)

    @pl.loop(0, TILES)
    def _(j):
        cols = tile_of(j)
        low = state[:, cols].astype(BF16)
        state_low[:, cols] = low
        carried = dot(bc[:, STATE:], low)
        value = y[:, cols] + carried * widen(enter_ref[...], j) + pmain[6:7, cols] * x_act[:, cols].astype(F32)
        y[:, cols] = value
        gated = value * silu(gate_in[:, cols])
        row_acc[...] += jnp.broadcast_to(jnp.sum(gated * gated, axis=1, keepdims=True), (BLOCK, LANES))

    gate_inv = lax.rsqrt(row_acc[:, :1] / DI + epsilon)
    row_acc[...] = jnp.zeros_like(row_acc)

    @pl.loop(0, TILES)
    def _(j):
        cols = tile_of(j)
        gated = y[:, cols] * silu(gate_in[:, cols])
        hat = gated * gate_inv
        gate_gain = pmain[5:6, cols]
        gate_out[:, cols] = (hat * gate_gain).astype(BF16)
        grad = work[:, cols]
        vec_gate[:, cols] = jnp.broadcast_to(jnp.sum(grad * hat, axis=0, keepdims=True), (8, TILE))
        dn = grad * gate_gain
        work[:, cols] = dn
        row_acc[...] += jnp.broadcast_to(jnp.sum(dn * gated, axis=1, keepdims=True), (BLOCK, LANES))

    inner = row_acc[:, :1] / DI * gate_inv * gate_inv * gate_inv
    acc_c[...] = jnp.zeros_like(acc_c)
    acc_heads[...] = jnp.zeros_like(acc_heads)

    @pl.loop(0, TILES)
    def _(j):
        cols = tile_of(j)
        gate, value = gate_in[:, cols], y[:, cols]
        s = sigmoid(gate)
        act = gate * s
        grad_gated = gate_inv * work[:, cols] - value * act * inner
        grad = (grad_gated * act).astype(BF16)
        dy[:, cols] = grad
        gate_grad[:, cols] = (grad_gated * value * (s * (1.0 + gate * (1.0 - s)))).astype(BF16)
        grad = grad.astype(F32)
        carried_grad = (grad * widen(enter_ref[...], j)).astype(BF16)
        low = state_low[:, cols]
        grad_add[:, cols] = dot(bc[:, STATE:], carried_grad, (0, 0))
        acc_c[...] += dot(carried_grad, low, (1, 1))
        acc_heads[0] += by_head(grad * dot(bc[:, STATE:], low), j)

    rows_acc[...] = jnp.zeros_like(rows_acc)
    gs[...] = jnp.zeros_like(gs)
    acc[...] = jnp.zeros_like(acc)
    mixed_acc[...] = jnp.zeros_like(mixed_acc)

    def intra_backward(p):
        cols = pair_of(p)
        x, grad = x_act[:, cols], dy[:, cols]
        grad2 = [only(grad, True), only(grad, False)]
        columns = [head_column(cum2, 2 * p + k) for k in (0, 1)]
        lane = iota((HALF, LANES), 1)
        parts = []
        q_rows = [[], []]
        for rows, js in halves:
            mixes = []
            gs_sum = gs[rows, js]
            pulls = jnp.zeros((HALF, LANES), F32)
            for k in (0, 1):
                h = 2 * p + k
                decay = decay_of(h, columns[k], rows, js)
                decay_step = decay * step_t[h, :, js]
                mixes.append((scores[rows, js] * decay_step).astype(BF16))
                grad_mix = dot(grad2[k][rows], x[js], (1, 1))
                gs_sum = gs_sum + grad_mix * decay_step
                q = grad_mix * scores[rows, js] * decay
                q_rows[k].append(jnp.sum(q, axis=0, keepdims=True))
                pull = jnp.sum(q * step_t[h, :, js], axis=1, keepdims=True)
                pulls = jnp.where(lane == h, pull, pulls)
            gs[rows, js] = gs_sum
            rows_acc[rows] += pulls
            parts.append(dot(jnp.concatenate(mixes, 0), jnp.concatenate([v[rows] for v in grad2], 0), (0, 0)))
        grad_x[pl.ds(0, HALF), cols] = parts[0] + parts[1][:HALF]
        grad_x[pl.ds(HALF, HALF), cols] = parts[1][HALF:]
        for k in (0, 1):
            first, second = q_rows[k]
            q_t[2 * p + k, :, 0:HALF] = first + second[:, :HALF]
            q_t[2 * p + k, :, HALF:BLOCK] = second[:, HALF:]

    def put(ref, j, slot):
        return [
            pltpu.make_async_copy(
                staged.at[slot, pl.ds(i * ROWS, ROWS)], ref.at[0, lo, y_, c, :, tile_of(j)], put_sem.at[slot, i]
            )
            for i, (lo, y_, c) in enumerate((lo, y_, c) for lo in range(2) for y_ in range(4) for c in range(2))
        ]

    def put_tile(ref, j, slot, lhs, grad):
        @pl.when(j >= 1)
        def _():
            for c in put(ref, j, slot):
                c.wait()

        staged[slot] = dot(lhs[...], grad).astype(BF16)
        for c in put(ref, j, slot):
            c.start()

    @pl.loop(0, PAIRS)
    def _(i):
        backward_slot(i)
        intra_backward(i)
        j = lax.div(i, 4)
        cols = tile_of(j)

        @pl.when(lax.rem(i, 4) == 0)
        def _():
            put_tile(grad_out, j, 0, cot_t, gate_out[:, cols])

        @pl.when(lax.rem(i, 4) == 1)
        def _():
            put_tile(grad_gate, j, 1, normed_t, gate_grad[:, cols])

        @pl.when(lax.rem(i, 4) == 2)
        def _():
            load(2, j, 1).wait()
            mixed_acc[...] += dot(gate_out[:, cols], w_in[1], (1, 1))

            @pl.when(j + 1 < TILES)
            def _():
                load(2, j + 1, 1).start()

        @pl.when(lax.rem(i, 4) == 3)
        def _():
            load(1, j, 0).wait()
            acc[...] += dot(gate_grad[:, cols], w_in[0], (1, 1))

            @pl.when(j + 1 < TILES)
            def _():
                load(1, j + 1, 0).start()

    @pl.loop(PAIRS, jnp.maximum(PAIRS, BACKWARD_LAG * (7 - t) + CHUNKS))
    def _(s):
        backward_slot(s)

    gs_low = gs[...].astype(BF16)
    grad_bc[:, STATE:] = acc_c[...] + dot(gs_low, bc[:, :STATE])
    acc_c[...] = dot(gs_low, bc[:, STATE:], (0, 0))

    @pl.loop(0, TILES)
    def _(j):
        cols = tile_of(j)
        wide = widen(weight_ref[...], j)
        grad_update = grad_state[:, cols].astype(BF16)
        spread_grad = dot(bc[:, :STATE], grad_update)
        x, grad = x_act[:, cols].astype(F32), dy[:, cols].astype(F32)
        grad_x[:, cols] += wide * spread_grad + pmain[6:7, cols] * grad
        acc_heads[1] += by_head(x * spread_grad, j)
        acc_c[...] += dot((x * wide).astype(BF16), grad_update, (1, 1))
        kept = jnp.sum(grad_state[:, cols] * state[:, cols], axis=0, keepdims=True)
        skip = jnp.sum(x * grad, axis=0, keepdims=True)
        row = iota((8, TILE), 0)
        both = jnp.where(row == 0, kept, jnp.where(row == 1, skip, 0.0))
        acc_heads[2, 0:8] += by_head(both, j)

    grad_bc[:, :STATE] = acc_c[...]
    grad_weight = acc_heads[1]
    none = jnp.zeros((LANES - HEADS, BLOCK), F32)
    step = jnp.concatenate([step_t[h] for h in range(HEADS)] + [none], 0).T
    q = jnp.concatenate([q_t[h] for h in range(HEADS)] + [none], 0).T
    weight_pull = grad_weight * weight_ref[...]
    grad_end = jnp.sum(weight_pull, axis=0, keepdims=True) + acc_heads[2, 0:1] * keep
    grad_cum = rows_acc[...] - step * q + enter_ref[...] * acc_heads[0] - weight_pull
    grad_cum = grad_cum + jnp.where(iota((BLOCK, LANES), 0) == BLOCK - 1, grad_end, 0.0)
    upper = (iota((BLOCK, BLOCK), 0) <= iota((BLOCK, BLOCK), 1)).astype(F32)
    grad_log = dot(upper, grad_cum, precision=lax.Precision.HIGHEST)
    grad_step = q + grad_weight * tail + rate * grad_log
    grad_in = grad_step * sigmoid(step_in[...])
    grad_step_in[...] = grad_in
    row = iota((8, LANES), 0)
    heads = jnp.where(row == 5, jnp.sum(grad_in, axis=0, keepdims=True), 0.0)
    heads = jnp.where(row == 6, rate * jnp.sum(grad_log * step, axis=0, keepdims=True), heads)
    vec_heads[...] = jnp.where(row == 7, acc_heads[2, 1:2], heads)
    mixed[...] = (hidden[...].astype(F32) + mixed_acc[...]).astype(BF16)

    for slot, ref in ((0, grad_out), (1, grad_gate)):
        for c in put(ref, TILES - 1, slot):
            c.wait()
    for by, ends, outgoing, incoming, send, recv in (
        (1, 7, f_out, f_in, f_send, f_recv),
        (7, 0, b_out, b_in, b_send, b_recv),
    ):

        @pl.when(t != ends)
        def _(by=by, outgoing=outgoing, incoming=incoming, send=send, recv=recv):
            @pl.loop(0, CHUNKS)
            def _(c):
                pltpu.make_async_remote_copy(
                    src_ref=outgoing.at[:, chunk_of(c)], dst_ref=incoming.at[:, chunk_of(c)], send_sem=send.at[c],
                    recv_sem=recv.at[c], device_id=tensor_peer(by), device_id_type=MESH,
                ).wait_send()


def mid(*args):
    vmem = pl.BlockSpec(memory_space=VMEM)
    anywhere = pl.BlockSpec(memory_space=pl.ANY)
    wide, heads, square = (BLOCK, DI), (BLOCK, LANES), (BLOCK, BLOCK)
    turned, own_state = (HEADS, 1, BLOCK), (STATE, DI)
    blocks = (1, 2, 4, 2, ROWS, DI)
    shapes = [
        ((BLOCK, D), BF16), ((D, BLOCK), BF16), ((EXT, SMALL), F32), (square, F32), (square, F32), (heads, F32),
        ((D, SMALL), BF16), ((BLOCK, D), F32), (wide, F32), ((8, DI), F32), ((8, LANES), F32),
        ((EXT, DI), F32), (wide, F32), (blocks, BF16), (blocks, BF16),
    ]
    scratch = [
        ((EXT, D), BF16), ((2, D, TILE), BF16), ((2, EXT, TILE), F32), ((2, BLOCK, TILE), F32), ((2, D, TILE), BF16),
        (wide, BF16), ((BLOCK, 2 * STATE), BF16), (square, F32), (wide, F32), (wide, F32), (wide, F32), (wide, BF16),
        (wide, BF16), (wide, BF16), (own_state, F32), (own_state, F32), (own_state, F32), (own_state, BF16),
        (own_state, F32), ((8, DI), F32), (own_state, BF16), (own_state, BF16), (own_state, BF16), (own_state, BF16),
        ((D, BLOCK), BF16), ((BLOCK, D), F32),
        (square, F32), (heads, F32), (turned, F32), (turned, F32), (heads, F32), (heads, F32), (heads, F32),
        (heads, F32), (turned, F32), (square, F32), (heads, F32), ((3,) + heads, F32), (heads, F32),
    ]
    return pl.pallas_call(
        mid_kernel,
        name="scan_and_gate",
        out_shape=[jax.ShapeDtypeStruct(*s) for s in shapes],
        in_specs=[vmem] * 9 + [anywhere],
        out_specs=[vmem] * 11 + [anywhere] * 4,
        scratch_shapes=[VMEM(*s) for s in scratch]
        + [pltpu.SemaphoreType.DMA((2,)), pltpu.SemaphoreType.DMA((2, 16)), pltpu.SemaphoreType.DMA((2, 2))]
        + [pltpu.SemaphoreType.DMA((CHUNKS,))] * 4,
        compiler_params=pltpu.CompilerParams(
            collective_id=1, has_side_effects=True, vmem_limit_bytes=60 * 2**20
        ),
    )(*args)


VEC = (8, 8 * WIDTH + 384)
VEC_STEPS = 7
MATS = (2, 1, 0)


def spread(whole):
    return (2 if 2 in whole else 1, 4 if 1 in whole else 1, (4 if 0 in whole else 1) * (2 if 2 in whole else 1))


def region_shape(u, phase, rows):
    lo, y, cols = spread(axes_of(u)[:phase])
    return (lo, y, rows, cols * WIDTHS[UNITS[u][0]])


def back_kernel(*refs):
    refs = list(refs)

    def take(n):
        got = refs[:n]
        del refs[:n]
        return got

    (normed_t, raw_ext, state_pre, grad_bc, grad_step_in, w_small, acc_in, pmain, phead, doc_col, hidden, cot, gain,
     vec_gate, vec_heads, x_ext, x_pre, grad_x, grad_gate, grad_out, full) = take(21)
    grad_main, grad_small, out_main, out_small, grad_hidden, vec_out = take(6)
    outs = (out_main, out_small)
    units = len(UNITS)
    other = take(2)
    half_buf = [take(3) for _ in range(units)]
    full_buf = [take(3) for _ in range(units)]
    own = take(units)
    (ext_in, pre_in, grad_in, first_grad, first_pre, first_out, after, w_in, staged, raw_x, acc, small_acc,
     small_out, vec_acc, vec_in) = take(15)
    (stream_sem, first_sem, halo_sem, w_sem, put_sem, small_sem, own_sem, vec_send, vec_recv, send, recv, core_send,
     core_recv) = take(13)
    at, core = coordinates()
    t = lax.axis_index("tensor")
    everything = range(units)

    def stream(j, slot):
        cols = tile_of(j)
        return [
            pltpu.make_async_copy(src.at[:, cols], dst.at[slot], stream_sem.at[i, slot])
            for i, (src, dst) in enumerate(((x_ext, ext_in), (x_pre, pre_in), (grad_x, grad_in)))
        ]

    firsts = [
        pltpu.make_async_copy(src.at[pl.ds(0, 8)], dst, first_sem.at[i])
        for i, (src, dst) in enumerate(((grad_x, first_grad), (x_pre, first_pre)))
    ]
    for c in firsts + stream(0, 0):
        c.start()
    greet(at, core, [device(moved(at, axis, 2), core) for axis in AXES] + [tensor_peer(1), tensor_peer(7)])

    def source_of(u, m):
        return grad_small if UNITS[u][0] else (grad_main, grad_gate, grad_out)[m]

    def units_of(m):
        return [u for u in everything if m == 0 or UNITS[u][0] == 0]

    def index_of(u, m):
        return 0 if UNITS[u][0] else m

    def part_of(ref, u, mats, where, whole, half=None):
        which, first, rows = UNITS[u][0], UNITS[u][1], 32
        if half is not None:
            first, rows = first + half * 16, 16
        return [ref.at[mats, lo, y, pl.ds(first, rows), cols] for lo, y, cols in pieces(where, whole, WIDTHS[which])]

    def place(u, by):
        return moved(at, axes_of(u)[2], by) if by else at

    groups = [[2], [1, -1], [0]]

    def to_partner(m):
        for g, group in enumerate(groups):
            for u in units_of(m):
                for by in group:
                    whole = axes_of(u)[:2]
                    for src, dst in zip(
                        region(source_of(u, m), u, 1 - core, pl.ds(0, 1), place(u, by), whole),
                        part_of(other[UNITS[u][0]], u, pl.ds(index_of(u, m), 1), place(u, by), whole),
                    ):
                        pltpu.make_async_remote_copy(
                            src_ref=src, dst_ref=dst, send_sem=core_send.at[u, m], recv_sem=core_recv.at[u, m, g],
                            device_id=device(at, 1 - core), device_id_type=MESH,
                        ).start()

    def await_partner(u, m, g):
        rows = 2 * len(groups[g])
        part = other[UNITS[u][0]].at[pl.ds(0, 1), pl.ds(0, 1), pl.ds(0, rows), pl.ds(0, 32)]
        pltpu.make_async_copy(part, part, core_recv.at[u, m, g]).wait()

    def own_loads(u, m, g):
        copies = []
        for slot, by in enumerate(groups[g]):
            parts = region(source_of(u, m), u, core, 0, place(u, by), axes_of(u)[:2])
            width = own[u].shape[-1] // len(parts)
            for i, src in enumerate(parts):
                copies.append(
                    pltpu.make_async_copy(src, own[u].at[slot, :, :, :, pl.ds(i * width, width)], own_sem.at[u, slot, i])
                )
        return copies

    def prefetch(m, g):
        for u in units_of(m):
            for c in own_loads(u, m, g):
                c.start()

    def add(u, phase, mats, where, half, terms, result=None):
        which, first, rows = UNITS[u][0], UNITS[u][1], 32
        if half is not None:
            first, rows = first + half * 16, 16
        whole = axes_of(u)[:phase]
        n_lo, n_y, _ = spread(whole)
        for i, (lo, y, cols) in enumerate(pieces(where, whole, WIDTHS[which])):

            @pl.loop(0, len(mats) * n_lo * n_y)
            def _(k, i=i, lo=lo, y=y, cols=cols):
                mat = mats[0] if len(mats) == 1 else lax.div(k, n_lo * n_y)
                a, b = lax.rem(lax.div(k, n_y), n_lo), lax.rem(k, n_y)
                here = (mat, lo.start + a, y.start + b, pl.ds(first, rows), cols)
                total = other[which][here].astype(F32)
                for term in terms:
                    total = total + term(mat, i, a, b).astype(F32)
                if result is None:
                    other[which][here] = total.astype(BF16)
                else:
                    result[mat, pl.ds(first, rows), :] = total

    def width_of(u, phase, ref):
        whole = axes_of(u)[:phase]
        return ref.shape[-1] // (2 if 2 in whole and 0 not in whole else 1)

    def from_own(u, slot, half=None):
        width = width_of(u, 2, own[u])
        rows = pl.ds(0, 32) if half is None else pl.ds(half * 16, 16)
        return lambda mat, i, a, b: own[u][slot, a, b, rows, pl.ds(i * width, width)]

    def from_buf(ref, side, u, phase):
        width = width_of(u, phase, ref)
        return lambda mat, i, a, b: ref[side, mat, a, b, :, pl.ds(i * width, width)]

    def mats_of(u, m):
        return pl.ds(0, STACK[UNITS[u][0]]) if m is None else pl.ds(index_of(u, m), 1)

    def send_step(u, phase, m, step):
        axes = axes_of(u)
        whole, axis = axes[:phase], axes[phase]
        index = phase if m is None else 2 + m
        buf = half_buf[u][phase] if step == 0 else full_buf[u][phase]
        for side, by in ((0, 1), (1, -1)):
            where = moved(at, axis, 2 if step == 0 else by)
            sources = part_of(other[UNITS[u][0]], u, mats_of(u, m), where, whole, side if step == 0 else None)
            width = buf.shape[-1] // len(sources)
            for i, src in enumerate(sources):
                pltpu.make_async_remote_copy(
                    src_ref=src, dst_ref=buf.at[side, mats_of(u, m), :, :, :, pl.ds(i * width, width)],
                    send_sem=send.at[u, index, step], recv_sem=recv.at[u, index, step],
                    device_id=device(moved(at, axis, by), core), device_id_type=MESH,
                ).start()

    def await_step(u, phase, m, step, sem):
        index = phase if m is None else 2 + m
        buf = half_buf[u][phase] if step == 0 else full_buf[u][phase]
        part = buf.at[:, mats_of(u, m)]
        pltpu.make_async_copy(part, part, sem.at[u, index, step]).wait()

    def stage(m, g):
        for u in units_of(m):
            for c in own_loads(u, m, g):
                c.wait()
            await_partner(u, m, g)
            mats = [index_of(u, m)]
            if g == 0:
                add(u, 2, mats, place(u, 2), None, [from_own(u, 0)])
                send_step(u, 2, m, 0)
            elif g == 1:
                await_step(u, 2, m, 0, recv)
                for side, by in ((0, 1), (1, -1)):
                    halves = [from_own(u, side, side), from_buf(half_buf[u][2], side, u, 2)]
                    add(u, 2, mats, place(u, by), side, halves)
                    add(u, 2, mats, place(u, by), 1 - side, [from_own(u, side, 1 - side)])
                send_step(u, 2, m, 1)
            else:
                await_step(u, 2, m, 1, recv)
                arrived = [from_buf(full_buf[u][2], side, u, 2) for side in (0, 1)]
                add(u, 2, mats, at, None, [from_own(u, 0)] + arrived)

    def vec_copy(k):
        (x, y, z) = at
        flip = lambda v: v + 1 - 2 * lax.rem(v, 2)
        to = [
            device(at, 1 - core),
            device((flip(x), y, z), core),
            device((x, flip(y), z), core),
            device((x, y, flip(z)), core),
            device(moved(at, 0, 2), core),
            device(moved(at, 1, 2), core),
            device(moved(at, 2, 2), core),
        ][k]
        return pltpu.make_async_remote_copy(
            src_ref=vec_acc.at[k], dst_ref=vec_in.at[k], send_sem=vec_send.at[k], recv_sem=vec_recv.at[k],
            device_id=to, device_id_type=MESH,
        )

    def vec_step(k):
        if k:
            vec_copy(k - 1).wait_recv()
            vec_acc[k] = vec_acc[k - 1] + vec_in[k - 1]
        if k < VEC_STEPS:
            vec_copy(k).start()
        else:
            vec_out[...] = vec_acc[VEC_STEPS]

    prefetch(2, 0)
    to_partner(2)
    to_partner(1)
    for c in firsts:
        c.wait()
    first_out[:, :DI] = first_grad[...] * silu_slope(first_pre[...])
    first_out[:, DI:] = grad_bc[:8] * silu_slope(state_pre[:8])

    def halo_copy():
        return pltpu.make_async_remote_copy(
            src_ref=first_out, dst_ref=after, send_sem=halo_sem.at[0], recv_sem=halo_sem.at[1],
            device_id=tensor_peer(7), device_id_type=MESH,
        )

    @pl.when(t > 0)
    def _():
        halo_copy().start()

    docs = doc_col[...]
    links = [None] + [conv_links(docs, o, BLOCK + 8) for o in range(1, TAPS)]
    params = small_params(phead[...])
    vec = vec_acc.at[0]
    vec[...] = jnp.zeros(VEC, F32)

    @pl.when(t < 7)
    def _():
        halo_copy().wait_recv()

    @pl.when(t == 7)
    def _():
        after[...] = jnp.zeros_like(after)

    def conv_back(grad, grad_after, ext, taps):
        grad_ext = jnp.concatenate([grad, grad_after], 0)
        total = taps[TAPS - 1 : TAPS] * grad
        rows = [None] * TAPS
        rows[TAPS - 1] = jnp.sum(grad * ext[HALO:], axis=0, keepdims=True)
        for offset in range(1, TAPS):
            masked = grad_ext * links[offset]
            rows[TAPS - 1 - offset] = jnp.sum(masked[:BLOCK] * ext[HALO - offset : EXT - offset], axis=0, keepdims=True)
            total = total + taps[TAPS - 1 - offset : TAPS - offset] * masked[offset : offset + BLOCK]
        return total, rows + [jnp.sum(grad, axis=0, keepdims=True)]

    flat_main = [(lo, y, c) for lo in range(2) for y in range(4) for c in range(2)]

    def put(j, slot):
        cols = tile_of(j)
        return [
            pltpu.make_async_copy(
                staged.at[slot, pl.ds(i * ROWS, ROWS)], grad_main.at[0, lo, y, c, :, cols], put_sem.at[slot, i]
            )
            for i, (lo, y, c) in enumerate(flat_main)
        ]

    def x_tiles(first, last):
        @pl.loop(first, last)
        def _(j):
            slot = lax.rem(j, 2)
            cols = tile_of(j)

            @pl.when(j + 1 < TILES)
            def _():
                for c in stream(j + 1, 1 - slot):
                    c.start()

            for c in stream(j, slot):
                c.wait()
            grad = grad_in[slot] * silu_slope(pre_in[slot])
            total, rows = conv_back(grad, after[:, cols], ext_in[slot], pmain[0:TAPS, cols])
            for i, row in enumerate(rows):
                vec[i : i + 1, cols] = row
            total = total.astype(BF16)
            raw_x[:, cols] = total

            @pl.when(j >= 2)
            def _():
                for c in put(j, slot):
                    c.wait()

            staged[slot] = dot(normed_t[...], total).astype(BF16)
            for c in put(j, slot):
                c.start()

    def small_part():
        grad = grad_bc[...] * silu_slope(state_pre[...])
        total, rows = conv_back(grad, after[:, DI:], raw_ext[:, :256], params[:TAPS, :256])
        for i, row in enumerate(rows):
            vec[i : i + 1, DI : DI + 256] = row
        raw = jnp.concatenate([total.astype(BF16), grad_step_in[...].astype(BF16)], 1)
        acc[...] = acc_in[...] + dot(raw, w_small[...], (1, 1))
        small_acc[...] = dot(normed_t[...], raw).astype(BF16)
        packed = jnp.zeros((512, 8 * LANES), F32)
        for r in range(3):
            rows_r = jnp.concatenate([small_acc[pl.ds(d * 96 + r * 32, 32)] for d in range(16)], 0)
            packed = packed + dot(rows_r, small_map(r), (1, 1))
        small_out[...] = packed.astype(BF16)
        for c in small_puts:
            c.start()

    small_puts = [
        pltpu.make_async_copy(small_out.at[pl.ds(i * 32, 32)], grad_small.at[0, lo, y, c], small_sem.at[i])
        for i, (lo, y, c) in enumerate(flat_main)
    ]

    def input_tiles(first, last):
        @pl.loop(first, last)
        def _(k):
            slot = lax.rem(k, 2)

            def load(n, into):
                return pltpu.make_async_copy(full.at[0, :, tile_of(n)], w_in.at[into], w_sem.at[into])

            @pl.when(k + 1 < TILES)
            def _():
                load(k + 1, 1 - slot).start()

            load(k, slot).wait()
            acc[...] += dot(raw_x[:, tile_of(k)], w_in[slot], (1, 1))

    def input_grad():
        value = hidden[...].astype(F32)
        inv = lax.rsqrt(jnp.mean(value * value, axis=1, keepdims=True) + epsilon)
        rows = value * inv
        grad = acc[...]
        vec[5:6, 0:DI] = vec_gate[0:1, :]
        vec[6:7, 0:D] = jnp.sum(grad * rows, axis=0, keepdims=True)
        vec[5:8, DI + 256 :] = vec_heads[5:8, :]
        dn = grad * gain[...]
        mean = jnp.mean(dn * rows, axis=1, keepdims=True)
        grad_hidden[...] = cot[...].astype(F32) + inv * dn - rows * inv * mean

    stage(2, 0)
    prefetch(1, 0)
    small_part()
    x_tiles(0, 1)
    stage(1, 0)
    prefetch(2, 1)
    x_tiles(1, 3)
    stage(2, 1)
    prefetch(1, 1)
    x_tiles(3, 5)
    stage(1, 1)
    prefetch(2, 2)
    x_tiles(5, 6)
    pltpu.make_async_copy(full.at[0, :, tile_of(0)], w_in.at[0], w_sem.at[0]).start()
    for slot in range(2):
        for c in put(TILES - 2 + slot, slot):
            c.wait()
    for c in small_puts:
        c.wait()
    to_partner(0)
    input_tiles(0, 3)
    stage(2, 2)
    prefetch(1, 2)
    input_tiles(3, 6)
    stage(1, 2)
    prefetch(0, 0)
    input_grad()
    vec_step(0)
    stage(0, 0)
    prefetch(0, 1)
    vec_step(1)
    stage(0, 1)
    prefetch(0, 2)
    vec_step(2)
    stage(0, 2)
    vec_step(3)
    for phase in (1, 0):
        for u in everything:
            send_step(u, phase, None, 0)
        vec_step(4 if phase else 6)
        for u in everything:
            axis = axes_of(u)[phase]
            mats = list(range(STACK[UNITS[u][0]]))
            await_step(u, phase, None, 0, recv)
            for side, by in ((0, 1), (1, -1)):
                add(u, phase, mats, moved(at, axis, by), side, [from_buf(half_buf[u][phase], side, u, phase)])
            send_step(u, phase, None, 1)
        vec_step(5 if phase else 7)
        for u in everything:
            mats = list(range(STACK[UNITS[u][0]]))
            await_step(u, phase, None, 1, recv)
            arrived = [from_buf(full_buf[u][phase], side, u, phase) for side in (0, 1)]
            add(u, phase, mats, at, None, arrived, None if phase else outs[UNITS[u][0]])
    for m in MATS:
        for u in units_of(m):
            part = other[UNITS[u][0]].at[pl.ds(0, 1), :, :, pl.ds(0, 32)]
            pltpu.make_async_copy(part, part, core_send.at[u, m]).wait()
            for step in (0, 1):
                await_step(u, 2, m, step, send)
    for u in everything:
        for phase in (0, 1):
            for step in (0, 1):
                await_step(u, phase, None, step, send)
    for k in range(VEC_STEPS):
        vec_copy(k).wait_send()

    @pl.when(t > 0)
    def _():
        halo_copy().wait_send()


def back(*args):
    vmem = pl.BlockSpec(memory_space=VMEM)
    anywhere = pl.BlockSpec(memory_space=pl.ANY)
    units = range(len(UNITS))
    n = len(UNITS)
    held = [(3, 2, 4, ROWS, 8 * WIDTH), (1, 2, 4, SMALL_ROWS, 8 * SMALL_WIDTH)]
    landing = [(2, STACK[UNITS[u][0]]) + region_shape(u, p, rows) for rows in (16, 32) for u in units for p in range(3)]
    return pl.pallas_call(
        back_kernel,
        name="project_back",
        out_shape=[
            jax.ShapeDtypeStruct((1, 2, 4, 2, ROWS, DI), BF16),
            jax.ShapeDtypeStruct((1, 2, 4, 2, SMALL_ROWS, 8 * LANES), BF16),
            jax.ShapeDtypeStruct((3, ROWS, WIDTH), F32),
            jax.ShapeDtypeStruct((1, SMALL_ROWS, SMALL_WIDTH), F32),
            jax.ShapeDtypeStruct((BLOCK, D), F32),
            jax.ShapeDtypeStruct(VEC, F32),
        ],
        in_specs=[vmem] * 15 + [anywhere] * 6,
        out_specs=[anywhere, anywhere, vmem, vmem, vmem, vmem],
        scratch_shapes=[VMEM(s, BF16) for s in held + landing]
        + [VMEM((2,) + region_shape(u, 2, 32), BF16) for u in units]
        + [
            VMEM((2, EXT, TILE), F32), VMEM((2, BLOCK, TILE), F32), VMEM((2, BLOCK, TILE), F32),
            VMEM((8, DI), F32), VMEM((8, DI), F32), VMEM((8, DI + 256), F32), VMEM((8, DI + 256), F32),
            VMEM((2, D, TILE), BF16), VMEM((2, D, TILE), BF16), VMEM((BLOCK, DI), BF16),
            VMEM((BLOCK, D), F32), VMEM((D, SMALL), BF16), VMEM((512, 8 * LANES), BF16),
            VMEM((VEC_STEPS + 1,) + VEC, F32), VMEM((VEC_STEPS,) + VEC, F32),
        ]
        + [
            pltpu.SemaphoreType.DMA(s)
            for s in (
                (3, 2), (2,), (2,), (2,), (2, 16), (16,), (n, 2, 2), (VEC_STEPS,), (VEC_STEPS,), (n, 5, 2), (n, 5, 2),
                (n, 3), (n, 3, 3),
            )
        ],
        compiler_params=pltpu.CompilerParams(collective_id=3, has_side_effects=True, vmem_limit_bytes=62 * 2**20),
    )(*args)


def per_device(
    hidden,
    doc_ids,
    norm_gain,
    main_proj,
    step_proj,
    state_proj,
    conv_main,
    conv_main_bias,
    conv_state,
    conv_state_bias,
    step_bias,
    decay_log,
    skip_gain,
    gate_gain,
    out_proj,
    cotangent,
):
    t = lax.axis_index("tensor")
    shards = jnp.stack([main_proj[:, 1], main_proj[:, 0], out_proj])
    small = jnp.concatenate([state_proj, step_proj], axis=1).reshape(3, SMALL_ROWS, 38)
    small = jnp.pad(small.transpose(1, 0, 2).reshape(SMALL_ROWS, 114), ((0, 0), (0, 14)))[None]
    params = pack_params(
        conv_main, conv_main_bias, conv_state, conv_state_bias, step_bias, decay_log, skip_gain, gate_gain
    )
    full, packed, halo, pmain, phead = gather_weights(shards, small, hidden[BLOCK - HALO :], params)
    full, packed = full.reshape(3, D, DI), packed.reshape(512, 8 * LANES)
    gain = norm_gain[None]

    docs_all = jnp.concatenate([jnp.full((HALO,), -1, jnp.int32), doc_ids, jnp.full((16,), -2, jnp.int32)])
    docs = lax.dynamic_slice(docs_all, (t * BLOCK,), (EXT + 16,))
    doc_col, doc_row = docs[:, None], docs[None, HALO:EXT]

    (mixed, normed_t, raw, state_pre, grad_bc, grad_step_in, w_small, acc, grad_x, vec_gate, vec_heads, x_ext, x_pre,
     grad_out, grad_gate) = mid(
        hidden, halo, gain, packed, pmain, phead, doc_col, doc_row, cotangent, full
    )
    _, _, own_main, own_small, grad_hidden, vec = back(
        normed_t, raw, state_pre, grad_bc, grad_step_in, w_small, acc, pmain, phead, doc_col, hidden, cotangent,
        gain, vec_gate, vec_heads, x_ext, x_pre, grad_x, grad_gate, grad_out, full,
    )
    own_small = own_small[0, :, :114].reshape(SMALL_ROWS, 3, 38).transpose(1, 0, 2).reshape(ROWS, 38)
    vec_main = lax.dynamic_slice(vec, (0, t * WIDTH), (8, WIDTH))
    vec_state = lax.dynamic_slice(vec, (0, DI + t * 32), (5, 32))
    vec_head = lax.dynamic_slice(vec, (5, DI + 256 + t * 6), (3, 6))
    return (
        mixed,
        grad_hidden,
        vec[6, :D],
        jnp.stack([own_main[1], own_main[0]], axis=1),
        own_small[:, 32:],
        own_small[:, :32],
        vec_main[:TAPS],
        vec_main[TAPS],
        vec_state[:TAPS],
        vec_state[TAPS],
        vec_head[0],
        vec_head[1],
        vec_head[2],
        vec_main[5],
        own_main[2],
    )


def solution(mesh):
    placed = (
        P(("dp", "tensor"), None),
        P("dp"),
        P(),
        P("dp", None, "tensor"),
        P("dp", "tensor"),
        P("dp", "tensor"),
        P(None, "tensor"),
        P("tensor"),
        P(None, "tensor"),
        P("tensor"),
        P("tensor"),
        P("tensor"),
        P("tensor"),
        P("tensor"),
        P("dp", "tensor"),
        P(("dp", "tensor"), None),
    )
    return jax.shard_map(
        per_device,
        mesh=mesh,
        in_specs=placed,
        out_specs=(
            P(("dp", "tensor"), None),
            P(("dp", "tensor"), None),
            P(),
            P("dp", None, "tensor"),
            P("dp", "tensor"),
            P("dp", "tensor"),
            P(None, "tensor"),
            P("tensor"),
            P(None, "tensor"),
            P("tensor"),
            P("tensor"),
            P("tensor"),
            P("tensor"),
            P("tensor"),
            P("dp", "tensor"),
        ),
        check_vma=False,
    )
```

```python
import functools

import jax
import jax.numpy as jnp
from jax import lax
from jax.experimental import pallas as pl
from jax.experimental.pallas import tpu as pltpu
from jax.sharding import PartitionSpec as P

BLOCK = 256
epsilon = 1e-05

MESH = pl.DeviceIdType.MESH
AXES = (0, 1, 2)
SIDE = 4


def coordinates():
    dp = lax.axis_index("dp")
    t = lax.axis_index("tensor")
    z = lax.div(t, 4) * 2 + lax.div(dp, 8)
    return (lax.rem(t, 4), lax.rem(lax.div(dp, 2), 4), z), lax.rem(dp, 2)


def device(at, core):
    x, y, z = at
    return (lax.rem(z, 2) * 8 + y * 2 + core, lax.div(z, 2) * 4 + x)


def moved(at, axis, by):
    return tuple(lax.rem(v + by + SIDE, SIDE) if i == axis else v for i, v in enumerate(at))


def pieces(at, whole, width):
    x, y, z = at
    lo = pl.ds(0, 2) if 2 in whole else pl.ds(lax.rem(z, 2), 1)
    row = pl.ds(0, 4) if 1 in whole else pl.ds(y, 1)
    hi = lax.div(z, 2)
    if 0 in whole and 2 in whole:
        cols = [pl.ds(0, 8 * width)]
    elif 0 in whole:
        cols = [pl.ds(pl.multiple_of(hi * 4 * width, 128), 4 * width)]
    elif 2 in whole:
        cols = [
            pl.ds(pl.multiple_of(x * width, 128), width),
            pl.ds(pl.multiple_of((4 + x) * width, 128), width),
        ]
    else:
        cols = [pl.ds(pl.multiple_of((hi * 4 + x) * width, 128), width)]
    return [(lo, row, c) for c in cols]


def greet(at, core, group):
    barrier = pltpu.get_barrier_semaphore()
    others = [device(moved(at, axis, by), core) for axis in AXES for by in (1, -1)]
    others.append(device(at, 1 - core))
    others += group
    for other in others:
        pl.semaphore_signal(barrier, inc=1, device_id=other, device_id_type=MESH)
    pl.semaphore_wait(barrier, len(others))


def tensor_peer(by):
    return (lax.axis_index("dp"), lax.rem(lax.axis_index("tensor") + by, 8))


ROWS, WIDTH, SMALL_ROWS, SMALL_WIDTH = 96, 384, 32, 128
UNITS = [(0, q * 32, q) for q in range(3)] + [(1, 0, 0)]
WIDTHS = [WIDTH, SMALL_WIDTH]
STACK = [3, 1]


def axes_of(u):
    return [(UNITS[u][2] + j) % 3 for j in range(3)]


def region(ref, u, core, mats, where, whole, half=None):
    which, first, rows = UNITS[u][0], UNITS[u][1], 32
    if half is not None:
        first, rows = first + half * 16, 16
    return [
        ref.at[mats, lo, row, core, pl.ds(first, rows), cols]
        for lo, row, cols in pieces(where, whole, WIDTHS[which])
    ]


def sized(ref, u, mats, blocks, halves=2):
    width = WIDTHS[UNITS[u][0]]
    cols = min(blocks, 8)
    rest = blocks // cols
    return ref.at[mats, pl.ds(0, max(rest // 4, 1)), pl.ds(0, min(rest, 4)), 0, pl.ds(0, 16 * halves), pl.ds(0, cols * width)]


def gather_ops(full, send, recv, core_send, core_recv):
    at, core = coordinates()

    def sends(u, phase, mats, step, key):
        axes = axes_of(u)
        whole, axis = axes[:phase], axes[phase]
        for kind, by in ((0, 1), (1, -1)):
            where = at if step == 0 else moved(at, axis, -by)
            for part in region(full[UNITS[u][0]], u, core, mats, where, whole, kind if step else None):
                pltpu.make_async_remote_copy(
                    src_ref=part, dst_ref=part, send_sem=send.at[u, key, step], recv_sem=recv.at[u, key, step],
                    device_id=device(moved(at, axis, by), core), device_id_type=MESH,
                ).start()

    def await_step(u, phase, mats, step, key, sem):
        part = sized(full[UNITS[u][0]], u, mats, 2 * 4**phase // (1 + step))
        pltpu.make_async_copy(part, part, sem.at[u, key, step]).wait()

    def to_partner(u, mats, bys, key):
        axes = axes_of(u)
        for by in bys:
            where = moved(at, axes[2], by) if by else at
            for part in region(full[UNITS[u][0]], u, core, mats, where, axes[:2]):
                pltpu.make_async_remote_copy(
                    src_ref=part, dst_ref=part, send_sem=core_send.at[u, key], recv_sem=core_recv.at[u, key],
                    device_id=device(at, 1 - core), device_id_type=MESH,
                ).start()

    def await_partner(u, mats, key, sem):
        part = sized(full[UNITS[u][0]], u, mats, 64)
        pltpu.make_async_copy(part, part, sem.at[u, key]).wait()

    return sends, await_step, to_partner, await_partner


MAIN_UNITS = range(3)
ALL = pl.ds(0, 3)


D, DI, HEADS, HEAD_DIM, STATE, TAPS, HALO = 1536, 3072, 48, 64, 128, 4, 16
BF16, F32 = jnp.bfloat16, jnp.float32
TILE, LANES, SMALL = 512, 128, 384
TILES = DI // TILE
LOG2E = 1.4426950408889634
EXT = HALO + BLOCK
VMEM = pltpu.VMEM


def dot(a, b, dims=(1, 0), precision=None):
    return lax.dot_general(
        a, b, ((dims[:1], dims[1:]), ((), ())), precision=precision, preferred_element_type=F32
    )


def iota(shape, dim):
    return lax.broadcasted_iota(jnp.int32, shape, dim)


def sigmoid(v):
    return 1.0 / (1.0 + jnp.exp(-v))


def silu(v):
    return v * sigmoid(v)


def silu_slope(v):
    s = sigmoid(v)
    return s * (1.0 + v * (1.0 - s))


def softplus(v):
    return jnp.maximum(v, 0.0) + jnp.log1p(jnp.exp(-jnp.abs(v)))


def split(v):
    high = v.astype(BF16)
    return high, (v - high.astype(F32)).astype(BF16)


def head_map(j):
    return (iota((LANES, TILE), 0) == j * (TILE // HEAD_DIM) + iota((LANES, TILE), 1) // HEAD_DIM).astype(BF16)


def widen(v, j):
    high, low = split(v)
    return dot(high, head_map(j)) + dot(low, head_map(j))


def by_head(v, j):
    high, low = split(v)
    return dot(high, head_map(j), (1, 1)) + dot(low, head_map(j), (1, 1))


def small_map(r):
    row, col = iota((8 * LANES, SMALL), 0), iota((8 * LANES, SMALL), 1)
    t, lane = row // LANES, row % LANES - 38 * r
    state = (lane >= 0) & (lane < 32) & (col == t * 32 + lane)
    step = (lane >= 32) & (lane < 38) & (col == 256 + t * 6 + lane - 32)
    return (state | step).astype(BF16)


def tile_of(j):
    return pl.ds(pl.multiple_of(j * TILE, TILE), TILE)


def conv_links(doc_col, offset, rows):
    return (doc_col[HALO : HALO + rows] == doc_col[HALO - offset : HALO - offset + rows]).astype(F32)


def conv(ext, taps, bias, links):
    total = bias + taps[TAPS - 1 : TAPS] * ext[HALO:]
    for offset in range(1, TAPS):
        total = total + taps[TAPS - 1 - offset : TAPS - offset] * ext[HALO - offset : EXT - offset] * links[offset]
    return total


def small_params(phead):
    return dot(phead, small_map(0).astype(F32), precision=lax.Precision.HIGHEST)


def decay_terms(step, cum, doc_col, doc_prev):
    block = doc_col[HALO:EXT]
    end = cum[BLOCK - 1 : BLOCK]
    tail = jnp.exp(end - cum) * (block == block[BLOCK - 1 : BLOCK]).astype(F32)
    enter = jnp.exp(cum) * (block == doc_prev).astype(F32)
    keep = jnp.exp(end) * (block[BLOCK - 1 : BLOCK] == doc_prev).astype(F32)
    return enter, tail, tail * step, keep


def pack_kernel(
    main_proj, out_proj, state_proj, step_proj, conv_main, conv_main_bias, conv_state, conv_state_bias, step_bias,
    decay_log, skip_gain, gate_gain, norm_gain, doc_ids,
    shards, small, pmain, phead, doc_col, doc_row, gain, docs,
):
    t = lax.axis_index("tensor")
    shards[0] = main_proj[:, 1, :]
    shards[1] = main_proj[:, 0, :]
    shards[2] = out_proj[...]
    lanes = [jnp.concatenate([state_proj[...], step_proj[...]], 1)[r * 32 : r * 32 + 32] for r in range(3)]
    small[0] = jnp.concatenate(lanes + [jnp.zeros((SMALL_ROWS, 14), BF16)], 1)
    pmain[0:TAPS] = conv_main[...]
    pmain[TAPS : TAPS + 1] = conv_main_bias[...].reshape(1, WIDTH)
    pmain[5:6] = gate_gain[...].reshape(1, WIDTH)
    own_skip = skip_gain[...].reshape(1, 6)
    pmain[6:7] = jnp.concatenate([jnp.broadcast_to(own_skip[:, h : h + 1], (1, HEAD_DIM)) for h in range(6)], 1)
    pmain[7:8] = jnp.zeros((1, WIDTH), F32)
    phead[...] = jnp.zeros_like(phead)
    phead[0:TAPS, 0:32] = conv_state[...]
    phead[TAPS : TAPS + 1, 0:32] = conv_state_bias[...].reshape(1, 32)
    phead[5:6, 32:38] = step_bias[...].reshape(1, 6)
    phead[6:7, 32:38] = decay_log[...].reshape(1, 6)
    phead[7:8, 32:38] = own_skip
    gain[...] = norm_gain[...].reshape(1, D)
    docs[:, 0:LANES] = jnp.full((8, LANES), -1, jnp.int32)
    docs[:, LANES : LANES + 2048] = jnp.broadcast_to(doc_ids[...].reshape(1, 2048), (8, 2048))
    docs[:, LANES + 2048 :] = jnp.full((8, LANES), -2, jnp.int32)
    window = docs[:, pl.ds(pl.multiple_of(t * BLOCK, LANES), 2 * BLOCK)]
    doc_row[...] = window[0:1, LANES : LANES + BLOCK]
    doc_col[...] = window.T[LANES - HALO : LANES + BLOCK + 16, 0:1]


def pack(*args):
    vmem = pl.BlockSpec(memory_space=VMEM)
    shapes = [
        ((3, ROWS, WIDTH), BF16), ((1, SMALL_ROWS, SMALL_WIDTH), BF16), ((8, WIDTH), F32), ((8, LANES), F32),
        ((EXT + 16, 1), jnp.int32), ((1, BLOCK), jnp.int32), ((1, D), F32),
    ]
    return pl.pallas_call(
        pack_kernel,
        name="pack",
        out_shape=[jax.ShapeDtypeStruct(*s) for s in shapes],
        in_specs=[vmem] * 14,
        out_specs=[vmem] * len(shapes),
        scratch_shapes=[VMEM((8, 2048 + 2 * LANES), jnp.int32)],
    )(*args)


def finish_kernel(
    own_main, own_small, vec,
    norm_gain, main_proj, step_proj, state_proj, conv_main, conv_main_bias, conv_state, conv_state_bias, step_bias,
    decay_log, skip_gain, gate_gain, out_proj,
):
    t = lax.axis_index("tensor")
    main_proj[:, 0, :] = own_main[1]
    main_proj[:, 1, :] = own_main[0]
    out_proj[...] = own_main[2]
    packed = own_small[0]
    for r in range(3):
        rows = pl.ds(r * 32, 32)
        state_proj[rows] = packed[:, r * 38 : r * 38 + 32]
        step_proj[rows] = packed[:, r * 38 + 32 : r * 38 + 38]
    own = vec[:, pl.ds(pl.multiple_of(t * WIDTH, LANES), WIDTH)]
    conv_main[...] = own[:TAPS]
    conv_main_bias[...] = own[TAPS : TAPS + 1]
    gate_gain[...] = own[5:6]
    state = pltpu.roll(vec[:, DI : DI + 256], lax.rem(256 - 32 * t, 256), axis=1)
    conv_state[...] = state[:TAPS, :32]
    conv_state_bias[...] = state[TAPS : TAPS + 1, :32]
    heads = pltpu.roll(vec[:, DI + 256 :], lax.rem(LANES - 6 * t, LANES), axis=1)
    step_bias[...] = heads[5:6, :6]
    decay_log[...] = heads[6:7, :6]
    skip_gain[...] = heads[7:8, :6]
    norm_gain[...] = vec[6:7, 0:D]


def finish(*args):
    vmem = pl.BlockSpec(memory_space=VMEM)
    shapes = [
        (1, D), (ROWS, 2, WIDTH), (ROWS, 6), (ROWS, 32), (TAPS, WIDTH), (1, WIDTH), (TAPS, 32), (1, 32), (1, 6), (1, 6),
        (1, 6), (1, WIDTH), (ROWS, WIDTH),
    ]
    outs = pl.pallas_call(
        finish_kernel,
        name="finish",
        out_shape=[jax.ShapeDtypeStruct(s, F32) for s in shapes],
        in_specs=[vmem] * 3,
        out_specs=[vmem] * len(shapes),
    )(*args)
    return [v[0] if v.shape[0] == 1 else v for v in outs]


PAIR = 2 * HEAD_DIM
PAIRS = DI // PAIR
HALF = BLOCK // 2
CHUNK = 128
CHUNKS = DI // CHUNK
FORWARD_LAG, BACKWARD_LAG = 7, 4


def pair_of(p):
    return pl.ds(pl.multiple_of(p * PAIR, PAIR), PAIR)


def chunk_of(c):
    return pl.ds(pl.multiple_of(c * CHUNK, CHUNK), CHUNK)


def only(value, first):
    lane = iota(value.shape, 1)
    return jnp.where((lane < HEAD_DIM) == first, value, jnp.zeros_like(value))


def head_column(ref, h):
    return pltpu.roll(ref[...], lax.rem(LANES - h, LANES), axis=1)[:, :1]


def mid_kernel(
    hidden, gain, doc_col, doc_row, cot, shards, small, pmain_own, phead_own,
    mixed, pmain, phead, normed_t, raw, state_pre, grad_bc, grad_step_in, w_small, acc, grad_x, vec_gate, vec_heads,
    x_ext, x_pre, grad_out, grad_gate, full,
    packed, halo, normed, w_in, ext_out, pre_out, staged, x_act, bc, scores, gate_in, work, y, gate_out, dy, gate_grad, update,
    grad_add, state, state_low, grad_state, keep_row, f_out, f_in, b_out, b_in, cot_t, mixed_acc,
    barred, cum2, cum_t, step_t, step_in, enter_ref, weight_ref, rows_acc, q_t, gs, acc_c, acc_heads, row_acc,
    w_sem, put_sem, x_sem, f_send, f_recv, b_send, b_recv, g_send, g_recv, core_send, core_recv, own_sem, halo_sem,
    param_send, param_recv,
):
    t = lax.axis_index("tensor")

    def load(m, j, slot):
        return pltpu.make_async_copy(full.at[m, :, :, :, :, tile_of(j)], w_in.at[slot], w_sem.at[slot])

    def held(slot):
        return w_in[slot].reshape(D, TILE)

    at, core = coordinates()
    both = [full, packed]
    own = []
    for w, source in enumerate((shards, small)):
        for lo, row, cols in pieces(at, (), WIDTHS[w]):
            own.append(
                pltpu.make_async_copy(source, both[w].at[:, lo.start, row.start, core, :, cols], own_sem.at[w])
            )
    params_own, params_all = (pmain_own, phead_own), (pmain, phead)

    def columns(i, of):
        width = params_own[i].shape[-1]
        return params_all[i].at[:, pl.ds(pl.multiple_of(of * width, 128), width)]

    for i in range(2):
        own.append(pltpu.make_async_copy(params_own[i], columns(i, t), own_sem.at[2 + i]))
    for c in own:
        c.start()
    greet(at, core, [tensor_peer(by) for by in range(1, 8)])
    sends, await_step, to_partner, await_partner = gather_ops(both, g_send, g_recv, core_send, core_recv)

    def halo_copy():
        return pltpu.make_async_remote_copy(
            src_ref=hidden.at[pl.ds(BLOCK - HALO, HALO)], dst_ref=halo, send_sem=halo_sem.at[0],
            recv_sem=halo_sem.at[1], device_id=tensor_peer(1), device_id_type=MESH,
        )

    def param_copy(by, i, of):
        return pltpu.make_async_remote_copy(
            src_ref=params_own[i], dst_ref=columns(i, of), send_sem=param_send.at[i, by - 1],
            recv_sem=param_recv.at[i, by - 1], device_id=tensor_peer(by), device_id_type=MESH,
        )

    everything = [3, 0, 1, 2]

    def early(u):
        return pl.ds(0, STACK[UNITS[u][0]])

    def rms(rows, part):
        value = part[...].astype(F32)
        inv = lax.rsqrt(jnp.mean(value * value, axis=1, keepdims=True) + epsilon)
        normed[rows] = (value * inv * gain[...]).astype(BF16)

    for c in own:
        c.wait()
    for u in everything:
        sends(u, 0, early(u), 0, 0)
    halo_copy().start()
    for by in range(1, 8):
        for i in range(2):
            param_copy(by, i, t).start()
    rms(pl.ds(HALO, BLOCK), hidden)
    for phase in (0, 1):
        for u in everything:
            await_step(u, phase, early(u), 0, phase, g_recv)
            sends(u, phase, early(u), 1, phase)
        if phase == 0:
            cot_t[...] = cot[...].T
        else:
            normed_t[...] = normed[pl.ds(HALO, BLOCK)].T
        for u in everything:
            await_step(u, phase, early(u), 1, phase, g_recv)
            if phase == 0:
                sends(u, 1, early(u), 0, 1)

    def units_with(m):
        return [3] if m == 3 else MAIN_UNITS

    def gather_first(m):
        for u in units_with(m):
            sends(u, 2, pl.ds(m % 3, 1), 0, 2 + m % 3)

    def gather_near(m):
        for u in units_with(m):
            to_partner(u, pl.ds(m % 3, 1), [0], m % 3)

    def gather_forward(m):
        for u in units_with(m):
            await_step(u, 2, pl.ds(m % 3, 1), 0, 2 + m % 3, g_recv)
            sends(u, 2, pl.ds(m % 3, 1), 1, 2 + m % 3)

    def gather_second(m):
        for u in units_with(m):
            to_partner(u, pl.ds(m % 3, 1), [-1, 1], m % 3)

    def gather_last(m):
        for u in units_with(m):
            await_step(u, 2, pl.ds(m % 3, 1), 1, 2 + m % 3, g_recv)
            to_partner(u, pl.ds(m % 3, 1), [2], m % 3)

    def gather_done(m):
        for u in units_with(m):
            await_partner(u, pl.ds(m % 3, 1), m % 3, core_recv)

    gather_first(3)
    gather_first(0)
    gather_near(3)
    gather_near(0)
    halo_copy().wait()
    rms(pl.ds(0, HALO), halo)
    for by in range(1, 8):
        for i in range(2):
            param_copy(by, i, lax.rem(t + 8 - by, 8)).wait()
    gather_forward(3)
    gather_second(3)
    gather_last(3)
    gather_forward(0)
    gather_first(1)
    gather_first(2)
    gather_second(0)
    gather_done(3)

    for r in range(3):
        rows = dot(packed[...].reshape(512, 8 * LANES), small_map(r)).astype(BF16)
        for d in range(16):
            w_small[pl.ds(d * 96 + r * 32, 32)] = rows[d * 32 : d * 32 + 32]
    raw[...] = dot(normed[...], w_small[...])
    params = small_params(phead[...])
    docs = doc_col[...]
    links = [None] + [conv_links(docs, o, BLOCK) for o in range(1, TAPS)]
    pre = conv(raw[:, :256], params[:TAPS, :256], params[TAPS : TAPS + 1, :256], links)
    state_pre[...] = pre
    act = silu(pre).astype(BF16)
    bc[...] = act
    scores[...] = dot(act[:, STATE:], act[:, :STATE], (1, 1))
    step_in[...] = raw[HALO:, 256:] + params[5:6, 256:]
    rate = -jnp.exp(params[6:7, 256:])
    step = softplus(step_in[...])
    lower = (iota((BLOCK, BLOCK), 0) >= iota((BLOCK, BLOCK), 1)).astype(F32)
    cum = dot(lower, step * rate, precision=lax.Precision.HIGHEST)
    enter, tail, weight, keep = decay_terms(step, cum, docs, docs[HALO - 1 : HALO])
    enter_ref[...] = enter
    weight_ref[...] = weight
    cum2[...] = cum * LOG2E
    for ref, turned in ((cum_t, (cum * LOG2E).T), (step_t, step.T)):
        for h in range(HEADS):
            ref[h] = turned[h : h + 1]
    linked = (docs[HALO:EXT] == doc_row[...]) & (iota((BLOCK, BLOCK), 0) >= iota((BLOCK, BLOCK), 1))
    barred[...] = jnp.where(linked, 0.0, -1e30)
    keep8 = jnp.broadcast_to(keep, (8, LANES))

    gather_last(0)
    gather_near(1)
    gather_near(2)
    gather_done(0)
    load(0, 0, 0).start()

    def chain(forward, c, add, into, outgoing, incoming, send, recv):
        cols = chunk_of(c)
        by = 1 if forward else 7
        is_first = t == (0 if forward else 7)
        is_last = t == (7 if forward else 0)

        def copy():
            return pltpu.make_async_remote_copy(
                src_ref=outgoing.at[:, cols], dst_ref=incoming.at[:, cols], send_sem=send.at[c],
                recv_sem=recv.at[c], device_id=tensor_peer(by), device_id_type=MESH,
            )

        @pl.when(is_first)
        def _():
            into[:, cols] = jnp.zeros((STATE, CHUNK), F32)

        @pl.when(jnp.logical_not(is_first))
        def _():
            copy().wait_recv()
            into[:, cols] = incoming[:, cols].astype(F32)

        @pl.when(jnp.logical_not(is_last))
        def _():
            outgoing[:, cols] = (keep_row[0:1, cols] * into[:, cols] + add[:, cols]).astype(BF16)
            copy().start()

    def forward_slot(s):
        c = s - FORWARD_LAG * t

        @pl.when((c >= 0) & (c < CHUNKS))
        def _():
            chain(True, c, update, state, f_out, f_in, f_send, f_recv)

    def backward_slot(s):
        c = s - BACKWARD_LAG * (7 - t)

        @pl.when((c >= 0) & (c < CHUNKS))
        def _():
            chain(False, c, grad_add, grad_state, b_out, b_in, b_send, b_recv)

    def x_puts(j, slot):
        return [
            pltpu.make_async_copy(src.at[slot], dst.at[:, tile_of(j)], x_sem.at[i, slot])
            for i, (src, dst) in enumerate(((ext_out, x_ext), (pre_out, x_pre)))
        ]

    def x_tile(j):
        cols = tile_of(j)
        slot = lax.rem(j, 2)

        @pl.when(j + 1 < TILES)
        def _():
            load(0, j + 1, 1 - slot).start()

        @pl.when(j >= 2)
        def _():
            for c in x_puts(j, slot):
                c.wait()

        load(0, j, slot).wait()
        ext = dot(normed[...], held(slot))
        ext_out[slot] = ext
        pre = conv(ext, pmain[0:TAPS, cols], pmain[TAPS : TAPS + 1, cols], links)
        pre_out[slot] = pre
        for c in x_puts(j, slot):
            c.start()
        act = silu(pre).astype(BF16)
        x_act[:, cols] = act
        heavy = (act.astype(F32) * widen(weight_ref[...], j)).astype(BF16)
        update[:, cols] = dot(bc[:, :STATE], heavy, (0, 0))
        keep_row[:, cols] = widen(keep8, j)
        for k in range(4):
            forward_slot(4 * j + k)

    gather_forward(1)
    gather_second(1)
    pl.loop(0, 3)(x_tile)
    gather_forward(2)
    gather_second(2)
    pl.loop(3, TILES)(x_tile)
    for slot in range(2):
        for c in x_puts(TILES - 2 + slot, slot):
            c.wait()

    halves = [(slice(0, HALF), slice(0, HALF)), (slice(HALF, BLOCK), slice(0, BLOCK))]

    def decay_of(h, column, rows, cols):
        return jnp.exp2(column[rows] - cum_t[h, :, cols] + barred[rows, cols])

    def intra_forward(p):
        cols = pair_of(p)
        x = x_act[:, cols]
        x2 = [only(x, True), only(x, False)]
        columns = [head_column(cum2, 2 * p + k) for k in (0, 1)]
        for rows, js in halves:
            mix = [
                (scores[rows, js] * (decay_of(2 * p + k, columns[k], rows, js) * step_t[2 * p + k, :, js])).astype(BF16)
                for k in (0, 1)
            ]
            y[rows, cols] = dot(jnp.concatenate(mix, 1), jnp.concatenate([v[js] for v in x2], 0))

    def scan_pairs(first, last):
        @pl.loop(first, last)
        def _(i):
            forward_slot(4 * TILES + 2 * i)
            intra_forward(i)
            forward_slot(4 * TILES + 2 * i + 1)

    def gate_tile(j, slot):
        gate_in[:, tile_of(j)] = dot(normed[pl.ds(HALO, BLOCK)], held(slot))

    def out_tile(j, slot):
        work[:, tile_of(j)] = dot(cot[...], held(slot))

    def tile_step(m, j, use):
        slot = lax.rem(j, 2)

        @pl.when(j + 1 < TILES)
        def _():
            load(m, j + 1, 1 - slot).start()

        load(m, j, slot).wait()
        use(j, slot)

    scan_pairs(0, 8)
    gather_last(1)
    scan_pairs(8, 12)
    gather_last(2)
    gather_done(1)
    load(1, 0, 0).start()

    @pl.loop(0, TILES)
    def _(j):
        for k in range(2):
            i = 12 + 2 * j + k
            forward_slot(4 * TILES + 2 * i)
            intra_forward(i)
            forward_slot(4 * TILES + 2 * i + 1)
        tile_step(1, j, gate_tile)

    base = 4 * TILES + 2 * PAIRS
    gather_done(2)
    load(2, 0, 0).start()

    @pl.loop(0, TILES)
    def _(j):
        forward_slot(base + j)
        tile_step(2, j, out_tile)

    base = base + TILES

    load(2, 0, 1).start()
    load(1, 0, 0).start()
    row_acc[...] = jnp.zeros_like(row_acc)

    @pl.loop(0, TILES)
    def _(j):
        @pl.loop(0, TILE // CHUNK)
        def _(k):
            c = j * (TILE // CHUNK) + k

            @pl.when(c + FORWARD_LAG * t >= base)
            def _():
                chain(True, c, update, state, f_out, f_in, f_send, f_recv)

        cols = tile_of(j)
        low = state[:, cols].astype(BF16)
        state_low[:, cols] = low
        carried = dot(bc[:, STATE:], low)
        value = y[:, cols] + carried * widen(enter_ref[...], j) + pmain[6:7, cols] * x_act[:, cols].astype(F32)
        y[:, cols] = value
        gated = value * silu(gate_in[:, cols])
        row_acc[...] += jnp.broadcast_to(jnp.sum(gated * gated, axis=1, keepdims=True), (BLOCK, LANES))

    gate_inv = lax.rsqrt(row_acc[:, :1] / DI + epsilon)
    row_acc[...] = jnp.zeros_like(row_acc)

    @pl.loop(0, TILES)
    def _(j):
        cols = tile_of(j)
        gated = y[:, cols] * silu(gate_in[:, cols])
        hat = gated * gate_inv
        gate_gain = pmain[5:6, cols]
        gate_out[:, cols] = (hat * gate_gain).astype(BF16)
        grad = work[:, cols]
        vec_gate[:, cols] = jnp.broadcast_to(jnp.sum(grad * hat, axis=0, keepdims=True), (8, TILE))
        dn = grad * gate_gain
        work[:, cols] = dn
        row_acc[...] += jnp.broadcast_to(jnp.sum(dn * gated, axis=1, keepdims=True), (BLOCK, LANES))

    inner = row_acc[:, :1] / DI * gate_inv * gate_inv * gate_inv
    acc_c[...] = jnp.zeros_like(acc_c)
    acc_heads[...] = jnp.zeros_like(acc_heads)

    @pl.loop(0, TILES)
    def _(j):
        cols = tile_of(j)
        gate, value = gate_in[:, cols], y[:, cols]
        s = sigmoid(gate)
        act = gate * s
        grad_gated = gate_inv * work[:, cols] - value * act * inner
        grad = (grad_gated * act).astype(BF16)
        dy[:, cols] = grad
        gate_grad[:, cols] = (grad_gated * value * (s * (1.0 + gate * (1.0 - s)))).astype(BF16)
        grad = grad.astype(F32)
        carried_grad = (grad * widen(enter_ref[...], j)).astype(BF16)
        low = state_low[:, cols]
        grad_add[:, cols] = dot(bc[:, STATE:], carried_grad, (0, 0))
        acc_c[...] += dot(carried_grad, low, (1, 1))
        acc_heads[0] += by_head(grad * dot(bc[:, STATE:], low), j)

    rows_acc[...] = jnp.zeros_like(rows_acc)
    gs[...] = jnp.zeros_like(gs)
    acc[...] = jnp.zeros_like(acc)
    mixed_acc[...] = jnp.zeros_like(mixed_acc)

    def intra_backward(p):
        cols = pair_of(p)
        x, grad = x_act[:, cols], dy[:, cols]
        grad2 = [only(grad, True), only(grad, False)]
        columns = [head_column(cum2, 2 * p + k) for k in (0, 1)]
        lane = iota((HALF, LANES), 1)
        parts = []
        q_rows = [[], []]
        for rows, js in halves:
            mixes = []
            gs_sum = gs[rows, js]
            pulls = jnp.zeros((HALF, LANES), F32)
            for k in (0, 1):
                h = 2 * p + k
                decay = decay_of(h, columns[k], rows, js)
                decay_step = decay * step_t[h, :, js]
                mixes.append((scores[rows, js] * decay_step).astype(BF16))
                grad_mix = dot(grad2[k][rows], x[js], (1, 1))
                gs_sum = gs_sum + grad_mix * decay_step
                q = grad_mix * scores[rows, js] * decay
                q_rows[k].append(jnp.sum(q, axis=0, keepdims=True))
                pull = jnp.sum(q * step_t[h, :, js], axis=1, keepdims=True)
                pulls = jnp.where(lane == h, pull, pulls)
            gs[rows, js] = gs_sum
            rows_acc[rows] += pulls
            parts.append(dot(jnp.concatenate(mixes, 0), jnp.concatenate([v[rows] for v in grad2], 0), (0, 0)))
        grad_x[pl.ds(0, HALF), cols] = parts[0] + parts[1][:HALF]
        grad_x[pl.ds(HALF, HALF), cols] = parts[1][HALF:]
        for k in (0, 1):
            first, second = q_rows[k]
            q_t[2 * p + k, :, 0:HALF] = first + second[:, :HALF]
            q_t[2 * p + k, :, HALF:BLOCK] = second[:, HALF:]

    def put(ref, j, slot):
        return [
            pltpu.make_async_copy(
                staged.at[slot, pl.ds(i * ROWS, ROWS)], ref.at[0, lo, y_, c, :, tile_of(j)], put_sem.at[slot, i]
            )
            for i, (lo, y_, c) in enumerate((lo, y_, c) for lo in range(2) for y_ in range(4) for c in range(2))
        ]

    def put_tile(ref, j, slot, lhs, grad):
        @pl.when(j >= 1)
        def _():
            for c in put(ref, j, slot):
                c.wait()

        staged[slot] = dot(lhs[...], grad).astype(BF16)
        for c in put(ref, j, slot):
            c.start()

    @pl.loop(0, PAIRS)
    def _(i):
        backward_slot(2 * i)
        intra_backward(i)
        backward_slot(2 * i + 1)
        j = lax.div(i, 4)
        cols = tile_of(j)

        @pl.when(lax.rem(i, 4) == 0)
        def _():
            put_tile(grad_out, j, 0, cot_t, gate_out[:, cols])

        @pl.when(lax.rem(i, 4) == 1)
        def _():
            put_tile(grad_gate, j, 1, normed_t, gate_grad[:, cols])

        @pl.when(lax.rem(i, 4) == 2)
        def _():
            load(2, j, 1).wait()
            mixed_acc[...] += dot(gate_out[:, cols], held(1), (1, 1))

            @pl.when(j + 1 < TILES)
            def _():
                load(2, j + 1, 1).start()

        @pl.when(lax.rem(i, 4) == 3)
        def _():
            load(1, j, 0).wait()
            acc[...] += dot(gate_grad[:, cols], held(0), (1, 1))

            @pl.when(j + 1 < TILES)
            def _():
                load(1, j + 1, 0).start()

    gs_low = gs[...].astype(BF16)
    grad_bc[:, STATE:] = acc_c[...] + dot(gs_low, bc[:, :STATE])
    acc_c[...] = dot(gs_low, bc[:, STATE:], (0, 0))

    @pl.loop(0, TILES)
    def _(j):
        @pl.loop(0, TILE // CHUNK)
        def _(k):
            c = j * (TILE // CHUNK) + k

            @pl.when(c + BACKWARD_LAG * (7 - t) >= 2 * PAIRS)
            def _():
                chain(False, c, grad_add, grad_state, b_out, b_in, b_send, b_recv)

        cols = tile_of(j)
        wide = widen(weight_ref[...], j)
        grad_update = grad_state[:, cols].astype(BF16)
        spread_grad = dot(bc[:, :STATE], grad_update)
        x, grad = x_act[:, cols].astype(F32), dy[:, cols].astype(F32)
        grad_x[:, cols] += wide * spread_grad + pmain[6:7, cols] * grad
        acc_heads[1] += by_head(x * spread_grad, j)
        acc_c[...] += dot((x * wide).astype(BF16), grad_update, (1, 1))
        kept = jnp.sum(grad_state[:, cols] * state[:, cols], axis=0, keepdims=True)
        skip = jnp.sum(x * grad, axis=0, keepdims=True)
        row = iota((8, TILE), 0)
        both = jnp.where(row == 0, kept, jnp.where(row == 1, skip, 0.0))
        acc_heads[2, 0:8] += by_head(both, j)

    grad_bc[:, :STATE] = acc_c[...]
    grad_weight = acc_heads[1]
    none = jnp.zeros((LANES - HEADS, BLOCK), F32)
    step = jnp.concatenate([step_t[h] for h in range(HEADS)] + [none], 0).T
    q = jnp.concatenate([q_t[h] for h in range(HEADS)] + [none], 0).T
    weight_pull = grad_weight * weight_ref[...]
    grad_end = jnp.sum(weight_pull, axis=0, keepdims=True) + acc_heads[2, 0:1] * keep
    grad_cum = rows_acc[...] - step * q + enter_ref[...] * acc_heads[0] - weight_pull
    grad_cum = grad_cum + jnp.where(iota((BLOCK, LANES), 0) == BLOCK - 1, grad_end, 0.0)
    upper = (iota((BLOCK, BLOCK), 0) <= iota((BLOCK, BLOCK), 1)).astype(F32)
    grad_log = dot(upper, grad_cum, precision=lax.Precision.HIGHEST)
    grad_step = q + grad_weight * tail + rate * grad_log
    grad_in = grad_step * sigmoid(step_in[...])
    grad_step_in[...] = grad_in
    row = iota((8, LANES), 0)
    heads = jnp.where(row == 5, jnp.sum(grad_in, axis=0, keepdims=True), 0.0)
    heads = jnp.where(row == 6, rate * jnp.sum(grad_log * step, axis=0, keepdims=True), heads)
    vec_heads[...] = jnp.where(row == 7, acc_heads[2, 1:2], heads)
    mixed[...] = (hidden[...].astype(F32) + mixed_acc[...]).astype(BF16)

    for u in everything:
        for step in (0, 1):
            for phase in (0, 1):
                await_step(u, phase, early(u), step, phase, g_send)
    for m in range(4):
        for u in units_with(m):
            await_partner(u, pl.ds(m % 3, 1), m % 3, core_send)
            for step in (0, 1):
                await_step(u, 2, pl.ds(m % 3, 1), step, 2 + m % 3, g_send)
    for slot, ref in ((0, grad_out), (1, grad_gate)):
        for c in put(ref, TILES - 1, slot):
            c.wait()
    for by, ends, outgoing, incoming, send, recv in (
        (1, 7, f_out, f_in, f_send, f_recv),
        (7, 0, b_out, b_in, b_send, b_recv),
    ):

        @pl.when(t != ends)
        def _(by=by, outgoing=outgoing, incoming=incoming, send=send, recv=recv):
            @pl.loop(0, CHUNKS)
            def _(c):
                pltpu.make_async_remote_copy(
                    src_ref=outgoing.at[:, chunk_of(c)], dst_ref=incoming.at[:, chunk_of(c)], send_sem=send.at[c],
                    recv_sem=recv.at[c], device_id=tensor_peer(by), device_id_type=MESH,
                ).wait_send()


def mid(*args):
    vmem = pl.BlockSpec(memory_space=VMEM)
    anywhere = pl.BlockSpec(memory_space=pl.ANY)
    wide, heads, square = (BLOCK, DI), (BLOCK, LANES), (BLOCK, BLOCK)
    turned, own_state = (HEADS, 1, BLOCK), (STATE, DI)
    blocks = (1, 2, 4, 2, ROWS, DI)
    shapes = [
        ((BLOCK, D), BF16), ((8, DI), F32), ((8, 8 * LANES), F32), ((D, BLOCK), BF16), ((EXT, SMALL), F32), (square, F32), (square, F32), (heads, F32),
        ((D, SMALL), BF16), ((BLOCK, D), F32), (wide, F32), ((8, DI), F32), ((8, LANES), F32),
        ((EXT, DI), F32), (wide, F32), (blocks, BF16), (blocks, BF16), ((3,) + blocks[1:], BF16),
    ]
    scratch = [
        ((1, 2, 4, 2, SMALL_ROWS, 8 * LANES), BF16), ((HALO, D), BF16), ((EXT, D), BF16), ((2, 2, 4, 2, ROWS, TILE), BF16), ((2, EXT, TILE), F32), ((2, BLOCK, TILE), F32), ((2, D, TILE), BF16),
        (wide, BF16), ((BLOCK, 2 * STATE), BF16), (square, F32), (wide, F32), (wide, F32), (wide, F32), (wide, BF16),
        (wide, BF16), (wide, BF16), (own_state, F32), (own_state, F32), (own_state, F32), (own_state, BF16),
        (own_state, F32), ((8, DI), F32), (own_state, BF16), (own_state, BF16), (own_state, BF16), (own_state, BF16),
        ((D, BLOCK), BF16), ((BLOCK, D), F32),
        (square, F32), (heads, F32), (turned, F32), (turned, F32), (heads, F32), (heads, F32), (heads, F32),
        (heads, F32), (turned, F32), (square, F32), (heads, F32), ((3,) + heads, F32), (heads, F32),
    ]
    return pl.pallas_call(
        mid_kernel,
        name="scan_and_gate",
        out_shape=[jax.ShapeDtypeStruct(*s) for s in shapes],
        in_specs=[vmem] * 5 + [anywhere] * 4,
        out_specs=[vmem] * 13 + [anywhere] * 5,
        scratch_shapes=[VMEM(*s) for s in scratch]
        + [pltpu.SemaphoreType.DMA((2,)), pltpu.SemaphoreType.DMA((2, 16)), pltpu.SemaphoreType.DMA((2, 2))]
        + [pltpu.SemaphoreType.DMA((CHUNKS,))] * 4
        + [pltpu.SemaphoreType.DMA((len(UNITS), 5, 2))] * 2
        + [pltpu.SemaphoreType.DMA((len(UNITS), 3))] * 2
        + [pltpu.SemaphoreType.DMA(s) for s in ((4,), (2,), (2, 7), (2, 7))],
        compiler_params=pltpu.CompilerParams(
            collective_id=1, has_side_effects=True, vmem_limit_bytes=60 * 2**20
        ),
    )(*args)


VEC = (8, 8 * WIDTH + 384)
VEC_STEPS = 7
MATS = (2, 1, 0)


def spread(whole):
    return (2 if 2 in whole else 1, 4 if 1 in whole else 1, (4 if 0 in whole else 1) * (2 if 2 in whole else 1))


def region_shape(u, phase, rows):
    lo, y, cols = spread(axes_of(u)[:phase])
    return (lo, y, rows, cols * WIDTHS[UNITS[u][0]])


def back_kernel(*refs):
    refs = list(refs)

    def take(n):
        got = refs[:n]
        del refs[:n]
        return got

    (normed_t, raw_ext, state_pre, grad_bc, grad_step_in, w_small, acc_in, pmain, phead, doc_col, hidden, cot, gain,
     vec_gate, vec_heads, x_ext, x_pre, grad_x, grad_gate, grad_out, full) = take(21)
    grad_main, grad_small, out_main, out_small, grad_hidden, vec_out = take(6)
    outs = (out_main, out_small)
    units = len(UNITS)
    other = take(2)
    half_buf = [take(3) for _ in range(units)]
    full_buf = [take(3) for _ in range(units)]
    own = take(units)
    (ext_in, pre_in, grad_in, first_grad, first_pre, first_out, after, w_in, staged, raw_x, acc, small_acc,
     small_out, vec_acc, vec_in) = take(15)
    (stream_sem, first_sem, halo_sem, w_sem, put_sem, small_sem, own_sem, vec_send, vec_recv, send, recv, core_send,
     core_recv) = take(13)
    at, core = coordinates()
    t = lax.axis_index("tensor")
    everything = range(units)

    def stream(j, slot):
        cols = tile_of(j)
        return [
            pltpu.make_async_copy(src.at[:, cols], dst.at[slot], stream_sem.at[i, slot])
            for i, (src, dst) in enumerate(((x_ext, ext_in), (x_pre, pre_in), (grad_x, grad_in)))
        ]

    firsts = [
        pltpu.make_async_copy(src.at[pl.ds(0, 8)], dst, first_sem.at[i])
        for i, (src, dst) in enumerate(((grad_x, first_grad), (x_pre, first_pre)))
    ]
    for c in firsts + stream(0, 0):
        c.start()
    greet(at, core, [device(moved(at, axis, 2), core) for axis in AXES] + [tensor_peer(1), tensor_peer(7)])

    def source_of(u, m):
        return grad_small if UNITS[u][0] else (grad_main, grad_gate, grad_out)[m]

    def units_of(m):
        return [u for u in everything if m == 0 or UNITS[u][0] == 0]

    def index_of(u, m):
        return 0 if UNITS[u][0] else m

    def part_of(ref, u, mats, where, whole, half=None):
        which, first, rows = UNITS[u][0], UNITS[u][1], 32
        if half is not None:
            first, rows = first + half * 16, 16
        return [ref.at[mats, lo, y, pl.ds(first, rows), cols] for lo, y, cols in pieces(where, whole, WIDTHS[which])]

    def place(u, by):
        return moved(at, axes_of(u)[2], by) if by else at

    groups = [[2], [1, -1], [0]]

    def to_partner(m):
        for g, group in enumerate(groups):
            for u in units_of(m):
                for by in group:
                    whole = axes_of(u)[:2]
                    for src, dst in zip(
                        region(source_of(u, m), u, 1 - core, pl.ds(0, 1), place(u, by), whole),
                        part_of(other[UNITS[u][0]], u, pl.ds(index_of(u, m), 1), place(u, by), whole),
                    ):
                        pltpu.make_async_remote_copy(
                            src_ref=src, dst_ref=dst, send_sem=core_send.at[u, m], recv_sem=core_recv.at[u, m, g],
                            device_id=device(at, 1 - core), device_id_type=MESH,
                        ).start()

    def await_partner(u, m, g):
        rows = 2 * len(groups[g])
        part = other[UNITS[u][0]].at[pl.ds(0, 1), pl.ds(0, 1), pl.ds(0, rows), pl.ds(0, 32)]
        pltpu.make_async_copy(part, part, core_recv.at[u, m, g]).wait()

    def own_loads(u, m, g):
        copies = []
        for slot, by in enumerate(groups[g]):
            parts = region(source_of(u, m), u, core, 0, place(u, by), axes_of(u)[:2])
            width = own[u].shape[-1] // len(parts)
            for i, src in enumerate(parts):
                copies.append(
                    pltpu.make_async_copy(src, own[u].at[slot, :, :, :, pl.ds(i * width, width)], own_sem.at[u, slot, i])
                )
        return copies

    def prefetch(m, g):
        for u in units_of(m):
            for c in own_loads(u, m, g):
                c.start()

    def add(u, phase, mats, where, half, terms, result=None):
        which, first, rows = UNITS[u][0], UNITS[u][1], 32
        if half is not None:
            first, rows = first + half * 16, 16
        whole = axes_of(u)[:phase]
        n_lo, n_y, _ = spread(whole)
        for i, (lo, y, cols) in enumerate(pieces(where, whole, WIDTHS[which])):

            @pl.loop(0, len(mats) * n_lo * n_y)
            def _(k, i=i, lo=lo, y=y, cols=cols):
                mat = mats[0] if len(mats) == 1 else lax.div(k, n_lo * n_y)
                a, b = lax.rem(lax.div(k, n_y), n_lo), lax.rem(k, n_y)
                here = (mat, lo.start + a, y.start + b, pl.ds(first, rows), cols)
                total = other[which][here].astype(F32)
                for term in terms:
                    total = total + term(mat, i, a, b).astype(F32)
                if result is None:
                    other[which][here] = total.astype(BF16)
                else:
                    result[mat, pl.ds(first, rows), :] = total

    def width_of(u, phase, ref):
        whole = axes_of(u)[:phase]
        return ref.shape[-1] // (2 if 2 in whole and 0 not in whole else 1)

    def from_own(u, slot, half=None):
        width = width_of(u, 2, own[u])
        rows = pl.ds(0, 32) if half is None else pl.ds(half * 16, 16)
        return lambda mat, i, a, b: own[u][slot, a, b, rows, pl.ds(i * width, width)]

    def from_buf(ref, side, u, phase):
        width = width_of(u, phase, ref)
        return lambda mat, i, a, b: ref[side, mat, a, b, :, pl.ds(i * width, width)]

    def mats_of(u, m):
        return pl.ds(index_of(u, m), 1)

    def send_step(u, phase, m, step):
        axes = axes_of(u)
        whole, axis = axes[:phase], axes[phase]
        index = 3 * index_of(u, m) + phase
        buf = half_buf[u][phase] if step == 0 else full_buf[u][phase]
        for side, by in ((0, 1), (1, -1)):
            where = moved(at, axis, 2 if step == 0 else by)
            sources = part_of(other[UNITS[u][0]], u, mats_of(u, m), where, whole, side if step == 0 else None)
            width = buf.shape[-1] // len(sources)
            for i, src in enumerate(sources):
                pltpu.make_async_remote_copy(
                    src_ref=src, dst_ref=buf.at[side, mats_of(u, m), :, :, :, pl.ds(i * width, width)],
                    send_sem=send.at[u, index, step], recv_sem=recv.at[u, index, step],
                    device_id=device(moved(at, axis, by), core), device_id_type=MESH,
                ).start()

    def await_step(u, phase, m, step, sem):
        index = 3 * index_of(u, m) + phase
        buf = half_buf[u][phase] if step == 0 else full_buf[u][phase]
        part = buf.at[:, mats_of(u, m)]
        pltpu.make_async_copy(part, part, sem.at[u, index, step]).wait()

    def stage(m, g):
        for u in units_of(m):
            for c in own_loads(u, m, g):
                c.wait()
            await_partner(u, m, g)
            mats = [index_of(u, m)]
            if g == 0:
                add(u, 2, mats, place(u, 2), None, [from_own(u, 0)])
                send_step(u, 2, m, 0)
            elif g == 1:
                await_step(u, 2, m, 0, recv)
                for side, by in ((0, 1), (1, -1)):
                    halves = [from_own(u, side, side), from_buf(half_buf[u][2], side, u, 2)]
                    add(u, 2, mats, place(u, by), side, halves)
                    add(u, 2, mats, place(u, by), 1 - side, [from_own(u, side, 1 - side)])
                send_step(u, 2, m, 1)
            else:
                await_step(u, 2, m, 1, recv)
                arrived = [from_buf(full_buf[u][2], side, u, 2) for side in (0, 1)]
                add(u, 2, mats, at, None, [from_own(u, 0)] + arrived)

    def later(m, phase, step):
        for u in units_of(m):
            axis, mats = axes_of(u)[phase], [index_of(u, m)]
            if step == 1:
                await_step(u, phase, m, 0, recv)
                for side, by in ((0, 1), (1, -1)):
                    add(u, phase, mats, moved(at, axis, by), side, [from_buf(half_buf[u][phase], side, u, phase)])
            elif step == 2:
                await_step(u, phase, m, 1, recv)
                arrived = [from_buf(full_buf[u][phase], side, u, phase) for side in (0, 1)]
                add(u, phase, mats, at, None, arrived, None if phase else outs[UNITS[u][0]])
            if step < 2:
                send_step(u, phase, m, step)

    def vec_copy(k):
        (x, y, z) = at
        flip = lambda v: v + 1 - 2 * lax.rem(v, 2)
        to = [
            device(at, 1 - core),
            device((flip(x), y, z), core),
            device((x, flip(y), z), core),
            device((x, y, flip(z)), core),
            device(moved(at, 0, 2), core),
            device(moved(at, 1, 2), core),
            device(moved(at, 2, 2), core),
        ][k]
        return pltpu.make_async_remote_copy(
            src_ref=vec_acc.at[k], dst_ref=vec_in.at[k], send_sem=vec_send.at[k], recv_sem=vec_recv.at[k],
            device_id=to, device_id_type=MESH,
        )

    def vec_step(k):
        if k:
            vec_copy(k - 1).wait_recv()
            vec_acc[k] = vec_acc[k - 1] + vec_in[k - 1]
        if k < VEC_STEPS:
            vec_copy(k).start()
        else:
            vec_out[...] = vec_acc[VEC_STEPS]

    prefetch(2, 0)
    to_partner(2)
    to_partner(1)
    for c in firsts:
        c.wait()
    first_out[:, :DI] = first_grad[...] * silu_slope(first_pre[...])
    first_out[:, DI:] = grad_bc[:8] * silu_slope(state_pre[:8])

    def halo_copy():
        return pltpu.make_async_remote_copy(
            src_ref=first_out, dst_ref=after, send_sem=halo_sem.at[0], recv_sem=halo_sem.at[1],
            device_id=tensor_peer(7), device_id_type=MESH,
        )

    @pl.when(t > 0)
    def _():
        halo_copy().start()

    docs = doc_col[...]
    links = [None] + [conv_links(docs, o, BLOCK + 8) for o in range(1, TAPS)]
    params = small_params(phead[...])
    vec = vec_acc.at[0]
    vec[...] = jnp.zeros(VEC, F32)

    stage(2, 0)
    prefetch(1, 0)

    @pl.when(t < 7)
    def _():
        halo_copy().wait_recv()

    @pl.when(t == 7)
    def _():
        after[...] = jnp.zeros_like(after)

    def conv_back(grad, grad_after, ext, taps):
        grad_ext = jnp.concatenate([grad, grad_after], 0)
        total = taps[TAPS - 1 : TAPS] * grad
        rows = [None] * TAPS
        rows[TAPS - 1] = jnp.sum(grad * ext[HALO:], axis=0, keepdims=True)
        for offset in range(1, TAPS):
            masked = grad_ext * links[offset]
            rows[TAPS - 1 - offset] = jnp.sum(masked[:BLOCK] * ext[HALO - offset : EXT - offset], axis=0, keepdims=True)
            total = total + taps[TAPS - 1 - offset : TAPS - offset] * masked[offset : offset + BLOCK]
        return total, rows + [jnp.sum(grad, axis=0, keepdims=True)]

    flat_main = [(lo, y, c) for lo in range(2) for y in range(4) for c in range(2)]

    def put(j, slot):
        cols = tile_of(j)
        return [
            pltpu.make_async_copy(
                staged.at[slot, pl.ds(i * ROWS, ROWS)], grad_main.at[0, lo, y, c, :, cols], put_sem.at[slot, i]
            )
            for i, (lo, y, c) in enumerate(flat_main)
        ]

    def x_tiles(first, last):
        @pl.loop(first, last)
        def _(j):
            slot = lax.rem(j, 2)
            cols = tile_of(j)

            @pl.when(j + 1 < TILES)
            def _():
                for c in stream(j + 1, 1 - slot):
                    c.start()

            for c in stream(j, slot):
                c.wait()
            grad = grad_in[slot] * silu_slope(pre_in[slot])
            total, rows = conv_back(grad, after[:, cols], ext_in[slot], pmain[0:TAPS, cols])
            for i, row in enumerate(rows):
                vec[i : i + 1, cols] = row
            total = total.astype(BF16)
            raw_x[:, cols] = total

            @pl.when(j >= 2)
            def _():
                for c in put(j, slot):
                    c.wait()

            staged[slot] = dot(normed_t[...], total).astype(BF16)
            for c in put(j, slot):
                c.start()

    def small_part():
        grad = grad_bc[...] * silu_slope(state_pre[...])
        total, rows = conv_back(grad, after[:, DI:], raw_ext[:, :256], params[:TAPS, :256])
        for i, row in enumerate(rows):
            vec[i : i + 1, DI : DI + 256] = row
        raw = jnp.concatenate([total.astype(BF16), grad_step_in[...].astype(BF16)], 1)
        acc[...] = acc_in[...] + dot(raw, w_small[...], (1, 1))
        small_acc[...] = dot(normed_t[...], raw).astype(BF16)
        packed = jnp.zeros((512, 8 * LANES), F32)
        for r in range(3):
            rows_r = jnp.concatenate([small_acc[pl.ds(d * 96 + r * 32, 32)] for d in range(16)], 0)
            packed = packed + dot(rows_r, small_map(r), (1, 1))
        small_out[...] = packed.astype(BF16)
        for c in small_puts:
            c.start()

    small_puts = [
        pltpu.make_async_copy(small_out.at[pl.ds(i * 32, 32)], grad_small.at[0, lo, y, c], small_sem.at[i])
        for i, (lo, y, c) in enumerate(flat_main)
    ]

    def input_tiles(first, last):
        @pl.loop(first, last)
        def _(k):
            slot = lax.rem(k, 2)

            def load(n, into):
                return pltpu.make_async_copy(full.at[0, :, tile_of(n)], w_in.at[into], w_sem.at[into])

            @pl.when(k + 1 < TILES)
            def _():
                load(k + 1, 1 - slot).start()

            load(k, slot).wait()
            acc[...] += dot(raw_x[:, tile_of(k)], w_in[slot], (1, 1))

    def input_grad():
        value = hidden[...].astype(F32)
        inv = lax.rsqrt(jnp.mean(value * value, axis=1, keepdims=True) + epsilon)
        rows = value * inv
        grad = acc[...]
        vec[5:6, 0:DI] = vec_gate[0:1, :]
        vec[6:7, 0:D] = jnp.sum(grad * rows, axis=0, keepdims=True)
        vec[5:8, DI + 256 :] = vec_heads[5:8, :]
        dn = grad * gain[...]
        mean = jnp.mean(dn * rows, axis=1, keepdims=True)
        grad_hidden[...] = cot[...].astype(F32) + inv * dn - rows * inv * mean

    small_part()
    x_tiles(0, 1)
    stage(1, 0)
    prefetch(2, 1)
    x_tiles(1, 3)
    stage(2, 1)
    prefetch(1, 1)
    x_tiles(3, 5)
    stage(1, 1)
    prefetch(2, 2)
    x_tiles(5, 6)
    pltpu.make_async_copy(full.at[0, :, tile_of(0)], w_in.at[0], w_sem.at[0]).start()
    for slot in range(2):
        for c in put(TILES - 2 + slot, slot):
            c.wait()
    for c in small_puts:
        c.wait()
    to_partner(0)
    input_tiles(0, 3)
    stage(2, 2)
    prefetch(0, 0)
    later(2, 1, 0)
    input_tiles(3, 6)
    stage(0, 0)
    prefetch(1, 2)
    later(2, 1, 1)
    input_grad()
    vec_step(0)
    stage(1, 2)
    prefetch(0, 1)
    later(1, 1, 0)
    later(2, 1, 2)
    later(2, 0, 0)
    vec_step(1)
    stage(0, 1)
    prefetch(0, 2)
    later(1, 1, 1)
    later(2, 0, 1)
    vec_step(2)
    later(1, 1, 2)
    later(1, 0, 0)
    later(2, 0, 2)
    vec_step(3)
    later(1, 0, 1)
    stage(0, 2)
    later(0, 1, 0)
    vec_step(4)
    later(1, 0, 2)
    later(0, 1, 1)
    vec_step(5)
    later(0, 1, 2)
    later(0, 0, 0)
    vec_step(6)
    later(0, 0, 1)
    vec_step(7)
    later(0, 0, 2)
    for m in MATS:
        for u in units_of(m):
            part = other[UNITS[u][0]].at[pl.ds(0, 1), :, :, pl.ds(0, 32)]
            pltpu.make_async_copy(part, part, core_send.at[u, m]).wait()
            for phase in range(3):
                for step in (0, 1):
                    await_step(u, phase, m, step, send)
    for k in range(VEC_STEPS):
        vec_copy(k).wait_send()

    @pl.when(t > 0)
    def _():
        halo_copy().wait_send()


def back(*args):
    vmem = pl.BlockSpec(memory_space=VMEM)
    anywhere = pl.BlockSpec(memory_space=pl.ANY)
    units = range(len(UNITS))
    n = len(UNITS)
    held = [(3, 2, 4, ROWS, 8 * WIDTH), (1, 2, 4, SMALL_ROWS, 8 * SMALL_WIDTH)]
    landing = [(2, STACK[UNITS[u][0]]) + region_shape(u, p, rows) for rows in (16, 32) for u in units for p in range(3)]
    return pl.pallas_call(
        back_kernel,
        name="project_back",
        out_shape=[
            jax.ShapeDtypeStruct((1, 2, 4, 2, ROWS, DI), BF16),
            jax.ShapeDtypeStruct((1, 2, 4, 2, SMALL_ROWS, 8 * LANES), BF16),
            jax.ShapeDtypeStruct((3, ROWS, WIDTH), F32),
            jax.ShapeDtypeStruct((1, SMALL_ROWS, SMALL_WIDTH), F32),
            jax.ShapeDtypeStruct((BLOCK, D), F32),
            jax.ShapeDtypeStruct(VEC, F32),
        ],
        in_specs=[vmem] * 15 + [anywhere] * 6,
        out_specs=[anywhere, anywhere, vmem, vmem, vmem, vmem],
        scratch_shapes=[VMEM(s, BF16) for s in held + landing]
        + [VMEM((2,) + region_shape(u, 2, 32), BF16) for u in units]
        + [
            VMEM((2, EXT, TILE), F32), VMEM((2, BLOCK, TILE), F32), VMEM((2, BLOCK, TILE), F32),
            VMEM((8, DI), F32), VMEM((8, DI), F32), VMEM((8, DI + 256), F32), VMEM((8, DI + 256), F32),
            VMEM((2, D, TILE), BF16), VMEM((2, D, TILE), BF16), VMEM((BLOCK, DI), BF16),
            VMEM((BLOCK, D), F32), VMEM((D, SMALL), BF16), VMEM((512, 8 * LANES), BF16),
            VMEM((VEC_STEPS + 1,) + VEC, F32), VMEM((VEC_STEPS,) + VEC, F32),
        ]
        + [
            pltpu.SemaphoreType.DMA(s)
            for s in (
                (3, 2), (2,), (2,), (2,), (2, 16), (16,), (n, 2, 2), (VEC_STEPS,), (VEC_STEPS,), (n, 9, 2), (n, 9, 2),
                (n, 3), (n, 3, 3),
            )
        ],
        compiler_params=pltpu.CompilerParams(collective_id=3, has_side_effects=True, vmem_limit_bytes=62 * 2**20),
    )(*args)


def per_device(
    hidden,
    doc_ids,
    norm_gain,
    main_proj,
    step_proj,
    state_proj,
    conv_main,
    conv_main_bias,
    conv_state,
    conv_state_bias,
    step_bias,
    decay_log,
    skip_gain,
    gate_gain,
    out_proj,
    cotangent,
):
    shards, small, pmain, phead, doc_col, doc_row, gain = pack(
        main_proj, out_proj, state_proj, step_proj, conv_main, conv_main_bias, conv_state, conv_state_bias, step_bias,
        decay_log, skip_gain, gate_gain, norm_gain, doc_ids,
    )
    (mixed, pmain, phead, normed_t, raw, state_pre, grad_bc, grad_step_in, w_small, acc, grad_x, vec_gate, vec_heads,
     x_ext, x_pre, grad_out, grad_gate, full) = mid(
        hidden, gain, doc_col, doc_row, cotangent, shards, small, pmain, phead
    )
    _, _, own_main, own_small, grad_hidden, vec = back(
        normed_t, raw, state_pre, grad_bc, grad_step_in, w_small, acc, pmain, phead, doc_col, hidden, cotangent,
        gain, vec_gate, vec_heads, x_ext, x_pre, grad_x, grad_gate, grad_out, full.reshape(3, D, DI),
    )
    return (mixed, grad_hidden, *finish(own_main, own_small, vec))


def solution(mesh):
    placed = (
        P(("dp", "tensor"), None),
        P("dp"),
        P(),
        P("dp", None, "tensor"),
        P("dp", "tensor"),
        P("dp", "tensor"),
        P(None, "tensor"),
        P("tensor"),
        P(None, "tensor"),
        P("tensor"),
        P("tensor"),
        P("tensor"),
        P("tensor"),
        P("tensor"),
        P("dp", "tensor"),
        P(("dp", "tensor"), None),
    )
    return jax.shard_map(
        per_device,
        mesh=mesh,
        in_specs=placed,
        out_specs=(
            P(("dp", "tensor"), None),
            P(("dp", "tensor"), None),
            P(),
            P("dp", None, "tensor"),
            P("dp", "tensor"),
            P("dp", "tensor"),
            P(None, "tensor"),
            P("tensor"),
            P(None, "tensor"),
            P("tensor"),
            P("tensor"),
            P("tensor"),
            P("tensor"),
            P("tensor"),
            P("dp", "tensor"),
        ),
        check_vma=False,
    )
```

```python
import functools

import jax
import jax.numpy as jnp
from jax import lax
from jax.experimental import pallas as pl
from jax.experimental.pallas import tpu as pltpu
from jax.sharding import PartitionSpec as P

BLOCK = 256
epsilon = 1e-05

MESH = pl.DeviceIdType.MESH
AXES = (0, 1, 2)
SIDE = 4


def coordinates():
    dp = lax.axis_index("dp")
    t = lax.axis_index("tensor")
    z = lax.div(t, 4) * 2 + lax.div(dp, 8)
    return (lax.rem(t, 4), lax.rem(lax.div(dp, 2), 4), z), lax.rem(dp, 2)


def device(at, core):
    x, y, z = at
    return (lax.rem(z, 2) * 8 + y * 2 + core, lax.div(z, 2) * 4 + x)


def moved(at, axis, by):
    return tuple(lax.rem(v + by + SIDE, SIDE) if i == axis else v for i, v in enumerate(at))


def pieces(at, whole, width):
    x, y, z = at
    lo = pl.ds(0, 2) if 2 in whole else pl.ds(lax.rem(z, 2), 1)
    row = pl.ds(0, 4) if 1 in whole else pl.ds(y, 1)
    hi = lax.div(z, 2)
    if 0 in whole and 2 in whole:
        cols = [pl.ds(0, 8 * width)]
    elif 0 in whole:
        cols = [pl.ds(pl.multiple_of(hi * 4 * width, 128), 4 * width)]
    elif 2 in whole:
        cols = [
            pl.ds(pl.multiple_of(x * width, 128), width),
            pl.ds(pl.multiple_of((4 + x) * width, 128), width),
        ]
    else:
        cols = [pl.ds(pl.multiple_of((hi * 4 + x) * width, 128), width)]
    return [(lo, row, c) for c in cols]


def greet(at, core, group):
    barrier = pltpu.get_barrier_semaphore()
    others = [device(moved(at, axis, by), core) for axis in AXES for by in (1, -1)]
    others.append(device(at, 1 - core))
    others += group
    for other in others:
        pl.semaphore_signal(barrier, inc=1, device_id=other, device_id_type=MESH)
    pl.semaphore_wait(barrier, len(others))


def tensor_peer(by):
    return (lax.axis_index("dp"), lax.rem(lax.axis_index("tensor") + by, 8))


ROWS, WIDTH, SMALL_ROWS, SMALL_WIDTH = 96, 384, 32, 128
UNITS = [(0, q * 32, q) for q in range(3)] + [(1, 0, 0)]
SUMMED = len(UNITS)
WIDTHS = [WIDTH, SMALL_WIDTH]
STACK = [3, 1]


def axes_of(u):
    return [(UNITS[u][2] + j) % 3 for j in range(3)]


def region(ref, u, core, mats, where, whole, half=None):
    which, first, rows = UNITS[u][0], UNITS[u][1], 32
    if half is not None:
        first, rows = first + half * 16, 16
    return [
        ref.at[mats, lo, row, core, pl.ds(first, rows), cols]
        for lo, row, cols in pieces(where, whole, WIDTHS[which])
    ]


def sized(ref, u, mats, blocks, halves=2):
    width = WIDTHS[UNITS[u][0]]
    cols = min(blocks, 8)
    rest = blocks // cols
    return ref.at[mats, pl.ds(0, max(rest // 4, 1)), pl.ds(0, min(rest, 4)), 0, pl.ds(0, 16 * halves), pl.ds(0, cols * width)]


def gather_ops(full, send, recv, core_send, core_recv):
    at, core = coordinates()

    def sends(u, phase, mats, step, key):
        axes = axes_of(u)
        whole, axis = axes[:phase], axes[phase]
        for kind, by in ((0, 1), (1, -1)):
            where = at if step == 0 else moved(at, axis, -by)
            for part in region(full[UNITS[u][0]], u, core, mats, where, whole, kind if step else None):
                pltpu.make_async_remote_copy(
                    src_ref=part, dst_ref=part, send_sem=send.at[u, key, step], recv_sem=recv.at[u, key, step],
                    device_id=device(moved(at, axis, by), core), device_id_type=MESH,
                ).start()

    def await_step(u, phase, mats, step, key, sem):
        part = sized(full[UNITS[u][0]], u, mats, 2 * 4**phase // (1 + step))
        pltpu.make_async_copy(part, part, sem.at[u, key, step]).wait()

    def to_partner(u, mats, bys, key):
        axes = axes_of(u)
        for by in bys:
            where = moved(at, axes[2], by) if by else at
            for part in region(full[UNITS[u][0]], u, core, mats, where, axes[:2]):
                pltpu.make_async_remote_copy(
                    src_ref=part, dst_ref=part, send_sem=core_send.at[u, key], recv_sem=core_recv.at[u, key],
                    device_id=device(at, 1 - core), device_id_type=MESH,
                ).start()

    def await_partner(u, mats, key, sem):
        part = sized(full[UNITS[u][0]], u, mats, 64)
        pltpu.make_async_copy(part, part, sem.at[u, key]).wait()

    return sends, await_step, to_partner, await_partner


MAIN_UNITS = range(3)
ALL = pl.ds(0, 3)


D, DI, HEADS, HEAD_DIM, STATE, TAPS, HALO = 1536, 3072, 48, 64, 128, 4, 16
BF16, F32 = jnp.bfloat16, jnp.float32
TILE, LANES, SMALL = 512, 128, 384
TILES = DI // TILE
LOG2E = 1.4426950408889634
EXT = HALO + BLOCK
VMEM = pltpu.VMEM


def dot(a, b, dims=(1, 0), precision=None):
    return lax.dot_general(
        a, b, ((dims[:1], dims[1:]), ((), ())), precision=precision, preferred_element_type=F32
    )


def iota(shape, dim):
    return lax.broadcasted_iota(jnp.int32, shape, dim)


def sigmoid(v):
    return 1.0 / (1.0 + jnp.exp(-v))


def silu(v):
    return v * sigmoid(v)


def silu_slope(v):
    s = sigmoid(v)
    return s * (1.0 + v * (1.0 - s))


def softplus(v):
    return jnp.maximum(v, 0.0) + jnp.log1p(jnp.exp(-jnp.abs(v)))


def split(v):
    high = v.astype(BF16)
    return high, (v - high.astype(F32)).astype(BF16)


def head_map(j):
    return (iota((LANES, TILE), 0) == j * (TILE // HEAD_DIM) + iota((LANES, TILE), 1) // HEAD_DIM).astype(BF16)


def widen(v, j):
    high, low = split(v)
    return dot(high, head_map(j)) + dot(low, head_map(j))


def by_head(v, j):
    high, low = split(v)
    return dot(high, head_map(j), (1, 1)) + dot(low, head_map(j), (1, 1))


def small_map(r):
    row, col = iota((8 * LANES, SMALL), 0), iota((8 * LANES, SMALL), 1)
    t, lane = row // LANES, row % LANES - 38 * r
    state = (lane >= 0) & (lane < 32) & (col == t * 32 + lane)
    step = (lane >= 32) & (lane < 38) & (col == 256 + t * 6 + lane - 32)
    return (state | step).astype(BF16)


def tile_of(j):
    return pl.ds(pl.multiple_of(j * TILE, TILE), TILE)


def conv_links(doc_col, offset, rows):
    return (doc_col[HALO : HALO + rows] == doc_col[HALO - offset : HALO - offset + rows]).astype(F32)


def conv(ext, taps, bias, links):
    total = bias + taps[TAPS - 1 : TAPS] * ext[HALO:]
    for offset in range(1, TAPS):
        total = total + taps[TAPS - 1 - offset : TAPS - offset] * ext[HALO - offset : EXT - offset] * links[offset]
    return total


def small_params(phead):
    return dot(phead, small_map(0).astype(F32), precision=lax.Precision.HIGHEST)


def decay_terms(step, cum, doc_col, doc_prev):
    block = doc_col[HALO:EXT]
    end = cum[BLOCK - 1 : BLOCK]
    tail = jnp.exp(end - cum) * (block == block[BLOCK - 1 : BLOCK]).astype(F32)
    enter = jnp.exp(cum) * (block == doc_prev).astype(F32)
    keep = jnp.exp(end) * (block[BLOCK - 1 : BLOCK] == doc_prev).astype(F32)
    return enter, tail, tail * step, keep


def pack_kernel(
    main_proj, out_proj, state_proj, step_proj, conv_main, conv_main_bias, conv_state, conv_state_bias, step_bias,
    decay_log, skip_gain, gate_gain, norm_gain, doc_ids,
    shards, small, pmain, phead, doc_col, doc_row, gain, docs,
):
    t = lax.axis_index("tensor")
    shards[0] = main_proj[:, 1, :]
    shards[1] = main_proj[:, 0, :]
    shards[2] = out_proj[...]
    both = jnp.concatenate([state_proj[...].T, step_proj[...].T], 1)
    lanes = [both[r * 32 : r * 32 + 32] for r in range(3)]
    small[0] = jnp.concatenate(lanes + [jnp.zeros((SMALL_ROWS, 14), BF16)], 1)
    pmain[0:TAPS] = conv_main[...]
    pmain[TAPS : TAPS + 1] = conv_main_bias[...].reshape(1, WIDTH)
    pmain[5:6] = gate_gain[...].reshape(1, WIDTH)
    own_skip = skip_gain[...].reshape(1, 6)
    pmain[6:7] = jnp.concatenate([jnp.broadcast_to(own_skip[:, h : h + 1], (1, HEAD_DIM)) for h in range(6)], 1)
    pmain[7:8] = jnp.zeros((1, WIDTH), F32)
    phead[...] = jnp.zeros_like(phead)
    phead[0:TAPS, 0:32] = conv_state[...]
    phead[TAPS : TAPS + 1, 0:32] = conv_state_bias[...].reshape(1, 32)
    phead[5:6, 32:38] = step_bias[...].reshape(1, 6)
    phead[6:7, 32:38] = decay_log[...].reshape(1, 6)
    phead[7:8, 32:38] = own_skip
    gain[...] = norm_gain[...].reshape(1, D)
    docs[:, 0:LANES] = jnp.full((8, LANES), -1, jnp.int32)
    docs[:, LANES : LANES + 2048] = jnp.broadcast_to(doc_ids[...].reshape(1, 2048), (8, 2048))
    docs[:, LANES + 2048 :] = jnp.full((8, LANES), -2, jnp.int32)
    window = docs[:, pl.ds(pl.multiple_of(t * BLOCK, LANES), 2 * BLOCK)]
    doc_row[...] = window[0:1, LANES : LANES + BLOCK]
    doc_col[...] = window.T[LANES - HALO : LANES + BLOCK + 16, 0:1]


def pack(*args):
    vmem = pl.BlockSpec(memory_space=VMEM)
    shapes = [
        ((3, ROWS, WIDTH), BF16), ((1, SMALL_ROWS, SMALL_WIDTH), BF16), ((8, WIDTH), F32), ((8, LANES), F32),
        ((EXT + 16, 1), jnp.int32), ((1, BLOCK), jnp.int32), ((1, D), F32),
    ]
    return pl.pallas_call(
        pack_kernel,
        name="pack",
        out_shape=[jax.ShapeDtypeStruct(*s) for s in shapes],
        in_specs=[vmem] * 14,
        out_specs=[vmem] * len(shapes),
        scratch_shapes=[VMEM((8, 2048 + 2 * LANES), jnp.int32)],
    )(*args)


def finish_kernel(
    own_main, own_small, vec,
    norm_gain, main_proj, step_proj, state_proj, conv_main, conv_main_bias, conv_state, conv_state_bias, step_bias,
    decay_log, skip_gain, gate_gain, out_proj,
):
    t = lax.axis_index("tensor")
    main_proj[:, 0, :] = own_main[1]
    main_proj[:, 1, :] = own_main[0]
    out_proj[...] = own_main[2]
    packed = own_small[0]
    for r in range(3):
        rows_t = packed[:, r * 38 : r * 38 + 38].T
        state_proj[:, r * 32 : r * 32 + 32] = rows_t[:32]
        step_proj[:, r * 32 : r * 32 + 32] = rows_t[32:]
    own = vec[:, pl.ds(pl.multiple_of(t * WIDTH, LANES), WIDTH)]
    conv_main[...] = own[:TAPS]
    conv_main_bias[...] = own[TAPS : TAPS + 1].reshape(WIDTH)
    gate_gain[...] = own[5:6].reshape(WIDTH)
    state = pltpu.roll(vec[:, DI : DI + 256], lax.rem(256 - 32 * t, 256), axis=1)
    conv_state[...] = state[:TAPS, :32]
    conv_state_bias[...] = state[TAPS : TAPS + 1, :32].reshape(32)
    heads = pltpu.roll(vec[:, DI + 256 :], lax.rem(LANES - 6 * t, LANES), axis=1)
    step_bias[...] = heads[5:6, :6].reshape(6)
    decay_log[...] = heads[6:7, :6].reshape(6)
    skip_gain[...] = heads[7:8, :6].reshape(6)
    norm_gain[...] = vec[6:7, 0:D].reshape(D)


def finish(*args):
    vmem = pl.BlockSpec(memory_space=VMEM)
    shapes = [
        (D,), (ROWS, 2, WIDTH), (6, ROWS), (32, ROWS), (TAPS, WIDTH), (WIDTH,), (TAPS, 32), (32,), (6,), (6,), (6,),
        (WIDTH,), (ROWS, WIDTH),
    ]
    outs = pl.pallas_call(
        finish_kernel,
        name="finish",
        out_shape=[jax.ShapeDtypeStruct(s, F32) for s in shapes],
        in_specs=[vmem] * 3,
        out_specs=[vmem] * len(shapes),
    )(*args)
    return [v.T if i in (2, 3) else v for i, v in enumerate(outs)]


PAIR = 2 * HEAD_DIM
PAIRS = DI // PAIR
HALF = BLOCK // 2
CHUNK = 128
CHUNKS = DI // CHUNK
FORWARD_LAG, BACKWARD_LAG = 10, 4


def pair_of(p):
    return pl.ds(pl.multiple_of(p * PAIR, PAIR), PAIR)


def chunk_of(c):
    return pl.ds(pl.multiple_of(c * CHUNK, CHUNK), CHUNK)


def only(value, first):
    lane = iota(value.shape, 1)
    return jnp.where((lane < HEAD_DIM) == first, value, jnp.zeros_like(value))


def head_column(ref, h):
    return pltpu.roll(ref[...], lax.rem(LANES - h, LANES), axis=1)[:, :1]


def mid_kernel(
    hidden, gain, doc_col, doc_row, cot, shards, small, pmain_own, phead_own,
    pmain, phead, raw, state_pre, grad_bc, grad_step_in, vec_gate, vec_heads,
    mixed_out, normed_out, w_small_out, acc_out, grad_x_out, x_ext, x_pre, grad_out, grad_gate, full,
    mixed, normed_t, w_small, acc, grad_x, packed, halo, normed, w_in, ext_out, pre_out, staged, x_act, bc, scores, gate_in, work, y, gate_out, dy, gate_grad, update,
    grad_add, state, state_low, grad_state, keep_row, f_out, f_in, b_out, b_in, cot_t, mixed_acc,
    barred, cum2, cum_t, step_t, step_in, enter_ref, weight_ref, rows_acc, q_t, gs, acc_c, acc_heads, row_acc,
    w_sem, put_sem, x_sem, f_send, f_recv, b_send, b_recv, g_send, g_recv, core_send, core_recv, own_sem, halo_sem,
    param_send, param_recv, out_sem,
):
    t = lax.axis_index("tensor")

    def load(m, j, slot):
        return pltpu.make_async_copy(full.at[m, :, :, :, :, tile_of(j)], w_in.at[slot], w_sem.at[slot])

    def held(slot):
        return w_in[slot].reshape(D, TILE)

    at, core = coordinates()
    both = [full, packed]
    own = []
    for w, source in enumerate((shards, small)):
        for lo, row, cols in pieces(at, (), WIDTHS[w]):
            own.append(
                pltpu.make_async_copy(source, both[w].at[:, lo.start, row.start, core, :, cols], own_sem.at[w])
            )
    params_own, params_all = (pmain_own, phead_own), (pmain, phead)

    def columns(i, of):
        width = params_own[i].shape[-1]
        return params_all[i].at[:, pl.ds(pl.multiple_of(of * width, 128), width)]

    for i in range(2):
        own.append(pltpu.make_async_copy(params_own[i], columns(i, t), own_sem.at[2 + i]))
    for c in own:
        c.start()
    greet(at, core, [tensor_peer(by) for by in range(1, 8)])
    sends, await_step, to_partner, await_partner = gather_ops(both, g_send, g_recv, core_send, core_recv)

    def halo_copy():
        return pltpu.make_async_remote_copy(
            src_ref=hidden.at[pl.ds(BLOCK - HALO, HALO)], dst_ref=halo, send_sem=halo_sem.at[0],
            recv_sem=halo_sem.at[1], device_id=tensor_peer(1), device_id_type=MESH,
        )

    def param_copy(by, i, of):
        return pltpu.make_async_remote_copy(
            src_ref=params_own[i], dst_ref=columns(i, of), send_sem=param_send.at[i, by - 1],
            recv_sem=param_recv.at[i, by - 1], device_id=tensor_peer(by), device_id_type=MESH,
        )

    everything = [3, 0, 1, 2]

    def rms(rows, part):
        value = part[...].astype(F32)
        inv = lax.rsqrt(jnp.mean(value * value, axis=1, keepdims=True) + epsilon)
        normed[rows] = (value * inv * gain[...]).astype(BF16)

    def units_with(m):
        return [3] if m == 3 else MAIN_UNITS

    def gather_first(m):
        for u in units_with(m):
            sends(u, 2, pl.ds(m % 3, 1), 0, 2 + m % 3)

    def gather_near(m):
        for u in units_with(m):
            to_partner(u, pl.ds(m % 3, 1), [0], m % 3)

    def gather_forward(m):
        for u in units_with(m):
            await_step(u, 2, pl.ds(m % 3, 1), 0, 2 + m % 3, g_recv)
            sends(u, 2, pl.ds(m % 3, 1), 1, 2 + m % 3)

    def gather_second(m):
        for u in units_with(m):
            to_partner(u, pl.ds(m % 3, 1), [-1, 1], m % 3)

    def gather_last(m):
        for u in units_with(m):
            await_step(u, 2, pl.ds(m % 3, 1), 1, 2 + m % 3, g_recv)
            to_partner(u, pl.ds(m % 3, 1), [2], m % 3)

    def gather_done(m):
        for u in units_with(m):
            await_partner(u, pl.ds(m % 3, 1), m % 3, core_recv)

    one, others = pl.ds(0, 1), pl.ds(1, 2)
    for c in own:
        c.wait()
    for u in everything:
        sends(u, 0, one, 0, 0)
    halo_copy().start()
    for by in range(1, 8):
        for i in range(2):
            param_copy(by, i, t).start()
    for u in MAIN_UNITS:
        sends(u, 0, others, 0, 5)
    rms(pl.ds(HALO, BLOCK), hidden)
    for u in everything:
        await_step(u, 0, one, 0, 0, g_recv)
        sends(u, 0, one, 1, 0)
    for u in everything:
        await_step(u, 0, one, 1, 0, g_recv)
        sends(u, 1, one, 0, 1)
    for u in MAIN_UNITS:
        await_step(u, 0, others, 0, 5, g_recv)
        sends(u, 0, others, 1, 5)
    cot_t[...] = cot[...].T
    for u in everything:
        await_step(u, 1, one, 0, 1, g_recv)
        sends(u, 1, one, 1, 1)
    normed_t[...] = normed[pl.ds(HALO, BLOCK)].T
    leaving = [
        pltpu.make_async_copy(src, dst, out_sem.at[i])
        for i, (src, dst) in enumerate(
            ((normed_t, normed_out), (w_small, w_small_out), (acc, acc_out), (mixed, mixed_out))
        )
    ]
    leaving[0].start()

    def grad_x_put(j):
        return pltpu.make_async_copy(grad_x.at[:, tile_of(j)], grad_x_out.at[:, tile_of(j)], out_sem.at[4 + j])

    for u in everything:
        await_step(u, 1, one, 1, 1, g_recv)
        sends(u, 2, one, 0, 2)
    gather_near(3)
    gather_near(0)
    for u in MAIN_UNITS:
        await_step(u, 0, others, 1, 5, g_recv)
        sends(u, 1, others, 0, 6)
    halo_copy().wait()
    rms(pl.ds(0, HALO), halo)
    for by in range(1, 8):
        for i in range(2):
            param_copy(by, i, lax.rem(t + 8 - by, 8)).wait()
    gather_forward(3)
    gather_second(3)
    gather_forward(0)
    gather_second(0)
    for u in MAIN_UNITS:
        await_step(u, 1, others, 0, 6, g_recv)
        sends(u, 1, others, 1, 6)
    gather_last(3)
    gather_done(3)

    for r in range(3):
        rows = dot(packed[...].reshape(512, 8 * LANES), small_map(r)).astype(BF16)
        for d in range(16):
            w_small[pl.ds(d * 96 + r * 32, 32)] = rows[d * 32 : d * 32 + 32]
    raw[...] = dot(normed[...], w_small[...])
    leaving[1].start()
    for u in MAIN_UNITS:
        await_step(u, 1, others, 1, 6, g_recv)
        sends(u, 2, pl.ds(1, 1), 0, 3)
    gather_first(2)
    params = small_params(phead[...])
    docs = doc_col[...]
    links = [None] + [conv_links(docs, o, BLOCK) for o in range(1, TAPS)]
    pre = conv(raw[:, :256], params[:TAPS, :256], params[TAPS : TAPS + 1, :256], links)
    state_pre[...] = pre
    act = silu(pre).astype(BF16)
    bc[...] = act
    scores[...] = dot(act[:, STATE:], act[:, :STATE], (1, 1))
    step_in[...] = raw[HALO:, 256:] + params[5:6, 256:]
    rate = -jnp.exp(params[6:7, 256:])
    step = softplus(step_in[...])
    lower = (iota((BLOCK, BLOCK), 0) >= iota((BLOCK, BLOCK), 1)).astype(F32)
    cum = dot(lower, step * rate, precision=lax.Precision.HIGHEST)
    enter, tail, weight, keep = decay_terms(step, cum, docs, docs[HALO - 1 : HALO])
    enter_ref[...] = enter
    weight_ref[...] = weight
    cum2[...] = cum * LOG2E
    for ref, turned in ((cum_t, (cum * LOG2E).T), (step_t, step.T)):
        for h in range(HEADS):
            ref[h] = turned[h : h + 1]
    linked = (docs[HALO:EXT] == doc_row[...]) & (iota((BLOCK, BLOCK), 0) >= iota((BLOCK, BLOCK), 1))
    barred[...] = jnp.where(linked, 0.0, -1e30)
    keep8 = jnp.broadcast_to(keep, (8, LANES))

    gather_last(0)
    gather_near(1)
    gather_near(2)
    gather_done(0)
    load(0, 0, 0).start()

    def chain(forward, c, add, into, outgoing, incoming, send, recv):
        cols = chunk_of(c)
        by = 1 if forward else 7
        is_first = t == (0 if forward else 7)
        is_last = t == (7 if forward else 0)

        def copy():
            return pltpu.make_async_remote_copy(
                src_ref=outgoing.at[:, cols], dst_ref=incoming.at[:, cols], send_sem=send.at[c],
                recv_sem=recv.at[c], device_id=tensor_peer(by), device_id_type=MESH,
            )

        @pl.when(is_first)
        def _():
            into[:, cols] = jnp.zeros((STATE, CHUNK), F32)

        @pl.when(jnp.logical_not(is_first))
        def _():
            copy().wait_recv()
            into[:, cols] = incoming[:, cols].astype(F32)

        @pl.when(jnp.logical_not(is_last))
        def _():
            outgoing[:, cols] = (keep_row[0:1, cols] * into[:, cols] + add[:, cols]).astype(BF16)
            copy().start()

    def forward_slot(s):
        c = s - FORWARD_LAG * t

        @pl.when((c >= 0) & (c < CHUNKS))
        def _():
            chain(True, c, update, state, f_out, f_in, f_send, f_recv)

    def backward_slot(s):
        c = s - BACKWARD_LAG * (7 - t)

        @pl.when((c >= 0) & (c < CHUNKS))
        def _():
            chain(False, c, grad_add, grad_state, b_out, b_in, b_send, b_recv)

    def x_puts(j, slot):
        return [
            pltpu.make_async_copy(src.at[slot], dst.at[:, tile_of(j)], x_sem.at[i, slot])
            for i, (src, dst) in enumerate(((ext_out, x_ext), (pre_out, x_pre)))
        ]

    def x_tile(j):
        cols = tile_of(j)
        slot = lax.rem(j, 2)

        @pl.when(j + 1 < TILES)
        def _():
            load(0, j + 1, 1 - slot).start()

        @pl.when(j >= 2)
        def _():
            for c in x_puts(j, slot):
                c.wait()

        load(0, j, slot).wait()
        ext = dot(normed[...], held(slot))
        ext_out[slot] = ext
        pre = conv(ext, pmain[0:TAPS, cols], pmain[TAPS : TAPS + 1, cols], links)
        pre_out[slot] = pre
        for c in x_puts(j, slot):
            c.start()
        act = silu(pre).astype(BF16)
        x_act[:, cols] = act
        heavy = (act.astype(F32) * widen(weight_ref[...], j)).astype(BF16)
        update[:, cols] = dot(bc[:, :STATE], heavy, (0, 0))
        keep_row[:, cols] = widen(keep8, j)
        for k in range(4):
            forward_slot(4 * j + k)

    gather_forward(1)
    gather_second(1)
    pl.loop(0, 3)(x_tile)
    gather_forward(2)
    gather_second(2)
    pl.loop(3, TILES)(x_tile)
    for slot in range(2):
        for c in x_puts(TILES - 2 + slot, slot):
            c.wait()

    halves = [(slice(0, HALF), slice(0, HALF)), (slice(HALF, BLOCK), slice(0, BLOCK))]

    def decay_of(h, column, rows, cols):
        return jnp.exp2(column[rows] - cum_t[h, :, cols] + barred[rows, cols])

    def intra_forward(p):
        cols = pair_of(p)
        x = x_act[:, cols]
        x2 = [only(x, True), only(x, False)]
        columns = [head_column(cum2, 2 * p + k) for k in (0, 1)]
        for rows, js in halves:
            mix = [
                (scores[rows, js] * (decay_of(2 * p + k, columns[k], rows, js) * step_t[2 * p + k, :, js])).astype(BF16)
                for k in (0, 1)
            ]
            y[rows, cols] = dot(jnp.concatenate(mix, 1), jnp.concatenate([v[js] for v in x2], 0))

    def scan_pairs(first, last):
        @pl.loop(first, last)
        def _(i):
            forward_slot(4 * TILES + 2 * i)
            intra_forward(i)
            forward_slot(4 * TILES + 2 * i + 1)

    def gate_tile(j, slot):
        gate_in[:, tile_of(j)] = dot(normed[pl.ds(HALO, BLOCK)], held(slot))

    def out_tile(j, slot):
        work[:, tile_of(j)] = dot(cot[...], held(slot))

    def tile_step(m, j, use):
        slot = lax.rem(j, 2)

        @pl.when(j + 1 < TILES)
        def _():
            load(m, j + 1, 1 - slot).start()

        load(m, j, slot).wait()
        use(j, slot)

    scan_pairs(0, 8)
    gather_last(1)
    scan_pairs(8, 12)
    gather_last(2)
    gather_done(1)
    load(1, 0, 0).start()

    @pl.loop(0, TILES)
    def _(j):
        for k in range(2):
            i = 12 + 2 * j + k
            forward_slot(4 * TILES + 2 * i)
            intra_forward(i)
            forward_slot(4 * TILES + 2 * i + 1)
        tile_step(1, j, gate_tile)

    base = 4 * TILES + 2 * PAIRS
    gather_done(2)
    load(2, 0, 0).start()

    @pl.loop(0, TILES)
    def _(j):
        forward_slot(base + j)
        tile_step(2, j, out_tile)

    base = base + TILES

    load(2, 0, 1).start()
    load(1, 0, 0).start()
    row_acc[...] = jnp.zeros_like(row_acc)

    @pl.loop(0, TILES)
    def _(j):
        @pl.loop(0, TILE // CHUNK)
        def _(k):
            c = j * (TILE // CHUNK) + k

            @pl.when(c + FORWARD_LAG * t >= base)
            def _():
                chain(True, c, update, state, f_out, f_in, f_send, f_recv)

        cols = tile_of(j)
        low = state[:, cols].astype(BF16)
        state_low[:, cols] = low
        carried = dot(bc[:, STATE:], low)
        value = y[:, cols] + carried * widen(enter_ref[...], j) + pmain[6:7, cols] * x_act[:, cols].astype(F32)
        y[:, cols] = value
        gated = value * silu(gate_in[:, cols])
        row_acc[...] += jnp.broadcast_to(jnp.sum(gated * gated, axis=1, keepdims=True), (BLOCK, LANES))

    gate_inv = lax.rsqrt(row_acc[:, :1] / DI + epsilon)
    row_acc[...] = jnp.zeros_like(row_acc)

    @pl.loop(0, TILES)
    def _(j):
        cols = tile_of(j)
        gated = y[:, cols] * silu(gate_in[:, cols])
        hat = gated * gate_inv
        gate_gain = pmain[5:6, cols]
        gate_out[:, cols] = (hat * gate_gain).astype(BF16)
        grad = work[:, cols]
        vec_gate[:, cols] = jnp.broadcast_to(jnp.sum(grad * hat, axis=0, keepdims=True), (8, TILE))
        dn = grad * gate_gain
        work[:, cols] = dn
        row_acc[...] += jnp.broadcast_to(jnp.sum(dn * gated, axis=1, keepdims=True), (BLOCK, LANES))

    inner = row_acc[:, :1] / DI * gate_inv * gate_inv * gate_inv
    acc_c[...] = jnp.zeros_like(acc_c)
    acc_heads[...] = jnp.zeros_like(acc_heads)

    @pl.loop(0, TILES)
    def _(j):
        cols = tile_of(j)
        gate, value = gate_in[:, cols], y[:, cols]
        s = sigmoid(gate)
        act = gate * s
        grad_gated = gate_inv * work[:, cols] - value * act * inner
        grad = (grad_gated * act).astype(BF16)
        dy[:, cols] = grad
        gate_grad[:, cols] = (grad_gated * value * (s * (1.0 + gate * (1.0 - s)))).astype(BF16)
        grad = grad.astype(F32)
        carried_grad = (grad * widen(enter_ref[...], j)).astype(BF16)
        low = state_low[:, cols]
        grad_add[:, cols] = dot(bc[:, STATE:], carried_grad, (0, 0))
        acc_c[...] += dot(carried_grad, low, (1, 1))
        acc_heads[0] += by_head(grad * dot(bc[:, STATE:], low), j)

    rows_acc[...] = jnp.zeros_like(rows_acc)
    gs[...] = jnp.zeros_like(gs)
    acc[...] = jnp.zeros_like(acc)
    mixed_acc[...] = jnp.zeros_like(mixed_acc)

    def intra_backward(p):
        cols = pair_of(p)
        x, grad = x_act[:, cols], dy[:, cols]
        grad2 = [only(grad, True), only(grad, False)]
        columns = [head_column(cum2, 2 * p + k) for k in (0, 1)]
        lane = iota((HALF, LANES), 1)
        parts = []
        q_rows = [[], []]
        for rows, js in halves:
            mixes = []
            gs_sum = gs[rows, js]
            pulls = jnp.zeros((HALF, LANES), F32)
            for k in (0, 1):
                h = 2 * p + k
                decay = decay_of(h, columns[k], rows, js)
                decay_step = decay * step_t[h, :, js]
                mixes.append((scores[rows, js] * decay_step).astype(BF16))
                grad_mix = dot(grad2[k][rows], x[js], (1, 1))
                gs_sum = gs_sum + grad_mix * decay_step
                q = grad_mix * scores[rows, js] * decay
                q_rows[k].append(jnp.sum(q, axis=0, keepdims=True))
                pull = jnp.sum(q * step_t[h, :, js], axis=1, keepdims=True)
                pulls = jnp.where(lane == h, pull, pulls)
            gs[rows, js] = gs_sum
            rows_acc[rows] += pulls
            parts.append(dot(jnp.concatenate(mixes, 0), jnp.concatenate([v[rows] for v in grad2], 0), (0, 0)))
        grad_x[pl.ds(0, HALF), cols] = parts[0] + parts[1][:HALF]
        grad_x[pl.ds(HALF, HALF), cols] = parts[1][HALF:]
        for k in (0, 1):
            first, second = q_rows[k]
            q_t[2 * p + k, :, 0:HALF] = first + second[:, :HALF]
            q_t[2 * p + k, :, HALF:BLOCK] = second[:, HALF:]

    def put(ref, j, slot):
        return [
            pltpu.make_async_copy(
                staged.at[slot, pl.ds(i * ROWS, ROWS)], ref.at[0, lo, y_, c, :, tile_of(j)], put_sem.at[slot, i]
            )
            for i, (lo, y_, c) in enumerate((lo, y_, c) for lo in range(2) for y_ in range(4) for c in range(2))
        ]

    def put_tile(ref, j, slot, lhs, grad):
        @pl.when(j >= 1)
        def _():
            for c in put(ref, j, slot):
                c.wait()

        staged[slot] = dot(lhs[...], grad).astype(BF16)
        for c in put(ref, j, slot):
            c.start()

    @pl.loop(0, PAIRS)
    def _(i):
        backward_slot(2 * i)
        intra_backward(i)
        backward_slot(2 * i + 1)
        j = lax.div(i, 4)
        cols = tile_of(j)

        @pl.when(lax.rem(i, 4) == 0)
        def _():
            put_tile(grad_out, j, 0, cot_t, gate_out[:, cols])

        @pl.when(lax.rem(i, 4) == 1)
        def _():
            put_tile(grad_gate, j, 1, normed_t, gate_grad[:, cols])

        @pl.when(lax.rem(i, 4) == 2)
        def _():
            load(2, j, 1).wait()
            mixed_acc[...] += dot(gate_out[:, cols], held(1), (1, 1))

            @pl.when(j + 1 < TILES)
            def _():
                load(2, j + 1, 1).start()

        @pl.when(lax.rem(i, 4) == 3)
        def _():
            load(1, j, 0).wait()
            acc[...] += dot(gate_grad[:, cols], held(0), (1, 1))

            @pl.when(j + 1 < TILES)
            def _():
                load(1, j + 1, 0).start()

    leaving[2].start()
    mixed[...] = (hidden[...].astype(F32) + mixed_acc[...]).astype(BF16)
    leaving[3].start()
    gs_low = gs[...].astype(BF16)
    grad_bc[:, STATE:] = acc_c[...] + dot(gs_low, bc[:, :STATE])
    acc_c[...] = dot(gs_low, bc[:, STATE:], (0, 0))

    @pl.loop(0, TILES)
    def _(j):
        @pl.loop(0, TILE // CHUNK)
        def _(k):
            c = j * (TILE // CHUNK) + k

            @pl.when(c + BACKWARD_LAG * (7 - t) >= 2 * PAIRS)
            def _():
                chain(False, c, grad_add, grad_state, b_out, b_in, b_send, b_recv)

        cols = tile_of(j)
        wide = widen(weight_ref[...], j)
        grad_update = grad_state[:, cols].astype(BF16)
        spread_grad = dot(bc[:, :STATE], grad_update)
        x, grad = x_act[:, cols].astype(F32), dy[:, cols].astype(F32)
        grad_x[:, cols] += wide * spread_grad + pmain[6:7, cols] * grad
        grad_x_put(j).start()
        acc_heads[1] += by_head(x * spread_grad, j)
        acc_c[...] += dot((x * wide).astype(BF16), grad_update, (1, 1))
        kept = jnp.sum(grad_state[:, cols] * state[:, cols], axis=0, keepdims=True)
        skip = jnp.sum(x * grad, axis=0, keepdims=True)
        row = iota((8, TILE), 0)
        both = jnp.where(row == 0, kept, jnp.where(row == 1, skip, 0.0))
        acc_heads[2, 0:8] += by_head(both, j)

    grad_bc[:, :STATE] = acc_c[...]
    grad_weight = acc_heads[1]
    none = jnp.zeros((LANES - HEADS, BLOCK), F32)
    step = jnp.concatenate([step_t[h] for h in range(HEADS)] + [none], 0).T
    q = jnp.concatenate([q_t[h] for h in range(HEADS)] + [none], 0).T
    weight_pull = grad_weight * weight_ref[...]
    grad_end = jnp.sum(weight_pull, axis=0, keepdims=True) + acc_heads[2, 0:1] * keep
    grad_cum = rows_acc[...] - step * q + enter_ref[...] * acc_heads[0] - weight_pull
    grad_cum = grad_cum + jnp.where(iota((BLOCK, LANES), 0) == BLOCK - 1, grad_end, 0.0)
    upper = (iota((BLOCK, BLOCK), 0) <= iota((BLOCK, BLOCK), 1)).astype(F32)
    grad_log = dot(upper, grad_cum, precision=lax.Precision.HIGHEST)
    grad_step = q + grad_weight * tail + rate * grad_log
    grad_in = grad_step * sigmoid(step_in[...])
    grad_step_in[...] = grad_in
    row = iota((8, LANES), 0)
    heads = jnp.where(row == 5, jnp.sum(grad_in, axis=0, keepdims=True), 0.0)
    heads = jnp.where(row == 6, rate * jnp.sum(grad_log * step, axis=0, keepdims=True), heads)
    vec_heads[...] = jnp.where(row == 7, acc_heads[2, 1:2], heads)

    for c in leaving:
        c.wait()
    for j in range(TILES):
        grad_x_put(j).wait()
    for u in everything:
        for step in (0, 1):
            for phase in (0, 1):
                await_step(u, phase, one, step, phase, g_send)
                if u in MAIN_UNITS:
                    await_step(u, phase, others, step, 5 + phase, g_send)
    for m in range(4):
        for u in units_with(m):
            await_partner(u, pl.ds(m % 3, 1), m % 3, core_send)
            for step in (0, 1):
                await_step(u, 2, pl.ds(m % 3, 1), step, 2 + m % 3, g_send)
    for slot, ref in ((0, grad_out), (1, grad_gate)):
        for c in put(ref, TILES - 1, slot):
            c.wait()
    for by, ends, outgoing, incoming, send, recv in (
        (1, 7, f_out, f_in, f_send, f_recv),
        (7, 0, b_out, b_in, b_send, b_recv),
    ):

        @pl.when(t != ends)
        def _(by=by, outgoing=outgoing, incoming=incoming, send=send, recv=recv):
            @pl.loop(0, CHUNKS)
            def _(c):
                pltpu.make_async_remote_copy(
                    src_ref=outgoing.at[:, chunk_of(c)], dst_ref=incoming.at[:, chunk_of(c)], send_sem=send.at[c],
                    recv_sem=recv.at[c], device_id=tensor_peer(by), device_id_type=MESH,
                ).wait_send()


def mid(*args):
    vmem = pl.BlockSpec(memory_space=VMEM)
    anywhere = pl.BlockSpec(memory_space=pl.ANY)
    wide, heads, square = (BLOCK, DI), (BLOCK, LANES), (BLOCK, BLOCK)
    turned, own_state = (HEADS, 1, BLOCK), (STATE, DI)
    blocks = (1, 2, 4, 2, ROWS, DI)
    shapes = [
        ((8, DI), F32), ((8, 8 * LANES), F32), ((EXT, SMALL), F32), (square, F32), (square, F32), (heads, F32),
        ((8, DI), F32), ((8, LANES), F32),
    ]
    moved_out = [((BLOCK, D), BF16), ((D, BLOCK), BF16), ((D, SMALL), BF16), ((BLOCK, D), F32), (wide, F32)]
    in_hbm = [((EXT, DI), F32), (wide, F32), (blocks, BF16), (blocks, BF16), ((3,) + blocks[1:], BF16)]
    scratch = [
        ((1, 2, 4, 2, SMALL_ROWS, 8 * LANES), BF16), ((HALO, D), BF16), ((EXT, D), BF16), ((2, 2, 4, 2, ROWS, TILE), BF16), ((2, EXT, TILE), F32), ((2, BLOCK, TILE), F32), ((2, D, TILE), BF16),
        (wide, BF16), ((BLOCK, 2 * STATE), BF16), (square, F32), (wide, F32), (wide, F32), (wide, F32), (wide, BF16),
        (wide, BF16), (wide, BF16), (own_state, F32), (own_state, F32), (own_state, F32), (own_state, BF16),
        (own_state, F32), ((8, DI), F32), (own_state, BF16), (own_state, BF16), (own_state, BF16), (own_state, BF16),
        ((D, BLOCK), BF16), ((BLOCK, D), F32),
        (square, F32), (heads, F32), (turned, F32), (turned, F32), (heads, F32), (heads, F32), (heads, F32),
        (heads, F32), (turned, F32), (square, F32), (heads, F32), ((3,) + heads, F32), (heads, F32),
    ]
    return pl.pallas_call(
        mid_kernel,
        name="scan_and_gate",
        out_shape=[jax.ShapeDtypeStruct(*s) for s in shapes + moved_out + in_hbm],
        in_specs=[vmem] * 5 + [anywhere] * 4,
        out_specs=[vmem] * 8 + [anywhere] * 10,
        scratch_shapes=[VMEM(*s) for s in moved_out + scratch]
        + [pltpu.SemaphoreType.DMA((2,)), pltpu.SemaphoreType.DMA((2, 16)), pltpu.SemaphoreType.DMA((2, 2))]
        + [pltpu.SemaphoreType.DMA((CHUNKS,))] * 4
        + [pltpu.SemaphoreType.DMA((len(UNITS), 7, 2))] * 2
        + [pltpu.SemaphoreType.DMA((len(UNITS), 3))] * 2
        + [pltpu.SemaphoreType.DMA(s) for s in ((4,), (2,), (2, 7), (2, 7), (4 + TILES,))],
        compiler_params=pltpu.CompilerParams(
            collective_id=1, has_side_effects=True, vmem_limit_bytes=60 * 2**20
        ),
    )(*args)


VEC = (8, 8 * WIDTH + 384)
VEC_STEPS = 7
MATS = (2, 1, 0)


def spread(whole):
    return (2 if 2 in whole else 1, 4 if 1 in whole else 1, (4 if 0 in whole else 1) * (2 if 2 in whole else 1))


def region_shape(u, phase, rows):
    lo, y, cols = spread(axes_of(u)[:phase])
    return (lo, y, rows, cols * WIDTHS[UNITS[u][0]])


def back_kernel(*refs):
    refs = list(refs)

    def take(n):
        got = refs[:n]
        del refs[:n]
        return got

    (raw_ext, state_pre, grad_bc, grad_step_in, pmain, phead, doc_col, gain, vec_gate, vec_heads,
     normed_in, w_small_in, acc_in, hidden_in, cot_in, x_ext, x_pre, grad_x, grad_gate, grad_out, full) = take(21)
    grad_main, grad_small, out_main, out_small, grad_hidden, vec_out = take(6)
    outs = (out_main, out_small)
    units = SUMMED
    other = take(2)
    half_buf = [take(3) for _ in range(units)]
    full_buf = [take(3) for _ in range(units)]
    own = take(units)
    (ext_in, pre_in, grad_in, first_grad, first_pre, first_out, after, w_in, staged, raw_x, acc, small_acc,
     small_out, vec_acc, vec_in, normed_t, w_small, hidden, cot) = take(19)
    (stream_sem, first_sem, halo_sem, w_sem, put_sem, small_sem, own_sem, vec_send, vec_recv, send, recv, core_send,
     core_recv, entry_sem) = take(14)
    at, core = coordinates()
    t = lax.axis_index("tensor")
    everything = range(units)

    def stream(j, slot):
        cols = tile_of(j)
        return [
            pltpu.make_async_copy(src.at[:, cols], dst.at[slot], stream_sem.at[i, slot])
            for i, (src, dst) in enumerate(((x_ext, ext_in), (x_pre, pre_in), (grad_x, grad_in)))
        ]

    firsts = [
        pltpu.make_async_copy(src.at[pl.ds(0, 8)], dst, first_sem.at[i])
        for i, (src, dst) in enumerate(((grad_x, first_grad), (x_pre, first_pre)))
    ]
    entering = [
        pltpu.make_async_copy(src, dst, entry_sem.at[i])
        for i, (src, dst) in enumerate(
            ((normed_in, normed_t), (w_small_in, w_small), (acc_in, acc), (hidden_in, hidden), (cot_in, cot))
        )
    ]
    for c in firsts + stream(0, 0) + entering:
        c.start()
    greet(at, core, [device(moved(at, axis, 2), core) for axis in AXES] + [tensor_peer(1), tensor_peer(7)])

    def source_of(u, m):
        return grad_small if UNITS[u][0] else (grad_main, grad_gate, grad_out)[m]

    def units_of(m):
        return [u for u in everything if m == 0 or UNITS[u][0] == 0]

    def index_of(u, m):
        return 0 if UNITS[u][0] else m

    def part_of(ref, u, mats, where, whole, half=None):
        which, first, rows = UNITS[u][0], UNITS[u][1], 32
        if half is not None:
            first, rows = first + half * 16, 16
        return [ref.at[mats, lo, y, pl.ds(first, rows), cols] for lo, y, cols in pieces(where, whole, WIDTHS[which])]

    def place(u, by):
        return moved(at, axes_of(u)[2], by) if by else at

    groups = [[2], [1, -1], [0]]

    def to_partner(m):
        for g, group in enumerate(groups):
            for u in units_of(m):
                for by in group:
                    whole = axes_of(u)[:2]
                    for src, dst in zip(
                        region(source_of(u, m), u, 1 - core, pl.ds(0, 1), place(u, by), whole),
                        part_of(other[UNITS[u][0]], u, pl.ds(index_of(u, m), 1), place(u, by), whole),
                    ):
                        pltpu.make_async_remote_copy(
                            src_ref=src, dst_ref=dst, send_sem=core_send.at[u, m], recv_sem=core_recv.at[u, m, g],
                            device_id=device(at, 1 - core), device_id_type=MESH,
                        ).start()

    def await_partner(u, m, g):
        rows = 2 * len(groups[g])
        part = other[UNITS[u][0]].at[pl.ds(0, 1), pl.ds(0, 1), pl.ds(0, rows), pl.ds(0, 32)]
        pltpu.make_async_copy(part, part, core_recv.at[u, m, g]).wait()

    def own_loads(u, m, g):
        copies = []
        for slot, by in enumerate(groups[g]):
            parts = region(source_of(u, m), u, core, 0, place(u, by), axes_of(u)[:2])
            width = own[u].shape[-1] // len(parts)
            for i, src in enumerate(parts):
                copies.append(
                    pltpu.make_async_copy(src, own[u].at[slot, :, :, :, pl.ds(i * width, width)], own_sem.at[u, slot, i])
                )
        return copies

    def prefetch(m, g):
        for u in units_of(m):
            for c in own_loads(u, m, g):
                c.start()

    def add(u, phase, mats, where, half, terms, result=None):
        which, first, rows = UNITS[u][0], UNITS[u][1], 32
        if half is not None:
            first, rows = first + half * 16, 16
        whole = axes_of(u)[:phase]
        n_lo, n_y, _ = spread(whole)
        for i, (lo, y, cols) in enumerate(pieces(where, whole, WIDTHS[which])):

            @pl.loop(0, len(mats) * n_lo * n_y)
            def _(k, i=i, lo=lo, y=y, cols=cols):
                mat = mats[0] if len(mats) == 1 else lax.div(k, n_lo * n_y)
                a, b = lax.rem(lax.div(k, n_y), n_lo), lax.rem(k, n_y)
                here = (mat, lo.start + a, y.start + b, pl.ds(first, rows), cols)
                total = other[which][here].astype(F32)
                for term in terms:
                    total = total + term(mat, i, a, b).astype(F32)
                if result is None:
                    other[which][here] = total.astype(BF16)
                else:
                    result[mat, pl.ds(first, rows), :] = total

    def width_of(u, phase, ref):
        whole = axes_of(u)[:phase]
        return ref.shape[-1] // (2 if 2 in whole and 0 not in whole else 1)

    def from_own(u, slot, half=None):
        width = width_of(u, 2, own[u])
        rows = pl.ds(0, 32) if half is None else pl.ds(half * 16, 16)
        return lambda mat, i, a, b: own[u][slot, a, b, rows, pl.ds(i * width, width)]

    def from_buf(ref, side, u, phase):
        width = width_of(u, phase, ref)
        return lambda mat, i, a, b: ref[side, mat, a, b, :, pl.ds(i * width, width)]

    def mats_of(u, m):
        return pl.ds(index_of(u, m), 1)

    def send_step(u, phase, m, step):
        axes = axes_of(u)
        whole, axis = axes[:phase], axes[phase]
        index = 3 * index_of(u, m) + phase
        buf = half_buf[u][phase] if step == 0 else full_buf[u][phase]
        for side, by in ((0, 1), (1, -1)):
            where = moved(at, axis, 2 if step == 0 else by)
            sources = part_of(other[UNITS[u][0]], u, mats_of(u, m), where, whole, side if step == 0 else None)
            width = buf.shape[-1] // len(sources)
            for i, src in enumerate(sources):
                pltpu.make_async_remote_copy(
                    src_ref=src, dst_ref=buf.at[side, mats_of(u, m), :, :, :, pl.ds(i * width, width)],
                    send_sem=send.at[u, index, step], recv_sem=recv.at[u, index, step],
                    device_id=device(moved(at, axis, by), core), device_id_type=MESH,
                ).start()

    def await_step(u, phase, m, step, sem):
        index = 3 * index_of(u, m) + phase
        buf = half_buf[u][phase] if step == 0 else full_buf[u][phase]
        part = buf.at[:, mats_of(u, m)]
        pltpu.make_async_copy(part, part, sem.at[u, index, step]).wait()

    def stage(m, g):
        for u in units_of(m):
            for c in own_loads(u, m, g):
                c.wait()
            await_partner(u, m, g)
            mats = [index_of(u, m)]
            if g == 0:
                add(u, 2, mats, place(u, 2), None, [from_own(u, 0)])
                send_step(u, 2, m, 0)
            elif g == 1:
                await_step(u, 2, m, 0, recv)
                for side, by in ((0, 1), (1, -1)):
                    halves = [from_own(u, side, side), from_buf(half_buf[u][2], side, u, 2)]
                    add(u, 2, mats, place(u, by), side, halves)
                    add(u, 2, mats, place(u, by), 1 - side, [from_own(u, side, 1 - side)])
                send_step(u, 2, m, 1)
            else:
                await_step(u, 2, m, 1, recv)
                arrived = [from_buf(full_buf[u][2], side, u, 2) for side in (0, 1)]
                add(u, 2, mats, at, None, [from_own(u, 0)] + arrived)

    def later(m, phase, step):
        for u in units_of(m):
            axis, mats = axes_of(u)[phase], [index_of(u, m)]
            if step == 1:
                await_step(u, phase, m, 0, recv)
                for side, by in ((0, 1), (1, -1)):
                    add(u, phase, mats, moved(at, axis, by), side, [from_buf(half_buf[u][phase], side, u, phase)])
            elif step == 2:
                await_step(u, phase, m, 1, recv)
                arrived = [from_buf(full_buf[u][phase], side, u, phase) for side in (0, 1)]
                add(u, phase, mats, at, None, arrived, None if phase else outs[UNITS[u][0]])
            if step < 2:
                send_step(u, phase, m, step)

    def vec_copy(k):
        (x, y, z) = at
        flip = lambda v: v + 1 - 2 * lax.rem(v, 2)
        to = [
            device(at, 1 - core),
            device((flip(x), y, z), core),
            device((x, flip(y), z), core),
            device((x, y, flip(z)), core),
            device(moved(at, 0, 2), core),
            device(moved(at, 1, 2), core),
            device(moved(at, 2, 2), core),
        ][k]
        return pltpu.make_async_remote_copy(
            src_ref=vec_acc.at[k], dst_ref=vec_in.at[k], send_sem=vec_send.at[k], recv_sem=vec_recv.at[k],
            device_id=to, device_id_type=MESH,
        )

    def vec_step(k):
        if k:
            vec_copy(k - 1).wait_recv()
            vec_acc[k] = vec_acc[k - 1] + vec_in[k - 1]
        if k < VEC_STEPS:
            vec_copy(k).start()
        else:
            vec_out[...] = vec_acc[VEC_STEPS]

    prefetch(2, 0)
    to_partner(2)
    to_partner(1)
    for c in firsts:
        c.wait()
    first_out[:, :DI] = first_grad[...] * silu_slope(first_pre[...])
    first_out[:, DI:] = grad_bc[:8] * silu_slope(state_pre[:8])

    def halo_copy():
        return pltpu.make_async_remote_copy(
            src_ref=first_out, dst_ref=after, send_sem=halo_sem.at[0], recv_sem=halo_sem.at[1],
            device_id=tensor_peer(7), device_id_type=MESH,
        )

    @pl.when(t > 0)
    def _():
        halo_copy().start()

    docs = doc_col[...]
    links = [None] + [conv_links(docs, o, BLOCK + 8) for o in range(1, TAPS)]
    params = small_params(phead[...])
    vec = vec_acc.at[0]
    vec[...] = jnp.zeros(VEC, F32)

    stage(2, 0)
    prefetch(1, 0)

    @pl.when(t < 7)
    def _():
        halo_copy().wait_recv()

    @pl.when(t == 7)
    def _():
        after[...] = jnp.zeros_like(after)

    def conv_back(grad, grad_after, ext, taps):
        grad_ext = jnp.concatenate([grad, grad_after], 0)
        total = taps[TAPS - 1 : TAPS] * grad
        rows = [None] * TAPS
        rows[TAPS - 1] = jnp.sum(grad * ext[HALO:], axis=0, keepdims=True)
        for offset in range(1, TAPS):
            masked = grad_ext * links[offset]
            rows[TAPS - 1 - offset] = jnp.sum(masked[:BLOCK] * ext[HALO - offset : EXT - offset], axis=0, keepdims=True)
            total = total + taps[TAPS - 1 - offset : TAPS - offset] * masked[offset : offset + BLOCK]
        return total, rows + [jnp.sum(grad, axis=0, keepdims=True)]

    flat_main = [(lo, y, c) for lo in range(2) for y in range(4) for c in range(2)]

    def put(j, slot):
        cols = tile_of(j)
        return [
            pltpu.make_async_copy(
                staged.at[slot, pl.ds(i * ROWS, ROWS)], grad_main.at[0, lo, y, c, :, cols], put_sem.at[slot, i]
            )
            for i, (lo, y, c) in enumerate(flat_main)
        ]

    def x_tiles(first, last):
        @pl.loop(first, last)
        def _(j):
            slot = lax.rem(j, 2)
            cols = tile_of(j)

            @pl.when(j + 1 < TILES)
            def _():
                for c in stream(j + 1, 1 - slot):
                    c.start()

            for c in stream(j, slot):
                c.wait()
            grad = grad_in[slot] * silu_slope(pre_in[slot])
            total, rows = conv_back(grad, after[:, cols], ext_in[slot], pmain[0:TAPS, cols])
            for i, row in enumerate(rows):
                vec[i : i + 1, cols] = row
            total = total.astype(BF16)
            raw_x[:, cols] = total

            @pl.when(j >= 2)
            def _():
                for c in put(j, slot):
                    c.wait()

            staged[slot] = dot(normed_t[...], total).astype(BF16)
            for c in put(j, slot):
                c.start()

    def small_part():
        grad = grad_bc[...] * silu_slope(state_pre[...])
        total, rows = conv_back(grad, after[:, DI:], raw_ext[:, :256], params[:TAPS, :256])
        for i, row in enumerate(rows):
            vec[i : i + 1, DI : DI + 256] = row
        raw = jnp.concatenate([total.astype(BF16), grad_step_in[...].astype(BF16)], 1)
        acc[...] += dot(raw, w_small[...], (1, 1))
        small_acc[...] = dot(normed_t[...], raw).astype(BF16)
        packed = jnp.zeros((512, 8 * LANES), F32)
        for r in range(3):
            rows_r = jnp.concatenate([small_acc[pl.ds(d * 96 + r * 32, 32)] for d in range(16)], 0)
            packed = packed + dot(rows_r, small_map(r), (1, 1))
        small_out[...] = packed.astype(BF16)
        for c in small_puts:
            c.start()

    small_puts = [
        pltpu.make_async_copy(small_out.at[pl.ds(i * 32, 32)], grad_small.at[0, lo, y, c], small_sem.at[i])
        for i, (lo, y, c) in enumerate(flat_main)
    ]

    def input_tiles(first, last):
        @pl.loop(first, last)
        def _(k):
            slot = lax.rem(k, 2)

            def load(n, into):
                return pltpu.make_async_copy(full.at[0, :, tile_of(n)], w_in.at[into], w_sem.at[into])

            @pl.when(k + 1 < TILES)
            def _():
                load(k + 1, 1 - slot).start()

            load(k, slot).wait()
            acc[...] += dot(raw_x[:, tile_of(k)], w_in[slot], (1, 1))

    def input_grad():
        value = hidden[...].astype(F32)
        inv = lax.rsqrt(jnp.mean(value * value, axis=1, keepdims=True) + epsilon)
        rows = value * inv
        grad = acc[...]
        vec[5:6, 0:DI] = vec_gate[0:1, :]
        vec[6:7, 0:D] = jnp.sum(grad * rows, axis=0, keepdims=True)
        vec[5:8, DI + 256 :] = vec_heads[5:8, :]
        dn = grad * gain[...]
        mean = jnp.mean(dn * rows, axis=1, keepdims=True)
        grad_hidden[...] = cot[...].astype(F32) + inv * dn - rows * inv * mean

    for c in entering:
        c.wait()
    small_part()
    x_tiles(0, 1)
    stage(1, 0)
    prefetch(2, 1)
    x_tiles(1, 3)
    stage(2, 1)
    prefetch(1, 1)
    x_tiles(3, 5)
    stage(1, 1)
    prefetch(2, 2)
    x_tiles(5, 6)
    pltpu.make_async_copy(full.at[0, :, tile_of(0)], w_in.at[0], w_sem.at[0]).start()
    for slot in range(2):
        for c in put(TILES - 2 + slot, slot):
            c.wait()
    for c in small_puts:
        c.wait()
    to_partner(0)
    input_tiles(0, 3)
    stage(2, 2)
    prefetch(0, 0)
    later(2, 1, 0)
    input_tiles(3, 6)
    stage(0, 0)
    prefetch(1, 2)
    later(2, 1, 1)
    input_grad()
    vec_step(0)
    stage(1, 2)
    prefetch(0, 1)
    later(1, 1, 0)
    later(2, 1, 2)
    later(2, 0, 0)
    vec_step(1)
    stage(0, 1)
    prefetch(0, 2)
    later(1, 1, 1)
    later(2, 0, 1)
    vec_step(2)
    later(1, 1, 2)
    later(1, 0, 0)
    later(2, 0, 2)
    vec_step(3)
    later(1, 0, 1)
    stage(0, 2)
    later(0, 1, 0)
    vec_step(4)
    later(1, 0, 2)
    later(0, 1, 1)
    vec_step(5)
    later(0, 1, 2)
    later(0, 0, 0)
    vec_step(6)
    later(0, 0, 1)
    vec_step(7)
    later(0, 0, 2)
    for m in MATS:
        for u in units_of(m):
            part = other[UNITS[u][0]].at[pl.ds(0, 1), :, :, pl.ds(0, 32)]
            pltpu.make_async_copy(part, part, core_send.at[u, m]).wait()
            for phase in range(3):
                for step in (0, 1):
                    await_step(u, phase, m, step, send)
    for k in range(VEC_STEPS):
        vec_copy(k).wait_send()

    @pl.when(t > 0)
    def _():
        halo_copy().wait_send()


def back(*args):
    vmem = pl.BlockSpec(memory_space=VMEM)
    anywhere = pl.BlockSpec(memory_space=pl.ANY)
    units = range(SUMMED)
    n = SUMMED
    held = [(3, 2, 4, ROWS, 8 * WIDTH), (1, 2, 4, SMALL_ROWS, 8 * SMALL_WIDTH)]
    landing = [(2, STACK[UNITS[u][0]]) + region_shape(u, p, rows) for rows in (16, 32) for u in units for p in range(3)]
    return pl.pallas_call(
        back_kernel,
        name="project_back",
        out_shape=[
            jax.ShapeDtypeStruct((1, 2, 4, 2, ROWS, DI), BF16),
            jax.ShapeDtypeStruct((1, 2, 4, 2, SMALL_ROWS, 8 * LANES), BF16),
            jax.ShapeDtypeStruct((3, ROWS, WIDTH), F32),
            jax.ShapeDtypeStruct((1, SMALL_ROWS, SMALL_WIDTH), F32),
            jax.ShapeDtypeStruct((BLOCK, D), F32),
            jax.ShapeDtypeStruct(VEC, F32),
        ],
        in_specs=[vmem] * 10 + [anywhere] * 11,
        out_specs=[anywhere, anywhere, vmem, vmem, vmem, vmem],
        scratch_shapes=[VMEM(s, BF16) for s in held + landing]
        + [VMEM((2,) + region_shape(u, 2, 32), BF16) for u in units]
        + [
            VMEM((2, EXT, TILE), F32), VMEM((2, BLOCK, TILE), F32), VMEM((2, BLOCK, TILE), F32),
            VMEM((8, DI), F32), VMEM((8, DI), F32), VMEM((8, DI + 256), F32), VMEM((8, DI + 256), F32),
            VMEM((2, D, TILE), BF16), VMEM((2, D, TILE), BF16), VMEM((BLOCK, DI), BF16),
            VMEM((BLOCK, D), F32), VMEM((D, SMALL), BF16), VMEM((512, 8 * LANES), BF16),
            VMEM((VEC_STEPS + 1,) + VEC, F32), VMEM((VEC_STEPS,) + VEC, F32),
            VMEM((D, BLOCK), BF16), VMEM((D, SMALL), BF16), VMEM((BLOCK, D), BF16), VMEM((BLOCK, D), BF16),
        ]
        + [
            pltpu.SemaphoreType.DMA(s)
            for s in (
                (3, 2), (2,), (2,), (2,), (2, 16), (16,), (n, 2, 2), (VEC_STEPS,), (VEC_STEPS,), (n, 9, 2), (n, 9, 2),
                (n, 3), (n, 3, 3), (5,),
            )
        ],
        compiler_params=pltpu.CompilerParams(collective_id=3, has_side_effects=True, vmem_limit_bytes=62 * 2**20),
    )(*args)


def per_device(
    hidden,
    doc_ids,
    norm_gain,
    main_proj,
    step_proj,
    state_proj,
    conv_main,
    conv_main_bias,
    conv_state,
    conv_state_bias,
    step_bias,
    decay_log,
    skip_gain,
    gate_gain,
    out_proj,
    cotangent,
):
    shards, small, pmain, phead, doc_col, doc_row, gain = pack(
        main_proj, out_proj, state_proj.T, step_proj.T, conv_main, conv_main_bias, conv_state, conv_state_bias, step_bias,
        decay_log, skip_gain, gate_gain, norm_gain, doc_ids,
    )
    (pmain, phead, raw, state_pre, grad_bc, grad_step_in, vec_gate, vec_heads, mixed, normed_t, w_small, acc, grad_x,
     x_ext, x_pre, grad_out, grad_gate, full) = mid(
        hidden, gain, doc_col, doc_row, cotangent, shards, small, pmain, phead
    )
    _, _, own_main, own_small, grad_hidden, vec = back(
        raw, state_pre, grad_bc, grad_step_in, pmain, phead, doc_col, gain, vec_gate, vec_heads,
        normed_t, w_small, acc, hidden, cotangent, x_ext, x_pre, grad_x, grad_gate, grad_out, full.reshape(3, D, DI),
    )
    return (mixed, grad_hidden, *finish(own_main, own_small, vec))


def solution(mesh):
    placed = (
        P(("dp", "tensor"), None),
        P("dp"),
        P(),
        P("dp", None, "tensor"),
        P("dp", "tensor"),
        P("dp", "tensor"),
        P(None, "tensor"),
        P("tensor"),
        P(None, "tensor"),
        P("tensor"),
        P("tensor"),
        P("tensor"),
        P("tensor"),
        P("tensor"),
        P("dp", "tensor"),
        P(("dp", "tensor"), None),
    )
    return jax.shard_map(
        per_device,
        mesh=mesh,
        in_specs=placed,
        out_specs=(
            P(("dp", "tensor"), None),
            P(("dp", "tensor"), None),
            P(),
            P("dp", None, "tensor"),
            P("dp", "tensor"),
            P("dp", "tensor"),
            P(None, "tensor"),
            P("tensor"),
            P(None, "tensor"),
            P("tensor"),
            P("tensor"),
            P("tensor"),
            P("tensor"),
            P("tensor"),
            P("dp", "tensor"),
        ),
        check_vma=False,
    )
```

```python
import functools

import jax
import jax.numpy as jnp
from jax import lax
from jax.experimental import pallas as pl
from jax.experimental.pallas import tpu as pltpu
from jax.sharding import PartitionSpec as P

BLOCK = 256
epsilon = 1e-05

MESH = pl.DeviceIdType.MESH
AXES = (0, 1, 2)
SIDE = 4


def coordinates():
    dp = lax.axis_index("dp")
    t = lax.axis_index("tensor")
    z = lax.div(t, 4) * 2 + lax.div(dp, 8)
    return (lax.rem(t, 4), lax.rem(lax.div(dp, 2), 4), z), lax.rem(dp, 2)


def device(at, core):
    x, y, z = at
    return (lax.rem(z, 2) * 8 + y * 2 + core, lax.div(z, 2) * 4 + x)


def moved(at, axis, by):
    return tuple(lax.rem(v + by + SIDE, SIDE) if i == axis else v for i, v in enumerate(at))


def pieces(at, whole, width):
    x, y, z = at
    lo = pl.ds(0, 2) if 2 in whole else pl.ds(lax.rem(z, 2), 1)
    row = pl.ds(0, 4) if 1 in whole else pl.ds(y, 1)
    hi = lax.div(z, 2)
    if 0 in whole and 2 in whole:
        cols = [pl.ds(0, 8 * width)]
    elif 0 in whole:
        cols = [pl.ds(pl.multiple_of(hi * 4 * width, 128), 4 * width)]
    elif 2 in whole:
        cols = [
            pl.ds(pl.multiple_of(x * width, 128), width),
            pl.ds(pl.multiple_of((4 + x) * width, 128), width),
        ]
    else:
        cols = [pl.ds(pl.multiple_of((hi * 4 + x) * width, 128), width)]
    return [(lo, row, c) for c in cols]


def greet(at, core, group):
    barrier = pltpu.get_barrier_semaphore()
    others = [device(moved(at, axis, by), core) for axis in AXES for by in (1, -1)]
    others.append(device(at, 1 - core))
    others += group
    for other in others:
        pl.semaphore_signal(barrier, inc=1, device_id=other, device_id_type=MESH)
    pl.semaphore_wait(barrier, len(others))


def tensor_peer(by):
    return (lax.axis_index("dp"), lax.rem(lax.axis_index("tensor") + by, 8))


ROWS, WIDTH, SMALL_ROWS, SMALL_WIDTH = 96, 384, 32, 128
UNITS = [(0, q * 32, q) for q in range(3)] + [(1, 0, 0)]
SUMMED = len(UNITS)
WIDTHS = [WIDTH, SMALL_WIDTH]
STACK = [3, 1]


def axes_of(u):
    return [(UNITS[u][2] + j) % 3 for j in range(3)]


def region(ref, u, core, mats, where, whole, half=None):
    which, first, rows = UNITS[u][0], UNITS[u][1], 32
    if half is not None:
        first, rows = first + half * 16, 16
    return [
        ref.at[mats, lo, row, core, pl.ds(first, rows), cols]
        for lo, row, cols in pieces(where, whole, WIDTHS[which])
    ]


def sized(ref, u, mats, blocks, halves=2):
    width = WIDTHS[UNITS[u][0]]
    cols = min(blocks, 8)
    rest = blocks // cols
    return ref.at[mats, pl.ds(0, max(rest // 4, 1)), pl.ds(0, min(rest, 4)), 0, pl.ds(0, 16 * halves), pl.ds(0, cols * width)]


def gather_ops(full, send, recv, core_send, core_recv):
    at, core = coordinates()

    def sends(u, phase, mats, step, key):
        axes = axes_of(u)
        whole, axis = axes[:phase], axes[phase]
        for kind, by in ((0, 1), (1, -1)):
            where = at if step == 0 else moved(at, axis, -by)
            for part in region(full[UNITS[u][0]], u, core, mats, where, whole, kind if step else None):
                pltpu.make_async_remote_copy(
                    src_ref=part, dst_ref=part, send_sem=send.at[u, key, step], recv_sem=recv.at[u, key, step],
                    device_id=device(moved(at, axis, by), core), device_id_type=MESH,
                ).start()

    def await_step(u, phase, mats, step, key, sem):
        part = sized(full[UNITS[u][0]], u, mats, 2 * 4**phase // (1 + step))
        pltpu.make_async_copy(part, part, sem.at[u, key, step]).wait()

    def to_partner(u, mats, bys, key):
        axes = axes_of(u)
        for by in bys:
            where = moved(at, axes[2], by) if by else at
            for part in region(full[UNITS[u][0]], u, core, mats, where, axes[:2]):
                pltpu.make_async_remote_copy(
                    src_ref=part, dst_ref=part, send_sem=core_send.at[u, key], recv_sem=core_recv.at[u, key],
                    device_id=device(at, 1 - core), device_id_type=MESH,
                ).start()

    def await_partner(u, mats, key, sem):
        part = sized(full[UNITS[u][0]], u, mats, 64)
        pltpu.make_async_copy(part, part, sem.at[u, key]).wait()

    return sends, await_step, to_partner, await_partner


MAIN_UNITS = range(3)
ALL = pl.ds(0, 3)


D, DI, HEADS, HEAD_DIM, STATE, TAPS, HALO = 1536, 3072, 48, 64, 128, 4, 16
BF16, F32 = jnp.bfloat16, jnp.float32
TILE, LANES, SMALL = 512, 128, 384
TILES = DI // TILE
LOG2E = 1.4426950408889634
EXT = HALO + BLOCK
VMEM = pltpu.VMEM


def dot(a, b, dims=(1, 0), precision=None):
    return lax.dot_general(
        a, b, ((dims[:1], dims[1:]), ((), ())), precision=precision, preferred_element_type=F32
    )


def iota(shape, dim):
    return lax.broadcasted_iota(jnp.int32, shape, dim)


def sigmoid(v):
    return 1.0 / (1.0 + jnp.exp(-v))


def silu(v):
    return v * sigmoid(v)


def silu_slope(v):
    s = sigmoid(v)
    return s * (1.0 + v * (1.0 - s))


def softplus(v):
    return jnp.maximum(v, 0.0) + jnp.log1p(jnp.exp(-jnp.abs(v)))


def split(v):
    high = v.astype(BF16)
    return high, (v - high.astype(F32)).astype(BF16)


def head_map(j):
    return (iota((LANES, TILE), 0) == j * (TILE // HEAD_DIM) + iota((LANES, TILE), 1) // HEAD_DIM).astype(BF16)


def widen(v, j):
    high, low = split(v)
    return dot(high, head_map(j)) + dot(low, head_map(j))


def by_head(v, j):
    high, low = split(v)
    return dot(high, head_map(j), (1, 1)) + dot(low, head_map(j), (1, 1))


def small_map(r):
    row, col = iota((8 * LANES, SMALL), 0), iota((8 * LANES, SMALL), 1)
    t, lane = row // LANES, row % LANES - 38 * r
    state = (lane >= 0) & (lane < 32) & (col == t * 32 + lane)
    step = (lane >= 32) & (lane < 38) & (col == 256 + t * 6 + lane - 32)
    return (state | step).astype(BF16)


def tile_of(j):
    return pl.ds(pl.multiple_of(j * TILE, TILE), TILE)


def conv_links(doc_col, offset, rows):
    return (doc_col[HALO : HALO + rows] == doc_col[HALO - offset : HALO - offset + rows]).astype(F32)


def conv(ext, taps, bias, links):
    total = bias + taps[TAPS - 1 : TAPS] * ext[HALO:]
    for offset in range(1, TAPS):
        total = total + taps[TAPS - 1 - offset : TAPS - offset] * ext[HALO - offset : EXT - offset] * links[offset]
    return total


def small_params(phead):
    return dot(phead, small_map(0).astype(F32), precision=lax.Precision.HIGHEST)


def decay_terms(step, cum, doc_col, doc_prev):
    block = doc_col[HALO:EXT]
    end = cum[BLOCK - 1 : BLOCK]
    tail = jnp.exp(end - cum) * (block == block[BLOCK - 1 : BLOCK]).astype(F32)
    enter = jnp.exp(cum) * (block == doc_prev).astype(F32)
    keep = jnp.exp(end) * (block[BLOCK - 1 : BLOCK] == doc_prev).astype(F32)
    return enter, tail, tail * step, keep


def pack_kernel(
    main_proj, out_proj, state_proj, step_proj, conv_main, conv_main_bias, conv_state, conv_state_bias, step_bias,
    decay_log, skip_gain, gate_gain, norm_gain, doc_ids,
    shards, small, pmain, phead, doc_col, doc_row, gain, docs,
):
    t = lax.axis_index("tensor")
    shards[0] = main_proj[:, 1, :]
    shards[1] = main_proj[:, 0, :]
    shards[2] = out_proj[...]
    both = jnp.concatenate([state_proj[...].T, step_proj[...].T], 1)
    lanes = [both[r * 32 : r * 32 + 32] for r in range(3)]
    small[0] = jnp.concatenate(lanes + [jnp.zeros((SMALL_ROWS, 14), BF16)], 1)
    pmain[0:TAPS] = conv_main[...]
    pmain[TAPS : TAPS + 1] = conv_main_bias[...].reshape(1, WIDTH)
    pmain[5:6] = gate_gain[...].reshape(1, WIDTH)
    own_skip = skip_gain[...].reshape(1, 6)
    pmain[6:7] = jnp.concatenate([jnp.broadcast_to(own_skip[:, h : h + 1], (1, HEAD_DIM)) for h in range(6)], 1)
    pmain[7:8] = jnp.zeros((1, WIDTH), F32)
    phead[...] = jnp.zeros_like(phead)
    phead[0:TAPS, 0:32] = conv_state[...]
    phead[TAPS : TAPS + 1, 0:32] = conv_state_bias[...].reshape(1, 32)
    phead[5:6, 32:38] = step_bias[...].reshape(1, 6)
    phead[6:7, 32:38] = decay_log[...].reshape(1, 6)
    phead[7:8, 32:38] = own_skip
    gain[...] = norm_gain[...].reshape(1, D)
    docs[:, 0:LANES] = jnp.full((8, LANES), -1, jnp.int32)
    docs[:, LANES : LANES + 2048] = jnp.broadcast_to(doc_ids[...].reshape(1, 2048), (8, 2048))
    docs[:, LANES + 2048 :] = jnp.full((8, LANES), -2, jnp.int32)
    window = docs[:, pl.ds(pl.multiple_of(t * BLOCK, LANES), 2 * BLOCK)]
    doc_row[...] = window[0:1, LANES : LANES + BLOCK]
    doc_col[...] = window.T[LANES - HALO : LANES + BLOCK + 16, 0:1]


def pack(*args):
    vmem = pl.BlockSpec(memory_space=VMEM)
    shapes = [
        ((3, ROWS, WIDTH), BF16), ((1, SMALL_ROWS, SMALL_WIDTH), BF16), ((8, WIDTH), F32), ((8, LANES), F32),
        ((EXT + 16, 1), jnp.int32), ((1, BLOCK), jnp.int32), ((1, D), F32),
    ]
    return pl.pallas_call(
        pack_kernel,
        name="pack",
        out_shape=[jax.ShapeDtypeStruct(*s) for s in shapes],
        in_specs=[vmem] * 14,
        out_specs=[vmem] * len(shapes),
        scratch_shapes=[VMEM((8, 2048 + 2 * LANES), jnp.int32)],
    )(*args)


def finish_kernel(
    own_main, own_small, vec,
    norm_gain, main_proj, step_proj, state_proj, conv_main, conv_main_bias, conv_state, conv_state_bias, step_bias,
    decay_log, skip_gain, gate_gain, out_proj,
):
    t = lax.axis_index("tensor")
    main_proj[:, 0, :] = own_main[1]
    main_proj[:, 1, :] = own_main[0]
    out_proj[...] = own_main[2]
    packed = own_small[0]
    for r in range(3):
        rows_t = packed[:, r * 38 : r * 38 + 38].T
        state_proj[:, r * 32 : r * 32 + 32] = rows_t[:32]
        step_proj[:, r * 32 : r * 32 + 32] = rows_t[32:]
    own = vec[:, pl.ds(pl.multiple_of(t * WIDTH, LANES), WIDTH)]
    conv_main[...] = own[:TAPS]
    conv_main_bias[...] = own[TAPS : TAPS + 1].reshape(WIDTH)
    gate_gain[...] = own[5:6].reshape(WIDTH)
    state = pltpu.roll(vec[:, DI : DI + 256], lax.rem(256 - 32 * t, 256), axis=1)
    conv_state[...] = state[:TAPS, :32]
    conv_state_bias[...] = state[TAPS : TAPS + 1, :32].reshape(32)
    heads = pltpu.roll(vec[:, DI + 256 :], lax.rem(LANES - 6 * t, LANES), axis=1)
    step_bias[...] = heads[5:6, :6].reshape(6)
    decay_log[...] = heads[6:7, :6].reshape(6)
    skip_gain[...] = heads[7:8, :6].reshape(6)
    norm_gain[...] = vec[6:7, 0:D].reshape(D)


def finish(*args):
    vmem = pl.BlockSpec(memory_space=VMEM)
    shapes = [
        (D,), (ROWS, 2, WIDTH), (6, ROWS), (32, ROWS), (TAPS, WIDTH), (WIDTH,), (TAPS, 32), (32,), (6,), (6,), (6,),
        (WIDTH,), (ROWS, WIDTH),
    ]
    outs = pl.pallas_call(
        finish_kernel,
        name="finish",
        out_shape=[jax.ShapeDtypeStruct(s, F32) for s in shapes],
        in_specs=[vmem] * 3,
        out_specs=[vmem] * len(shapes),
    )(*args)
    return [v.T if i in (2, 3) else v for i, v in enumerate(outs)]


PAIR = 2 * HEAD_DIM
PAIRS = DI // PAIR
HALF = BLOCK // 2
CHUNK = 128
CHUNKS = DI // CHUNK
FORWARD_LAG, BACKWARD_LAG = 10, 4


def pair_of(p):
    return pl.ds(pl.multiple_of(p * PAIR, PAIR), PAIR)


def chunk_of(c):
    return pl.ds(pl.multiple_of(c * CHUNK, CHUNK), CHUNK)


def only(value, first):
    lane = iota(value.shape, 1)
    return jnp.where((lane < HEAD_DIM) == first, value, jnp.zeros_like(value))


def head_column(ref, h):
    return pltpu.roll(ref[...], lax.rem(LANES - h, LANES), axis=1)[:, :1]


def mid_kernel(
    hidden, gain, doc_col, doc_row, cot, shards, small, pmain_own, phead_own,
    pmain, phead, raw, state_pre, grad_bc, grad_step_in, vec_gate, vec_heads,
    mixed_out, normed_out, w_small_out, acc_out, grad_x_out, x_ext, x_pre, grad_out, grad_gate, full,
    mixed, normed_t, w_small, acc, grad_x, packed, halo, normed, w_in, ext_out, pre_out, staged, x_act, bc, scores, gate_in, work, y, gate_out, dy, gate_grad, update,
    grad_add, state, state_low, grad_state, keep_row, f_out, f_in, b_out, b_in, cot_t, mixed_acc,
    barred, cum2, cum_t, step_t, step_in, enter_ref, weight_ref, rows_acc, q_t, gs, acc_c, acc_heads, row_acc,
    w_sem, put_sem, x_sem, f_send, f_recv, b_send, b_recv, g_send, g_recv, core_send, core_recv, own_sem, halo_sem,
    param_send, param_recv, out_sem,
):
    t = lax.axis_index("tensor")

    def load(m, j, slot):
        return pltpu.make_async_copy(full.at[m, :, :, :, :, tile_of(j)], w_in.at[slot], w_sem.at[slot])

    def held(slot):
        return w_in[slot].reshape(D, TILE)

    at, core = coordinates()
    both = [full, packed]
    own = []
    for w, source in enumerate((shards, small)):
        for lo, row, cols in pieces(at, (), WIDTHS[w]):
            own.append(
                pltpu.make_async_copy(source, both[w].at[:, lo.start, row.start, core, :, cols], own_sem.at[w])
            )
    params_own, params_all = (pmain_own, phead_own), (pmain, phead)

    def columns(i, of):
        width = params_own[i].shape[-1]
        return params_all[i].at[:, pl.ds(pl.multiple_of(of * width, 128), width)]

    for i in range(2):
        own.append(pltpu.make_async_copy(params_own[i], columns(i, t), own_sem.at[2 + i]))
    for c in own:
        c.start()
    greet(at, core, [tensor_peer(by) for by in range(1, 8)])
    sends, await_step, to_partner, await_partner = gather_ops(both, g_send, g_recv, core_send, core_recv)

    def halo_copy():
        return pltpu.make_async_remote_copy(
            src_ref=hidden.at[pl.ds(BLOCK - HALO, HALO)], dst_ref=halo, send_sem=halo_sem.at[0],
            recv_sem=halo_sem.at[1], device_id=tensor_peer(1), device_id_type=MESH,
        )

    def param_copy(by, i, of):
        return pltpu.make_async_remote_copy(
            src_ref=params_own[i], dst_ref=columns(i, of), send_sem=param_send.at[i, by - 1],
            recv_sem=param_recv.at[i, by - 1], device_id=tensor_peer(by), device_id_type=MESH,
        )

    everything = [3, 0, 1, 2]

    def rms(rows, part):
        value = part[...].astype(F32)
        inv = lax.rsqrt(jnp.mean(value * value, axis=1, keepdims=True) + epsilon)
        normed[rows] = (value * inv * gain[...]).astype(BF16)

    def units_with(m):
        return [3] if m == 3 else MAIN_UNITS

    def gather_first(m):
        for u in units_with(m):
            sends(u, 2, pl.ds(m % 3, 1), 0, 2 + m % 3)

    def gather_near(m):
        for u in units_with(m):
            to_partner(u, pl.ds(m % 3, 1), [0], m % 3)

    def gather_forward(m):
        for u in units_with(m):
            await_step(u, 2, pl.ds(m % 3, 1), 0, 2 + m % 3, g_recv)
            sends(u, 2, pl.ds(m % 3, 1), 1, 2 + m % 3)

    def gather_second(m):
        for u in units_with(m):
            to_partner(u, pl.ds(m % 3, 1), [-1, 1], m % 3)

    def gather_last(m):
        for u in units_with(m):
            await_step(u, 2, pl.ds(m % 3, 1), 1, 2 + m % 3, g_recv)
            to_partner(u, pl.ds(m % 3, 1), [2], m % 3)

    def gather_done(m):
        for u in units_with(m):
            await_partner(u, pl.ds(m % 3, 1), m % 3, core_recv)

    one, others = pl.ds(0, 1), pl.ds(1, 2)
    for c in own:
        c.wait()
    for u in everything:
        sends(u, 0, one, 0, 0)
    halo_copy().start()
    for by in range(1, 8):
        for i in range(2):
            param_copy(by, i, t).start()
    for u in MAIN_UNITS:
        sends(u, 0, others, 0, 5)
    rms(pl.ds(HALO, BLOCK), hidden)
    for u in everything:
        await_step(u, 0, one, 0, 0, g_recv)
        sends(u, 0, one, 1, 0)
    for u in everything:
        await_step(u, 0, one, 1, 0, g_recv)
        sends(u, 1, one, 0, 1)
    for u in MAIN_UNITS:
        await_step(u, 0, others, 0, 5, g_recv)
        sends(u, 0, others, 1, 5)
    cot_t[...] = cot[...].T
    for u in everything:
        await_step(u, 1, one, 0, 1, g_recv)
        sends(u, 1, one, 1, 1)
    normed_t[...] = normed[pl.ds(HALO, BLOCK)].T
    leaving = [
        pltpu.make_async_copy(src, dst, out_sem.at[i])
        for i, (src, dst) in enumerate(
            ((normed_t, normed_out), (w_small, w_small_out), (acc, acc_out), (mixed, mixed_out))
        )
    ]
    leaving[0].start()

    def grad_x_put(j):
        return pltpu.make_async_copy(grad_x.at[:, tile_of(j)], grad_x_out.at[:, tile_of(j)], out_sem.at[4 + j])

    for u in everything:
        await_step(u, 1, one, 1, 1, g_recv)
        sends(u, 2, one, 0, 2)
    gather_near(3)
    gather_near(0)
    for u in MAIN_UNITS:
        await_step(u, 0, others, 1, 5, g_recv)
        sends(u, 1, others, 0, 6)
    halo_copy().wait()
    rms(pl.ds(0, HALO), halo)
    for by in range(1, 8):
        for i in range(2):
            param_copy(by, i, lax.rem(t + 8 - by, 8)).wait()
    gather_forward(3)
    gather_second(3)
    gather_forward(0)
    gather_second(0)
    for u in MAIN_UNITS:
        await_step(u, 1, others, 0, 6, g_recv)
        sends(u, 1, others, 1, 6)
    gather_last(3)
    gather_done(3)

    for r in range(3):
        rows = dot(packed[...].reshape(512, 8 * LANES), small_map(r)).astype(BF16)
        for d in range(16):
            w_small[pl.ds(d * 96 + r * 32, 32)] = rows[d * 32 : d * 32 + 32]
    raw[...] = dot(normed[...], w_small[...])
    leaving[1].start()
    for u in MAIN_UNITS:
        await_step(u, 1, others, 1, 6, g_recv)
        sends(u, 2, pl.ds(1, 1), 0, 3)
    gather_first(2)
    params = small_params(phead[...])
    docs = doc_col[...]
    links = [None] + [conv_links(docs, o, BLOCK) for o in range(1, TAPS)]
    pre = conv(raw[:, :256], params[:TAPS, :256], params[TAPS : TAPS + 1, :256], links)
    state_pre[...] = pre
    act = silu(pre).astype(BF16)
    bc[...] = act
    scores[...] = dot(act[:, STATE:], act[:, :STATE], (1, 1))
    step_in[...] = raw[HALO:, 256:] + params[5:6, 256:]
    rate = -jnp.exp(params[6:7, 256:])
    step = softplus(step_in[...])
    lower = (iota((BLOCK, BLOCK), 0) >= iota((BLOCK, BLOCK), 1)).astype(F32)
    cum = dot(lower, step * rate, precision=lax.Precision.HIGHEST)
    enter, tail, weight, keep = decay_terms(step, cum, docs, docs[HALO - 1 : HALO])
    enter_ref[...] = enter
    weight_ref[...] = weight
    cum2[...] = cum * LOG2E
    for ref, turned in ((cum_t, (cum * LOG2E).T), (step_t, step.T)):
        for h in range(HEADS):
            ref[h] = turned[h : h + 1]
    linked = (docs[HALO:EXT] == doc_row[...]) & (iota((BLOCK, BLOCK), 0) >= iota((BLOCK, BLOCK), 1))
    barred[...] = jnp.where(linked, 0.0, -1e30)
    keep8 = jnp.broadcast_to(keep, (8, LANES))

    gather_last(0)
    gather_near(1)
    gather_near(2)
    gather_done(0)
    load(0, 0, 0).start()

    def chain(forward, c, add, into, outgoing, incoming, send, recv):
        cols = chunk_of(c)
        by = 1 if forward else 7
        is_first = t == (0 if forward else 7)
        is_last = t == (7 if forward else 0)

        def copy():
            return pltpu.make_async_remote_copy(
                src_ref=outgoing.at[:, cols], dst_ref=incoming.at[:, cols], send_sem=send.at[c],
                recv_sem=recv.at[c], device_id=tensor_peer(by), device_id_type=MESH,
            )

        @pl.when(is_first)
        def _():
            into[:, cols] = jnp.zeros((STATE, CHUNK), F32)

        @pl.when(jnp.logical_not(is_first))
        def _():
            copy().wait_recv()
            into[:, cols] = incoming[:, cols].astype(F32)

        @pl.when(jnp.logical_not(is_last))
        def _():
            outgoing[:, cols] = (keep_row[0:1, cols] * into[:, cols] + add[:, cols]).astype(BF16)
            copy().start()

    def forward_slot(s):
        c = s - FORWARD_LAG * t

        @pl.when((c >= 0) & (c < CHUNKS))
        def _():
            chain(True, c, update, state, f_out, f_in, f_send, f_recv)

    def backward_slot(s):
        c = s - BACKWARD_LAG * (7 - t)

        @pl.when((c >= 0) & (c < CHUNKS))
        def _():
            chain(False, c, grad_add, grad_state, b_out, b_in, b_send, b_recv)

    def x_puts(j, slot):
        return [
            pltpu.make_async_copy(src.at[slot], dst.at[:, tile_of(j)], x_sem.at[i, slot])
            for i, (src, dst) in enumerate(((ext_out, x_ext), (pre_out, x_pre)))
        ]

    def x_tile(j):
        cols = tile_of(j)
        slot = lax.rem(j, 2)

        @pl.when(j + 1 < TILES)
        def _():
            load(0, j + 1, 1 - slot).start()

        @pl.when(j >= 2)
        def _():
            for c in x_puts(j, slot):
                c.wait()

        load(0, j, slot).wait()
        ext = dot(normed[...], held(slot))
        ext_out[slot] = ext
        pre = conv(ext, pmain[0:TAPS, cols], pmain[TAPS : TAPS + 1, cols], links)
        pre_out[slot] = pre
        for c in x_puts(j, slot):
            c.start()
        act = silu(pre).astype(BF16)
        x_act[:, cols] = act
        heavy = (act.astype(F32) * widen(weight_ref[...], j)).astype(BF16)
        update[:, cols] = dot(bc[:, :STATE], heavy, (0, 0))
        keep_row[:, cols] = widen(keep8, j)
        for k in range(4):
            forward_slot(4 * j + k)

    gather_forward(1)
    gather_second(1)
    pl.loop(0, 3)(x_tile)
    gather_forward(2)
    gather_second(2)
    pl.loop(3, TILES)(x_tile)
    for slot in range(2):
        for c in x_puts(TILES - 2 + slot, slot):
            c.wait()

    halves = [(slice(0, HALF), slice(0, HALF)), (slice(HALF, BLOCK), slice(0, BLOCK))]

    def decay_of(h, column, rows, cols):
        return jnp.exp2(column[rows] - cum_t[h, :, cols] + barred[rows, cols])

    def intra_forward(p):
        cols = pair_of(p)
        x = x_act[:, cols]
        x2 = [only(x, True), only(x, False)]
        columns = [head_column(cum2, 2 * p + k) for k in (0, 1)]
        for rows, js in halves:
            mix = [
                (scores[rows, js] * (decay_of(2 * p + k, columns[k], rows, js) * step_t[2 * p + k, :, js])).astype(BF16)
                for k in (0, 1)
            ]
            y[rows, cols] = dot(jnp.concatenate(mix, 1), jnp.concatenate([v[js] for v in x2], 0))

    def scan_pairs(first, last):
        @pl.loop(first, last)
        def _(i):
            forward_slot(4 * TILES + 2 * i)
            intra_forward(i)
            forward_slot(4 * TILES + 2 * i + 1)

    def gate_tile(j, slot):
        gate_in[:, tile_of(j)] = dot(normed[pl.ds(HALO, BLOCK)], held(slot))

    def out_tile(j, slot):
        work[:, tile_of(j)] = dot(cot[...], held(slot))

    def tile_step(m, j, use):
        slot = lax.rem(j, 2)

        @pl.when(j + 1 < TILES)
        def _():
            load(m, j + 1, 1 - slot).start()

        load(m, j, slot).wait()
        use(j, slot)

    scan_pairs(0, 8)
    gather_last(1)
    scan_pairs(8, 12)
    gather_last(2)
    gather_done(1)
    load(1, 0, 0).start()

    @pl.loop(0, TILES)
    def _(j):
        for k in range(2):
            i = 12 + 2 * j + k
            forward_slot(4 * TILES + 2 * i)
            intra_forward(i)
            forward_slot(4 * TILES + 2 * i + 1)
        tile_step(1, j, gate_tile)

    base = 4 * TILES + 2 * PAIRS
    gather_done(2)
    load(2, 0, 0).start()

    @pl.loop(0, TILES)
    def _(j):
        forward_slot(base + j)
        tile_step(2, j, out_tile)

    base = base + TILES

    load(2, 0, 1).start()
    load(1, 0, 0).start()
    row_acc[...] = jnp.zeros_like(row_acc)

    @pl.loop(0, TILES)
    def _(j):
        @pl.loop(0, TILE // CHUNK)
        def _(k):
            c = j * (TILE // CHUNK) + k

            @pl.when(c + FORWARD_LAG * t >= base)
            def _():
                chain(True, c, update, state, f_out, f_in, f_send, f_recv)

        cols = tile_of(j)
        low = state[:, cols].astype(BF16)
        state_low[:, cols] = low
        carried = dot(bc[:, STATE:], low)
        value = y[:, cols] + carried * widen(enter_ref[...], j) + pmain[6:7, cols] * x_act[:, cols].astype(F32)
        y[:, cols] = value
        gated = value * silu(gate_in[:, cols])
        row_acc[...] += jnp.broadcast_to(jnp.sum(gated * gated, axis=1, keepdims=True), (BLOCK, LANES))

    gate_inv = lax.rsqrt(row_acc[:, :1] / DI + epsilon)
    row_acc[...] = jnp.zeros_like(row_acc)

    @pl.loop(0, TILES)
    def _(j):
        cols = tile_of(j)
        gated = y[:, cols] * silu(gate_in[:, cols])
        hat = gated * gate_inv
        gate_gain = pmain[5:6, cols]
        gate_out[:, cols] = (hat * gate_gain).astype(BF16)
        grad = work[:, cols]
        vec_gate[:, cols] = jnp.broadcast_to(jnp.sum(grad * hat, axis=0, keepdims=True), (8, TILE))
        dn = grad * gate_gain
        work[:, cols] = dn
        row_acc[...] += jnp.broadcast_to(jnp.sum(dn * gated, axis=1, keepdims=True), (BLOCK, LANES))

    inner = row_acc[:, :1] / DI * gate_inv * gate_inv * gate_inv
    acc_c[...] = jnp.zeros_like(acc_c)
    acc_heads[...] = jnp.zeros_like(acc_heads)

    @pl.loop(0, TILES)
    def _(j):
        cols = tile_of(j)
        gate, value = gate_in[:, cols], y[:, cols]
        s = sigmoid(gate)
        act = gate * s
        grad_gated = gate_inv * work[:, cols] - value * act * inner
        grad = (grad_gated * act).astype(BF16)
        dy[:, cols] = grad
        gate_grad[:, cols] = (grad_gated * value * (s * (1.0 + gate * (1.0 - s)))).astype(BF16)
        grad = grad.astype(F32)
        carried_grad = (grad * widen(enter_ref[...], j)).astype(BF16)
        low = state_low[:, cols]
        grad_add[:, cols] = dot(bc[:, STATE:], carried_grad, (0, 0))
        acc_c[...] += dot(carried_grad, low, (1, 1))
        acc_heads[0] += by_head(grad * dot(bc[:, STATE:], low), j)

    rows_acc[...] = jnp.zeros_like(rows_acc)
    gs[...] = jnp.zeros_like(gs)
    acc[...] = jnp.zeros_like(acc)
    mixed_acc[...] = jnp.zeros_like(mixed_acc)

    def intra_backward(p):
        cols = pair_of(p)
        x, grad = x_act[:, cols], dy[:, cols]
        grad2 = [only(grad, True), only(grad, False)]
        columns = [head_column(cum2, 2 * p + k) for k in (0, 1)]
        lane = iota((HALF, LANES), 1)
        parts = []
        q_rows = [[], []]
        for rows, js in halves:
            mixes = []
            gs_sum = gs[rows, js]
            pulls = jnp.zeros((HALF, LANES), F32)
            for k in (0, 1):
                h = 2 * p + k
                decay = decay_of(h, columns[k], rows, js)
                decay_step = decay * step_t[h, :, js]
                mixes.append((scores[rows, js] * decay_step).astype(BF16))
                grad_mix = dot(grad2[k][rows], x[js], (1, 1))
                gs_sum = gs_sum + grad_mix * decay_step
                q = grad_mix * scores[rows, js] * decay
                q_rows[k].append(jnp.sum(q, axis=0, keepdims=True))
                pull = jnp.sum(q * step_t[h, :, js], axis=1, keepdims=True)
                pulls = jnp.where(lane == h, pull, pulls)
            gs[rows, js] = gs_sum
            rows_acc[rows] += pulls
            parts.append(dot(jnp.concatenate(mixes, 0), jnp.concatenate([v[rows] for v in grad2], 0), (0, 0)))
        grad_x[pl.ds(0, HALF), cols] = parts[0] + parts[1][:HALF]
        grad_x[pl.ds(HALF, HALF), cols] = parts[1][HALF:]
        for k in (0, 1):
            first, second = q_rows[k]
            q_t[2 * p + k, :, 0:HALF] = first + second[:, :HALF]
            q_t[2 * p + k, :, HALF:BLOCK] = second[:, HALF:]

    def put(ref, j, slot):
        return [
            pltpu.make_async_copy(
                staged.at[slot, pl.ds(i * ROWS, ROWS)], ref.at[0, lo, y_, c, :, tile_of(j)], put_sem.at[slot, i]
            )
            for i, (lo, y_, c) in enumerate((lo, y_, c) for lo in range(2) for y_ in range(4) for c in range(2))
        ]

    def put_tile(ref, j, slot, lhs, grad):
        @pl.when(j >= 1)
        def _():
            for c in put(ref, j, slot):
                c.wait()

        staged[slot] = dot(lhs[...], grad).astype(BF16)
        for c in put(ref, j, slot):
            c.start()

    @pl.loop(0, PAIRS)
    def _(i):
        backward_slot(2 * i)
        intra_backward(i)
        backward_slot(2 * i + 1)
        j = lax.div(i, 4)
        cols = tile_of(j)

        @pl.when(lax.rem(i, 4) == 0)
        def _():
            put_tile(grad_out, j, 0, cot_t, gate_out[:, cols])

        @pl.when(lax.rem(i, 4) == 1)
        def _():
            put_tile(grad_gate, j, 1, normed_t, gate_grad[:, cols])

        @pl.when(lax.rem(i, 4) == 2)
        def _():
            load(2, j, 1).wait()
            mixed_acc[...] += dot(gate_out[:, cols], held(1), (1, 1))

            @pl.when(j + 1 < TILES)
            def _():
                load(2, j + 1, 1).start()

        @pl.when(lax.rem(i, 4) == 3)
        def _():
            load(1, j, 0).wait()
            acc[...] += dot(gate_grad[:, cols], held(0), (1, 1))

            @pl.when(j + 1 < TILES)
            def _():
                load(1, j + 1, 0).start()

    leaving[2].start()
    mixed[...] = (hidden[...].astype(F32) + mixed_acc[...]).astype(BF16)
    leaving[3].start()
    gs_low = gs[...].astype(BF16)
    grad_bc[:, STATE:] = acc_c[...] + dot(gs_low, bc[:, :STATE])
    acc_c[...] = dot(gs_low, bc[:, STATE:], (0, 0))

    @pl.loop(0, TILES)
    def _(j):
        @pl.loop(0, TILE // CHUNK)
        def _(k):
            c = j * (TILE // CHUNK) + k

            @pl.when(c + BACKWARD_LAG * (7 - t) >= 2 * PAIRS)
            def _():
                chain(False, c, grad_add, grad_state, b_out, b_in, b_send, b_recv)

        cols = tile_of(j)
        wide = widen(weight_ref[...], j)
        grad_update = grad_state[:, cols].astype(BF16)
        spread_grad = dot(bc[:, :STATE], grad_update)
        x, grad = x_act[:, cols].astype(F32), dy[:, cols].astype(F32)
        grad_x[:, cols] += wide * spread_grad + pmain[6:7, cols] * grad
        grad_x_put(j).start()
        acc_heads[1] += by_head(x * spread_grad, j)
        acc_c[...] += dot((x * wide).astype(BF16), grad_update, (1, 1))
        kept = jnp.sum(grad_state[:, cols] * state[:, cols], axis=0, keepdims=True)
        skip = jnp.sum(x * grad, axis=0, keepdims=True)
        row = iota((8, TILE), 0)
        both = jnp.where(row == 0, kept, jnp.where(row == 1, skip, 0.0))
        acc_heads[2, 0:8] += by_head(both, j)

    grad_bc[:, :STATE] = acc_c[...]
    grad_weight = acc_heads[1]
    none = jnp.zeros((LANES - HEADS, BLOCK), F32)
    step = jnp.concatenate([step_t[h] for h in range(HEADS)] + [none], 0).T
    q = jnp.concatenate([q_t[h] for h in range(HEADS)] + [none], 0).T
    weight_pull = grad_weight * weight_ref[...]
    grad_end = jnp.sum(weight_pull, axis=0, keepdims=True) + acc_heads[2, 0:1] * keep
    grad_cum = rows_acc[...] - step * q + enter_ref[...] * acc_heads[0] - weight_pull
    grad_cum = grad_cum + jnp.where(iota((BLOCK, LANES), 0) == BLOCK - 1, grad_end, 0.0)
    upper = (iota((BLOCK, BLOCK), 0) <= iota((BLOCK, BLOCK), 1)).astype(F32)
    grad_log = dot(upper, grad_cum, precision=lax.Precision.HIGHEST)
    grad_step = q + grad_weight * tail + rate * grad_log
    grad_in = grad_step * sigmoid(step_in[...])
    grad_step_in[...] = grad_in
    row = iota((8, LANES), 0)
    heads = jnp.where(row == 5, jnp.sum(grad_in, axis=0, keepdims=True), 0.0)
    heads = jnp.where(row == 6, rate * jnp.sum(grad_log * step, axis=0, keepdims=True), heads)
    vec_heads[...] = jnp.where(row == 7, acc_heads[2, 1:2], heads)

    for c in leaving:
        c.wait()
    for j in range(TILES):
        grad_x_put(j).wait()
    for u in everything:
        for step in (0, 1):
            for phase in (0, 1):
                await_step(u, phase, one, step, phase, g_send)
                if u in MAIN_UNITS:
                    await_step(u, phase, others, step, 5 + phase, g_send)
    for m in range(4):
        for u in units_with(m):
            await_partner(u, pl.ds(m % 3, 1), m % 3, core_send)
            for step in (0, 1):
                await_step(u, 2, pl.ds(m % 3, 1), step, 2 + m % 3, g_send)
    for slot, ref in ((0, grad_out), (1, grad_gate)):
        for c in put(ref, TILES - 1, slot):
            c.wait()
    for by, ends, outgoing, incoming, send, recv in (
        (1, 7, f_out, f_in, f_send, f_recv),
        (7, 0, b_out, b_in, b_send, b_recv),
    ):

        @pl.when(t != ends)
        def _(by=by, outgoing=outgoing, incoming=incoming, send=send, recv=recv):
            @pl.loop(0, CHUNKS)
            def _(c):
                pltpu.make_async_remote_copy(
                    src_ref=outgoing.at[:, chunk_of(c)], dst_ref=incoming.at[:, chunk_of(c)], send_sem=send.at[c],
                    recv_sem=recv.at[c], device_id=tensor_peer(by), device_id_type=MESH,
                ).wait_send()


def mid(*args):
    vmem = pl.BlockSpec(memory_space=VMEM)
    anywhere = pl.BlockSpec(memory_space=pl.ANY)
    wide, heads, square = (BLOCK, DI), (BLOCK, LANES), (BLOCK, BLOCK)
    turned, own_state = (HEADS, 1, BLOCK), (STATE, DI)
    blocks = (1, 2, 4, 2, ROWS, DI)
    shapes = [
        ((8, DI), F32), ((8, 8 * LANES), F32), ((EXT, SMALL), F32), (square, F32), (square, F32), (heads, F32),
        ((8, DI), F32), ((8, LANES), F32),
    ]
    moved_out = [((BLOCK, D), BF16), ((D, BLOCK), BF16), ((D, SMALL), BF16), ((BLOCK, D), F32), (wide, F32)]
    in_hbm = [((EXT, DI), F32), (wide, F32), (blocks, BF16), (blocks, BF16), ((3,) + blocks[1:], BF16)]
    scratch = [
        ((1, 2, 4, 2, SMALL_ROWS, 8 * LANES), BF16), ((HALO, D), BF16), ((EXT, D), BF16), ((2, 2, 4, 2, ROWS, TILE), BF16), ((2, EXT, TILE), F32), ((2, BLOCK, TILE), F32), ((2, D, TILE), BF16),
        (wide, BF16), ((BLOCK, 2 * STATE), BF16), (square, F32), (wide, F32), (wide, F32), (wide, F32), (wide, BF16),
        (wide, BF16), (wide, BF16), (own_state, F32), (own_state, F32), (own_state, F32), (own_state, BF16),
        (own_state, F32), ((8, DI), F32), (own_state, BF16), (own_state, BF16), (own_state, BF16), (own_state, BF16),
        ((D, BLOCK), BF16), ((BLOCK, D), F32),
        (square, F32), (heads, F32), (turned, F32), (turned, F32), (heads, F32), (heads, F32), (heads, F32),
        (heads, F32), (turned, F32), (square, F32), (heads, F32), ((3,) + heads, F32), (heads, F32),
    ]
    return pl.pallas_call(
        mid_kernel,
        name="scan_and_gate",
        out_shape=[jax.ShapeDtypeStruct(*s) for s in shapes + moved_out + in_hbm],
        in_specs=[vmem] * 5 + [anywhere] * 4,
        out_specs=[vmem] * 8 + [anywhere] * 10,
        scratch_shapes=[VMEM(*s) for s in moved_out + scratch]
        + [pltpu.SemaphoreType.DMA((2,)), pltpu.SemaphoreType.DMA((2, 16)), pltpu.SemaphoreType.DMA((2, 2))]
        + [pltpu.SemaphoreType.DMA((CHUNKS,))] * 4
        + [pltpu.SemaphoreType.DMA((len(UNITS), 7, 2))] * 2
        + [pltpu.SemaphoreType.DMA((len(UNITS), 3))] * 2
        + [pltpu.SemaphoreType.DMA(s) for s in ((4,), (2,), (2, 7), (2, 7), (4 + TILES,))],
        compiler_params=pltpu.CompilerParams(
            collective_id=1, has_side_effects=True, vmem_limit_bytes=60 * 2**20
        ),
    )(*args)


VEC = (8, 8 * WIDTH + 384)
VEC_STEPS = 7
MATS = (2, 1, 0)


def spread(whole):
    return (2 if 2 in whole else 1, 4 if 1 in whole else 1, (4 if 0 in whole else 1) * (2 if 2 in whole else 1))


def region_shape(u, phase, rows):
    lo, y, cols = spread(axes_of(u)[:phase])
    return (lo, y, rows, cols * WIDTHS[UNITS[u][0]])


def back_kernel(*refs):
    refs = list(refs)

    def take(n):
        got = refs[:n]
        del refs[:n]
        return got

    (raw_ext, state_pre, grad_bc, grad_step_in, pmain, phead, doc_col, gain, vec_gate, vec_heads,
     normed_in, w_small_in, acc_in, hidden_in, cot_in, x_ext, x_pre, grad_x, grad_gate, grad_out, full) = take(21)
    grad_main, grad_small, out_main, out_small, grad_hidden, vec_out = take(6)
    outs = (out_main, out_small)
    units = SUMMED
    other = take(2)
    half_buf = [take(3) for _ in range(units)]
    full_buf = [take(3) for _ in range(units)]
    own = take(units)
    (ext_in, pre_in, grad_in, first_grad, first_pre, first_out, after, w_in, staged, raw_x, acc, small_acc,
     small_out, vec_acc, vec_in, normed_t, w_small, hidden, cot) = take(19)
    (stream_sem, first_sem, halo_sem, w_sem, put_sem, small_sem, own_sem, vec_send, vec_recv, send, recv, core_send,
     core_recv, entry_sem) = take(14)
    at, core = coordinates()
    t = lax.axis_index("tensor")
    everything = range(units)

    def stream(j, slot):
        cols = tile_of(j)
        return [
            pltpu.make_async_copy(src.at[:, cols], dst.at[slot], stream_sem.at[i, slot])
            for i, (src, dst) in enumerate(((x_ext, ext_in), (x_pre, pre_in), (grad_x, grad_in)))
        ]

    firsts = [
        pltpu.make_async_copy(src.at[pl.ds(0, 8)], dst, first_sem.at[i])
        for i, (src, dst) in enumerate(((grad_x, first_grad), (x_pre, first_pre)))
    ]
    entering = [
        pltpu.make_async_copy(src, dst, entry_sem.at[i])
        for i, (src, dst) in enumerate(
            ((normed_in, normed_t), (w_small_in, w_small), (acc_in, acc), (hidden_in, hidden), (cot_in, cot))
        )
    ]
    for c in firsts + stream(0, 0) + entering:
        c.start()
    greet(at, core, [device(moved(at, axis, 2), core) for axis in AXES] + [tensor_peer(1), tensor_peer(7)])

    def source_of(u, m):
        return grad_small if UNITS[u][0] else (grad_main, grad_gate, grad_out)[m]

    def units_of(m):
        return [u for u in everything if m == 0 or UNITS[u][0] == 0]

    def index_of(u, m):
        return 0 if UNITS[u][0] else m

    def part_of(ref, u, mats, where, whole, half=None):
        which, first, rows = UNITS[u][0], UNITS[u][1], 32
        if half is not None:
            first, rows = first + half * 16, 16
        return [ref.at[mats, lo, y, pl.ds(first, rows), cols] for lo, y, cols in pieces(where, whole, WIDTHS[which])]

    def place(u, by):
        return moved(at, axes_of(u)[2], by) if by else at

    groups = [[2], [1, -1], [0]]

    def to_partner(m):
        for g, group in enumerate(groups):
            for u in units_of(m):
                for by in group:
                    whole = axes_of(u)[:2]
                    for src, dst in zip(
                        region(source_of(u, m), u, 1 - core, pl.ds(0, 1), place(u, by), whole),
                        part_of(other[UNITS[u][0]], u, pl.ds(index_of(u, m), 1), place(u, by), whole),
                    ):
                        pltpu.make_async_remote_copy(
                            src_ref=src, dst_ref=dst, send_sem=core_send.at[u, m], recv_sem=core_recv.at[u, m, g],
                            device_id=device(at, 1 - core), device_id_type=MESH,
                        ).start()

    def await_partner(u, m, g):
        rows = 2 * len(groups[g])
        part = other[UNITS[u][0]].at[pl.ds(0, 1), pl.ds(0, 1), pl.ds(0, rows), pl.ds(0, 32)]
        pltpu.make_async_copy(part, part, core_recv.at[u, m, g]).wait()

    def own_loads(u, m, g):
        copies = []
        for slot, by in enumerate(groups[g]):
            parts = region(source_of(u, m), u, core, 0, place(u, by), axes_of(u)[:2])
            width = own[u].shape[-1] // len(parts)
            for i, src in enumerate(parts):
                copies.append(
                    pltpu.make_async_copy(src, own[u].at[slot, :, :, :, pl.ds(i * width, width)], own_sem.at[u, slot, i])
                )
        return copies

    def prefetch(m, g):
        for u in units_of(m):
            for c in own_loads(u, m, g):
                c.start()

    def add(u, phase, mats, where, half, terms, result=None):
        which, first, rows = UNITS[u][0], UNITS[u][1], 32
        if half is not None:
            first, rows = first + half * 16, 16
        whole = axes_of(u)[:phase]
        n_lo, n_y, _ = spread(whole)
        for i, (lo, y, cols) in enumerate(pieces(where, whole, WIDTHS[which])):

            @pl.loop(0, len(mats) * n_lo * n_y)
            def _(k, i=i, lo=lo, y=y, cols=cols):
                mat = mats[0] if len(mats) == 1 else lax.div(k, n_lo * n_y)
                a, b = lax.rem(lax.div(k, n_y), n_lo), lax.rem(k, n_y)
                here = (mat, lo.start + a, y.start + b, pl.ds(first, rows), cols)
                total = other[which][here].astype(F32)
                for term in terms:
                    total = total + term(mat, i, a, b).astype(F32)
                if result is None:
                    other[which][here] = total.astype(BF16)
                else:
                    result[mat, pl.ds(first, rows), :] = total

    def width_of(u, phase, ref):
        whole = axes_of(u)[:phase]
        return ref.shape[-1] // (2 if 2 in whole and 0 not in whole else 1)

    def from_own(u, slot, half=None):
        width = width_of(u, 2, own[u])
        rows = pl.ds(0, 32) if half is None else pl.ds(half * 16, 16)
        return lambda mat, i, a, b: own[u][slot, a, b, rows, pl.ds(i * width, width)]

    def from_buf(ref, side, u, phase):
        width = width_of(u, phase, ref)
        return lambda mat, i, a, b: ref[side, mat, a, b, :, pl.ds(i * width, width)]

    def mats_of(u, m):
        return pl.ds(index_of(u, m), 1)

    def send_step(u, phase, m, step):
        axes = axes_of(u)
        whole, axis = axes[:phase], axes[phase]
        index = 3 * index_of(u, m) + phase
        buf = half_buf[u][phase] if step == 0 else full_buf[u][phase]
        for side, by in ((0, 1), (1, -1)):
            where = moved(at, axis, 2 if step == 0 else by)
            sources = part_of(other[UNITS[u][0]], u, mats_of(u, m), where, whole, side if step == 0 else None)
            width = buf.shape[-1] // len(sources)
            for i, src in enumerate(sources):
                pltpu.make_async_remote_copy(
                    src_ref=src, dst_ref=buf.at[side, mats_of(u, m), :, :, :, pl.ds(i * width, width)],
                    send_sem=send.at[u, index, step], recv_sem=recv.at[u, index, step],
                    device_id=device(moved(at, axis, by), core), device_id_type=MESH,
                ).start()

    def await_step(u, phase, m, step, sem):
        index = 3 * index_of(u, m) + phase
        buf = half_buf[u][phase] if step == 0 else full_buf[u][phase]
        part = buf.at[:, mats_of(u, m)]
        pltpu.make_async_copy(part, part, sem.at[u, index, step]).wait()

    def stage(m, g):
        for u in units_of(m):
            for c in own_loads(u, m, g):
                c.wait()
            await_partner(u, m, g)
            mats = [index_of(u, m)]
            if g == 0:
                add(u, 2, mats, place(u, 2), None, [from_own(u, 0)])
                send_step(u, 2, m, 0)
            elif g == 1:
                await_step(u, 2, m, 0, recv)
                for side, by in ((0, 1), (1, -1)):
                    halves = [from_own(u, side, side), from_buf(half_buf[u][2], side, u, 2)]
                    add(u, 2, mats, place(u, by), side, halves)
                    add(u, 2, mats, place(u, by), 1 - side, [from_own(u, side, 1 - side)])
                send_step(u, 2, m, 1)
            else:
                await_step(u, 2, m, 1, recv)
                arrived = [from_buf(full_buf[u][2], side, u, 2) for side in (0, 1)]
                add(u, 2, mats, at, None, [from_own(u, 0)] + arrived)

    def later(m, phase, step):
        for u in units_of(m):
            axis, mats = axes_of(u)[phase], [index_of(u, m)]
            if step == 1:
                await_step(u, phase, m, 0, recv)
                for side, by in ((0, 1), (1, -1)):
                    add(u, phase, mats, moved(at, axis, by), side, [from_buf(half_buf[u][phase], side, u, phase)])
            elif step == 2:
                await_step(u, phase, m, 1, recv)
                arrived = [from_buf(full_buf[u][phase], side, u, phase) for side in (0, 1)]
                add(u, phase, mats, at, None, arrived, None if phase else outs[UNITS[u][0]])
            if step < 2:
                send_step(u, phase, m, step)

    def vec_copy(k):
        (x, y, z) = at
        flip = lambda v: v + 1 - 2 * lax.rem(v, 2)
        to = [
            device(at, 1 - core),
            device((flip(x), y, z), core),
            device((x, flip(y), z), core),
            device((x, y, flip(z)), core),
            device(moved(at, 0, 2), core),
            device(moved(at, 1, 2), core),
            device(moved(at, 2, 2), core),
        ][k]
        return pltpu.make_async_remote_copy(
            src_ref=vec_acc.at[k], dst_ref=vec_in.at[k], send_sem=vec_send.at[k], recv_sem=vec_recv.at[k],
            device_id=to, device_id_type=MESH,
        )

    def vec_step(k):
        if k:
            vec_copy(k - 1).wait_recv()
            vec_acc[k] = vec_acc[k - 1] + vec_in[k - 1]
        if k < VEC_STEPS:
            vec_copy(k).start()
        else:
            vec_out[...] = vec_acc[VEC_STEPS]

    prefetch(2, 0)
    to_partner(2)
    to_partner(1)
    for c in firsts:
        c.wait()
    first_out[:, :DI] = first_grad[...] * silu_slope(first_pre[...])
    first_out[:, DI:] = grad_bc[:8] * silu_slope(state_pre[:8])

    def halo_copy():
        return pltpu.make_async_remote_copy(
            src_ref=first_out, dst_ref=after, send_sem=halo_sem.at[0], recv_sem=halo_sem.at[1],
            device_id=tensor_peer(7), device_id_type=MESH,
        )

    @pl.when(t > 0)
    def _():
        halo_copy().start()

    docs = doc_col[...]
    links = [None] + [conv_links(docs, o, BLOCK + 8) for o in range(1, TAPS)]
    params = small_params(phead[...])
    vec = vec_acc.at[0]
    vec[...] = jnp.zeros(VEC, F32)

    stage(2, 0)
    prefetch(1, 0)

    @pl.when(t < 7)
    def _():
        halo_copy().wait_recv()

    @pl.when(t == 7)
    def _():
        after[...] = jnp.zeros_like(after)

    def conv_back(grad, grad_after, ext, taps):
        grad_ext = jnp.concatenate([grad, grad_after], 0)
        total = taps[TAPS - 1 : TAPS] * grad
        rows = [None] * TAPS
        rows[TAPS - 1] = jnp.sum(grad * ext[HALO:], axis=0, keepdims=True)
        for offset in range(1, TAPS):
            masked = grad_ext * links[offset]
            rows[TAPS - 1 - offset] = jnp.sum(masked[:BLOCK] * ext[HALO - offset : EXT - offset], axis=0, keepdims=True)
            total = total + taps[TAPS - 1 - offset : TAPS - offset] * masked[offset : offset + BLOCK]
        return total, rows + [jnp.sum(grad, axis=0, keepdims=True)]

    flat_main = [(lo, y, c) for lo in range(2) for y in range(4) for c in range(2)]

    def put(j, slot):
        cols = tile_of(j)
        return [
            pltpu.make_async_copy(
                staged.at[slot, pl.ds(i * ROWS, ROWS)], grad_main.at[0, lo, y, c, :, cols], put_sem.at[slot, i]
            )
            for i, (lo, y, c) in enumerate(flat_main)
        ]

    def x_tiles(first, last):
        @pl.loop(first, last)
        def _(j):
            slot = lax.rem(j, 2)
            cols = tile_of(j)

            @pl.when(j + 1 < TILES)
            def _():
                for c in stream(j + 1, 1 - slot):
                    c.start()

            for c in stream(j, slot):
                c.wait()
            grad = grad_in[slot] * silu_slope(pre_in[slot])
            total, rows = conv_back(grad, after[:, cols], ext_in[slot], pmain[0:TAPS, cols])
            for i, row in enumerate(rows):
                vec[i : i + 1, cols] = row
            total = total.astype(BF16)
            raw_x[:, cols] = total

            @pl.when(j >= 2)
            def _():
                for c in put(j, slot):
                    c.wait()

            staged[slot] = dot(normed_t[...], total).astype(BF16)
            for c in put(j, slot):
                c.start()

    def small_part():
        grad = grad_bc[...] * silu_slope(state_pre[...])
        total, rows = conv_back(grad, after[:, DI:], raw_ext[:, :256], params[:TAPS, :256])
        for i, row in enumerate(rows):
            vec[i : i + 1, DI : DI + 256] = row
        raw = jnp.concatenate([total.astype(BF16), grad_step_in[...].astype(BF16)], 1)
        acc[...] += dot(raw, w_small[...], (1, 1))
        small_acc[...] = dot(normed_t[...], raw).astype(BF16)
        packed = jnp.zeros((512, 8 * LANES), F32)
        for r in range(3):
            rows_r = jnp.concatenate([small_acc[pl.ds(d * 96 + r * 32, 32)] for d in range(16)], 0)
            packed = packed + dot(rows_r, small_map(r), (1, 1))
        small_out[...] = packed.astype(BF16)
        for c in small_puts:
            c.start()

    small_puts = [
        pltpu.make_async_copy(small_out.at[pl.ds(i * 32, 32)], grad_small.at[0, lo, y, c], small_sem.at[i])
        for i, (lo, y, c) in enumerate(flat_main)
    ]

    def input_tiles(first, last):
        @pl.loop(first, last)
        def _(k):
            slot = lax.rem(k, 2)

            def load(n, into):
                return pltpu.make_async_copy(full.at[0, :, tile_of(n)], w_in.at[into], w_sem.at[into])

            @pl.when(k + 1 < TILES)
            def _():
                load(k + 1, 1 - slot).start()

            load(k, slot).wait()
            acc[...] += dot(raw_x[:, tile_of(k)], w_in[slot], (1, 1))

    def input_grad():
        value = hidden[...].astype(F32)
        inv = lax.rsqrt(jnp.mean(value * value, axis=1, keepdims=True) + epsilon)
        rows = value * inv
        grad = acc[...]
        vec[5:6, 0:DI] = vec_gate[0:1, :]
        vec[6:7, 0:D] = jnp.sum(grad * rows, axis=0, keepdims=True)
        vec[5:8, DI + 256 :] = vec_heads[5:8, :]
        dn = grad * gain[...]
        mean = jnp.mean(dn * rows, axis=1, keepdims=True)
        grad_hidden[...] = cot[...].astype(F32) + inv * dn - rows * inv * mean

    for c in entering:
        c.wait()
    small_part()
    x_tiles(0, 1)
    stage(1, 0)
    prefetch(2, 1)
    x_tiles(1, 3)
    stage(2, 1)
    prefetch(1, 1)
    x_tiles(3, 5)
    stage(1, 1)
    x_tiles(5, 6)
    pltpu.make_async_copy(full.at[0, :, tile_of(0)], w_in.at[0], w_sem.at[0]).start()
    for slot in range(2):
        for c in put(TILES - 2 + slot, slot):
            c.wait()
    for c in small_puts:
        c.wait()
    to_partner(0)
    prefetch(0, 0)
    input_tiles(0, 3)
    stage(0, 0)
    prefetch(2, 2)
    input_tiles(3, 6)
    stage(2, 2)
    prefetch(0, 1)
    later(2, 1, 0)
    input_grad()
    vec_step(0)
    stage(0, 1)
    prefetch(1, 2)
    vec_step(1)
    stage(1, 2)
    prefetch(0, 2)
    later(1, 1, 0)
    later(2, 1, 1)
    vec_step(2)
    later(1, 1, 1)
    later(2, 1, 2)
    later(2, 0, 0)
    vec_step(3)
    later(1, 1, 2)
    later(1, 0, 0)
    stage(0, 2)
    later(0, 1, 0)
    vec_step(4)
    later(2, 0, 1)
    later(1, 0, 1)
    later(0, 1, 1)
    vec_step(5)
    later(2, 0, 2)
    later(1, 0, 2)
    later(0, 1, 2)
    later(0, 0, 0)
    vec_step(6)
    later(0, 0, 1)
    vec_step(7)
    later(0, 0, 2)
    for m in MATS:
        for u in units_of(m):
            part = other[UNITS[u][0]].at[pl.ds(0, 1), :, :, pl.ds(0, 32)]
            pltpu.make_async_copy(part, part, core_send.at[u, m]).wait()
            for phase in range(3):
                for step in (0, 1):
                    await_step(u, phase, m, step, send)
    for k in range(VEC_STEPS):
        vec_copy(k).wait_send()

    @pl.when(t > 0)
    def _():
        halo_copy().wait_send()


def back(*args):
    vmem = pl.BlockSpec(memory_space=VMEM)
    anywhere = pl.BlockSpec(memory_space=pl.ANY)
    units = range(SUMMED)
    n = SUMMED
    held = [(3, 2, 4, ROWS, 8 * WIDTH), (1, 2, 4, SMALL_ROWS, 8 * SMALL_WIDTH)]
    landing = [(2, STACK[UNITS[u][0]]) + region_shape(u, p, rows) for rows in (16, 32) for u in units for p in range(3)]
    return pl.pallas_call(
        back_kernel,
        name="project_back",
        out_shape=[
            jax.ShapeDtypeStruct((1, 2, 4, 2, ROWS, DI), BF16),
            jax.ShapeDtypeStruct((1, 2, 4, 2, SMALL_ROWS, 8 * LANES), BF16),
            jax.ShapeDtypeStruct((3, ROWS, WIDTH), F32),
            jax.ShapeDtypeStruct((1, SMALL_ROWS, SMALL_WIDTH), F32),
            jax.ShapeDtypeStruct((BLOCK, D), F32),
            jax.ShapeDtypeStruct(VEC, F32),
        ],
        in_specs=[vmem] * 10 + [anywhere] * 11,
        out_specs=[anywhere, anywhere, vmem, vmem, vmem, vmem],
        scratch_shapes=[VMEM(s, BF16) for s in held + landing]
        + [VMEM((2,) + region_shape(u, 2, 32), BF16) for u in units]
        + [
            VMEM((2, EXT, TILE), F32), VMEM((2, BLOCK, TILE), F32), VMEM((2, BLOCK, TILE), F32),
            VMEM((8, DI), F32), VMEM((8, DI), F32), VMEM((8, DI + 256), F32), VMEM((8, DI + 256), F32),
            VMEM((2, D, TILE), BF16), VMEM((2, D, TILE), BF16), VMEM((BLOCK, DI), BF16),
            VMEM((BLOCK, D), F32), VMEM((D, SMALL), BF16), VMEM((512, 8 * LANES), BF16),
            VMEM((VEC_STEPS + 1,) + VEC, F32), VMEM((VEC_STEPS,) + VEC, F32),
            VMEM((D, BLOCK), BF16), VMEM((D, SMALL), BF16), VMEM((BLOCK, D), BF16), VMEM((BLOCK, D), BF16),
        ]
        + [
            pltpu.SemaphoreType.DMA(s)
            for s in (
                (3, 2), (2,), (2,), (2,), (2, 16), (16,), (n, 2, 2), (VEC_STEPS,), (VEC_STEPS,), (n, 9, 2), (n, 9, 2),
                (n, 3), (n, 3, 3), (5,),
            )
        ],
        compiler_params=pltpu.CompilerParams(collective_id=3, has_side_effects=True, vmem_limit_bytes=62 * 2**20),
    )(*args)


def per_device(
    hidden,
    doc_ids,
    norm_gain,
    main_proj,
    step_proj,
    state_proj,
    conv_main,
    conv_main_bias,
    conv_state,
    conv_state_bias,
    step_bias,
    decay_log,
    skip_gain,
    gate_gain,
    out_proj,
    cotangent,
):
    shards, small, pmain, phead, doc_col, doc_row, gain = pack(
        main_proj, out_proj, state_proj.T, step_proj.T, conv_main, conv_main_bias, conv_state, conv_state_bias, step_bias,
        decay_log, skip_gain, gate_gain, norm_gain, doc_ids,
    )
    (pmain, phead, raw, state_pre, grad_bc, grad_step_in, vec_gate, vec_heads, mixed, normed_t, w_small, acc, grad_x,
     x_ext, x_pre, grad_out, grad_gate, full) = mid(
        hidden, gain, doc_col, doc_row, cotangent, shards, small, pmain, phead
    )
    _, _, own_main, own_small, grad_hidden, vec = back(
        raw, state_pre, grad_bc, grad_step_in, pmain, phead, doc_col, gain, vec_gate, vec_heads,
        normed_t, w_small, acc, hidden, cotangent, x_ext, x_pre, grad_x, grad_gate, grad_out, full.reshape(3, D, DI),
    )
    return (mixed, grad_hidden, *finish(own_main, own_small, vec))


def solution(mesh):
    placed = (
        P(("dp", "tensor"), None),
        P("dp"),
        P(),
        P("dp", None, "tensor"),
        P("dp", "tensor"),
        P("dp", "tensor"),
        P(None, "tensor"),
        P("tensor"),
        P(None, "tensor"),
        P("tensor"),
        P("tensor"),
        P("tensor"),
        P("tensor"),
        P("tensor"),
        P("dp", "tensor"),
        P(("dp", "tensor"), None),
    )
    return jax.shard_map(
        per_device,
        mesh=mesh,
        in_specs=placed,
        out_specs=(
            P(("dp", "tensor"), None),
            P(("dp", "tensor"), None),
            P(),
            P("dp", None, "tensor"),
            P("dp", "tensor"),
            P("dp", "tensor"),
            P(None, "tensor"),
            P("tensor"),
            P(None, "tensor"),
            P("tensor"),
            P("tensor"),
            P("tensor"),
            P("tensor"),
            P("tensor"),
            P("dp", "tensor"),
        ),
        check_vma=False,
    )
```
